32 devices in a mesh: dp: 8 (over y, x, core), mp: 4 (over z).
Axes of the slice: x: 2, y: 2, z: 4, core: 2. Of those that a mesh axis runs over, the one named last changes fastest.
Arguments:
- patches: bfloat16 [16384, 1152], P(('dp', 'mp')), may hold values from -2.5 to 2.5
- cotangent: bfloat16 [16384, 1152], P(('dp', 'mp')), may hold values from -2.5 to 2.5
- conditioning: bfloat16 [40, 1152], P('dp'), may hold values from -2.5 to 2.5
- segment: int32 [16384], P('dp'), may hold values from 0 to 3, as said below
- image_ids: int32 [16384], P(('dp', 'mp')), may hold values from 0 to 39, as said below
- w_ada: bfloat16 [1152, 6912], P(None, ('dp', 'mp')), may hold values from -0.1875 to 0.1875
- b_ada: bfloat16 [6912], P(('dp', 'mp')), may hold values from -0.75 to 0.75
- w_qkv: bfloat16 [3, 1152, 1152], P(None, None, 'mp'), may hold values from -0.1875 to 0.1875
- b_qv: bfloat16 [2, 1152], P(None, 'mp'), may hold values from -0.75 to 0.75
- w_out: bfloat16 [1152, 1152], P('mp'), may hold values from -0.75 to 0.75
- b_out: bfloat16 [1152], replicated, may hold values from -0.75 to 0.75
- w_fc1: bfloat16 [1152, 4608], P(None, 'mp'), may hold values from -0.1875 to 0.1875
- b_fc1: bfloat16 [4608], P('mp'), may hold values from -0.75 to 0.75
- w_fc2: bfloat16 [4608, 1152], P('mp'), may hold values from -0.09375 to 0.09375
- b_fc2: bfloat16 [1152], replicated, may hold values from -0.75 to 0.75
Outputs:
- output: bfloat16 [16384, 1152], P(('dp', 'mp'))
- grad_patches: float32 [16384, 1152], P(('dp', 'mp'))
- grad_conditioning: float32 [40, 1152], P('dp')
- grad_w_ada: float32 [1152, 6912], P(None, ('dp', 'mp'))
- grad_b_ada: float32 [6912], P(('dp', 'mp'))
- grad_w_qkv: float32 [3, 1152, 1152], P(None, None, 'mp')
- grad_b_qv: float32 [2, 1152], P(None, 'mp')
- grad_w_out: float32 [1152, 1152], P('mp')
- grad_b_out: float32 [1152], replicated
- grad_w_fc1: float32 [1152, 4608], P(None, 'mp')
- grad_b_fc1: float32 [4608], P('mp')
- grad_w_fc2: float32 [4608, 1152], P('mp')
- grad_b_fc2: float32 [1152], replicated
The draws below stay inside these ranges and needn't reach their ends.
Inputs may be any that keep to these rules, and one draw needn't show every extreme that they name: Each packed row of 1024 patches holds either one image, all its patches with segment 0, or four images of 256 patches with segments 0, 1, 2, 3 in order; half of the 16 rows are of each kind. `image_ids`: all patches of one image carry one number, and each number of 0 to 39 belongs to exactly one image.
All inputs are finite; a program needn't handle non-finite values.
Results may differ from the reference program's by a relative error of at most 0.017.
The reference program's roundings to bfloat16 on the way count: a program that leaves them out, or rounds other values in their place, can miss the bound.
Values may be sent and summed in bfloat16 or wider, within the bound.
A program may use at most 192 MiB of HBM per device.

```python
import math
import jax
import jax.numpy as jnp
from jax import lax

D = 1152
HEADS = 16
HD = 72
FF = 4608
L = 1024
QBLK = 512
ROWS = 16
TOKENS = 16384
IMAGES = 40


def packing_layout(key):
    base_key = jax.random.fold_in(key, 7)
    row_key, image_key = jax.random.split(base_key)
    row_order = jax.random.permutation(row_key, ROWS)
    single = row_order < ROWS // 2
    position = jnp.arange(L, dtype=jnp.int32)
    quarter = (position // (L // 4)).astype(jnp.int32)
    segment_rows = jnp.where(single[:, None], 0, quarter[None, :]).astype(jnp.int32)
    per_row = jnp.where(single, 1, 4).astype(jnp.int32)
    first_image = (jnp.cumsum(per_row) - per_row).astype(jnp.int32)
    ordinal = first_image[:, None] + segment_rows
    numbering = jax.random.permutation(image_key, IMAGES).astype(jnp.int32)
    picture_rows = jnp.take(numbering, ordinal, axis=0)
    return (segment_rows.reshape(-1), picture_rows.reshape(-1).astype(jnp.int32))


def draw_segment(key, part):
    return packing_layout(key)[0]


def draw_image_ids(key, part):
    return packing_layout(key)[1]


def level_of(stream_key, dims, cuts, smallest, high):
    gain = 1.0
    for axis_at, blocks in cuts:
        steps = jax.random.uniform(jax.random.fold_in(jax.random.fold_in(stream_key, 6), axis_at), (blocks,), jnp.float32, smallest / len(cuts), high / len(cuts))
        gain = gain * jnp.repeat(jnp.exp(steps), dims[axis_at] // blocks).reshape((-1,) + (1,) * (len(dims) - 1 - axis_at))
    return gain


def scatter_about(own_key, extent, scale, most, cuts=(), kind=jnp.bfloat16):
    entries = jax.random.normal(own_key, extent, jnp.float32) * scale
    if len(cuts) > 0:
        entries = level_of(own_key, extent, cuts, -0.22, 0.18) * entries
    return jnp.clip(entries, min=-most, max=most).astype(kind)


def setup_inputs(seed: int = 0) -> dict:
    splits = jax.random.split(jax.random.key(seed), 16)
    return {
        "patches": scatter_about(splits[0], (TOKENS, D), 1.0, 2.5, ((0, 32),)),
        "cotangent": scatter_about(splits[1], (TOKENS, D), 1.0, 2.5, ((0, 32),)),
        "conditioning": scatter_about(splits[2], (IMAGES, D), 1.0, 2.5, ((0, 8),)),
        "segment": draw_segment(jax.random.fold_in(splits[15], 71), 0),
        "image_ids": draw_image_ids(jax.random.fold_in(splits[15], 71), 0),
        "w_ada": scatter_about(splits[5], (D, 6 * D), D ** -0.5, 0.1875, ((1, 32),)),
        "b_ada": scatter_about(splits[6], (6 * D,), 0.3, 0.75, ((0, 32),)),
        "w_qkv": scatter_about(splits[7], (3, D, D), D ** -0.5, 0.1875, ((2, 4),)),
        "b_qv": scatter_about(splits[8], (2, D), 0.3, 0.75, ((1, 4),)),
        "w_out": scatter_about(splits[9], (D, D), (D // 16) ** -0.5, 0.75, ((0, 4),)),
        "b_out": scatter_about(splits[10], (D,), 0.3, 0.75),
        "w_fc1": scatter_about(splits[11], (D, FF), D ** -0.5, 0.1875, ((1, 4),)),
        "b_fc1": scatter_about(splits[12], (FF,), 0.3, 0.75, ((0, 4),)),
        "w_fc2": scatter_about(splits[13], (FF, D), FF ** -0.5, 0.09375, ((0, 4),)),
        "b_fc2": scatter_about(splits[14], (D,), 0.3, 0.75),
    }


@jax.custom_vjp
def low(v):
    return lax.optimization_barrier(v.astype(jnp.bfloat16)).astype(jnp.float32)

@jax.custom_vjp
def low_back(v):
    return v

def low_keep(v):
    return (low(v), None)

def low_pass(kept, grad):
    return (grad,)

def back_keep(v):
    return (v, None)

def back_low(kept, grad):
    return (low(grad),)
low.defvjp(low_keep, low_pass)
low_back.defvjp(back_keep, back_low)

def layer_norm(vector):
    centred = vector - lax.optimization_barrier(jnp.mean(vector, axis=-1, keepdims=True))
    spread = lax.optimization_barrier(jnp.mean(centred * centred, axis=-1, keepdims=True))
    return centred * lax.rsqrt(spread + 1e-06)

def matmul(left, right):
    return jnp.dot(left, right, precision=lax.Precision.HIGHEST)

def gelu_tanh(values_in):
    inner_arg = math.sqrt(2.0 / math.pi) * (values_in + 0.044715 * values_in * values_in * values_in)
    return 0.5 * values_in * (1.0 + jnp.tanh(inner_arg))

def attend_row(row_in):
    queries, keys, values, seg_row = row_in
    num_blocks = L // QBLK

    def one_block(block_in):
        query_block, seg_block = block_in
        scores = low_back(jnp.einsum('qhd,khd->hqk', query_block, keys, precision=lax.Precision.HIGHEST) * HD ** (-0.5))
        allowed = seg_block[:, None] == seg_row[None, :]
        scores = jnp.where(allowed[None], scores, -1e+30)
        highest = lax.optimization_barrier(jnp.max(scores, axis=-1, keepdims=True))
        exponent = jnp.exp(scores - highest)
        weights_soft = low(exponent / lax.optimization_barrier(jnp.sum(exponent, axis=-1, keepdims=True)))
        return jnp.einsum('hqk,khd->qhd', weights_soft, values, precision=lax.Precision.HIGHEST)
    context = lax.map(jax.checkpoint(one_block), (queries.reshape(num_blocks, QBLK, HEADS, HD), seg_row.reshape(num_blocks, QBLK)))
    return context.reshape(L, HEADS, HD)

def diffusion_transformer_layer(patch_token_rows, modulation_lookup, parameters, segment_rows, picture_rows):
    w_qkv, b_qv, w_out, b_out, w_fc1, b_fc1, w_fc2, b_fc2 = parameters
    modulation = jnp.take(modulation_lookup, picture_rows, axis=0)
    shift_attn, scale_attn, gate_attn, shift_mlp, scale_mlp, gate_mlp = jnp.split(modulation, 6, axis=1)
    attn_in = low(layer_norm(patch_token_rows) * (1.0 + scale_attn) + shift_attn)
    queries = low(low_back(matmul(attn_in, w_qkv[0]) + b_qv[0]))
    keys = low(low_back(matmul(attn_in, w_qkv[1])))
    values = low(low_back(matmul(attn_in, w_qkv[2]) + b_qv[1]))
    num_rows = patch_token_rows.shape[0] // L
    context = lax.map(attend_row, (queries.reshape(num_rows, L, HEADS, HD), keys.reshape(num_rows, L, HEADS, HD), values.reshape(num_rows, L, HEADS, HD), segment_rows.reshape(num_rows, L)))
    context = low(low_back(context.reshape(num_rows * L, D)))
    attn_out = low_back(matmul(context, w_out) + b_out)
    resid = patch_token_rows + gate_attn * attn_out
    mlp_in = low(layer_norm(resid) * (1.0 + scale_mlp) + shift_mlp)
    pre_act = low_back(matmul(mlp_in, w_fc1) + b_fc1)
    hidden = low(gelu_tanh(pre_act))
    mlp_out = low_back(matmul(hidden, w_fc2) + b_fc2)
    return resid + gate_mlp * mlp_out

def reference(patches, cotangent, conditioning, segment, image_ids, w_ada, b_ada, w_qkv, b_qv, w_out, b_out, w_fc1, b_fc1, w_fc2, b_fc2):

    def widen(array_in):
        return array_in.astype(jnp.float32)

    def make_table(cond_in, weight_in, bias_in):
        silu_cond = low(cond_in * jax.nn.sigmoid(cond_in))
        return low(low_back(matmul(silu_cond, weight_in) + bias_in))
    modulation_lookup, table_back = jax.vjp(make_table, widen(conditioning), widen(w_ada), widen(b_ada))
    parameters = (widen(w_qkv), widen(b_qv), widen(w_out), widen(b_out), widen(w_fc1), widen(b_fc1), widen(w_fc2), widen(b_fc2))
    group_len = 2 * L
    num_groups = TOKENS // group_len
    stacked = (widen(patches).reshape(num_groups, group_len, D), widen(cotangent).reshape(num_groups, group_len, D), segment.reshape(num_groups, group_len), image_ids.reshape(num_groups, group_len))

    def one_group(totals, group_in):
        patch_token_rows, grad_rows, segment_rows, picture_rows = group_in

        def layer_fn(input_rows, input_table, parameters_input):
            return diffusion_transformer_layer(input_rows, input_table, parameters_input, segment_rows, picture_rows)
        result, backward = jax.vjp(layer_fn, patch_token_rows, modulation_lookup, parameters)
        grad_rows_in, grad_tab, grad_weights = backward(grad_rows)
        summed = (totals[0] + grad_tab, jax.tree.map(jnp.add, totals[1], grad_weights))
        return (summed, (result, grad_rows_in))
    zero_init = (jnp.zeros_like(modulation_lookup), jax.tree.map(jnp.zeros_like, parameters))
    (grad_table, grad_params), (results, grad_inputs) = lax.scan(one_group, zero_init, stacked)
    grad_cond, grad_w_ada, grad_b_ada = table_back(grad_table)
    return (results.reshape(TOKENS, D).astype(jnp.bfloat16), grad_inputs.reshape(TOKENS, D), grad_cond, grad_w_ada, grad_b_ada, grad_params[0], grad_params[1], grad_params[2], grad_params[3], grad_params[4], grad_params[5], grad_params[6], grad_params[7])
```

```python
import math

import jax
import jax.numpy as jnp
from jax import lax
from jax.experimental import pallas as pl
from jax.experimental.pallas import tpu as pltpu
from jax.sharding import PartitionSpec as P

HD = 72
HP = 80
L = 1024
BLOCK = 256
BF = jnp.bfloat16
F32 = jnp.float32
SCALE = HD**-0.5
SCALE2 = SCALE * math.log2(math.e)
MASKED = -1e30


def swap(value, axis, bit):
    n = lax.axis_size(axis)
    return lax.ppermute(value, axis, [(i, i ^ bit) for i in range(n)])


def dot(a, b, ca, cb):
    return lax.dot_general(
        a, b, (((ca,), (cb,)), ((), ())), preferred_element_type=F32
    )


def layer_norm(vector):
    centred = vector - jnp.mean(vector, axis=-1, keepdims=True)
    spread = jnp.mean(centred * centred, axis=-1, keepdims=True)
    rsig = lax.rsqrt(spread + 1e-06)
    return centred * rsig, rsig


def norm_back(grad_in, normed, rsig, scale):
    u = grad_in * (1.0 + scale)
    mean_u = jnp.mean(u, axis=-1, keepdims=True)
    mean_un = jnp.mean(u * normed, axis=-1, keepdims=True)
    return (u - mean_u - normed * mean_un) * rsig


def gelu_parts(u):
    a = math.sqrt(2.0 / math.pi)
    t = jnp.tanh(a * (u + 0.044715 * u * u * u))
    return 0.5 * u * (1.0 + t), 0.5 * (1.0 + t) + 0.5 * u * (1.0 - t * t) * (
        a * (1.0 + 3 * 0.044715 * u * u)
    )


def silu_fn(values_in):
    return values_in * jax.nn.sigmoid(values_in)


def head_window(h, width):
    start = h * HP
    base = jnp.minimum((start // 128) * 128, width - 256)
    return pl.multiple_of(base, 128), start - base


def attn_fwd_kernel(q_ref, k_ref, v_ref, ctx_ref, lse_ref, vt, ct):
    rows, width = q_ref.shape
    heads = width // HP
    qb = 256
    vt[...] = v_ref[...].T

    def head(h, carry):
        base, lo = head_window(h, width)
        lane = lax.broadcasted_iota(jnp.int32, (rows, 256), 1)
        here = (lane >= lo) & (lane < lo + HP)
        km = jnp.where(here, k_ref[:, pl.ds(base, 256)], jnp.zeros((), BF))
        vth = vt[pl.ds(pl.multiple_of(h * HP, 16), HP), :]
        for j in range(rows // qb):
            at = slice(j * qb, (j + 1) * qb)
            s = dot(km, q_ref[at, pl.ds(base, 256)], 1, 1)
            m = jnp.max(s, axis=0, keepdims=True) * SCALE2
            e = jnp.exp2(s * SCALE2 - m)
            total = jnp.sum(e, axis=0, keepdims=True)
            c = dot(vth, e.astype(BF), 1, 0)
            ct[pl.ds(pl.multiple_of(h * HP, 8), HP), at] = c / total
            lse_ref[h, :, at] = m + jnp.log2(total)
        return carry

    lax.fori_loop(0, heads, head, 0)
    ctx_ref[...] = ct[...].T.astype(BF)


def attn_fwd(q, k, v):
    rows, width = q.shape
    heads = width // HP
    return pl.pallas_call(
        attn_fwd_kernel,
        out_shape=(
            jax.ShapeDtypeStruct((rows, width), BF),
            jax.ShapeDtypeStruct((heads, 1, rows), F32),
        ),
        in_specs=[pl.BlockSpec(memory_space=pltpu.VMEM)] * 3,
        out_specs=[pl.BlockSpec(memory_space=pltpu.VMEM)] * 2,
        scratch_shapes=[
            pltpu.VMEM((width, rows), BF),
            pltpu.VMEM((width, rows), F32),
        ],
        compiler_params=pltpu.CompilerParams(vmem_limit_bytes=48 << 20),
        cost_estimate=pl.CostEstimate(
            flops=4 * rows * rows * 256 * heads,
            bytes_accessed=8 * rows * width,
            transcendentals=rows * rows * heads,
        ),
    )(q, k, v)


def attn_bwd_kernel(
    q_ref, k_ref, v_ref, g_ref, lse_ref, dq_ref, dk_ref, dv_ref, kt, dqt, dk_acc, dv_acc
):
    rows, width = q_ref.shape
    heads = width // HP
    qb = 512
    kt[...] = k_ref[...].T
    dk_acc[...] = jnp.zeros_like(dk_acc)
    dv_acc[...] = jnp.zeros_like(dv_acc)

    def head(h, carry):
        base, lo = head_window(h, width)
        win = pl.ds(base, 256)
        zero = jnp.zeros((), BF)
        lane = lax.broadcasted_iota(jnp.int32, (rows, 256), 1)
        here = (lane >= lo) & (lane < lo + HP)
        km = jnp.where(here, k_ref[:, win], zero)
        vm = jnp.where(here, v_ref[:, win], zero)
        kth = kt[pl.ds(pl.multiple_of(h * HP, 16), HP), :]
        row = lax.broadcasted_iota(jnp.int32, (HP, rows), 0)
        kth = jnp.where(row < HD, kth, zero)
        lane_b = lax.broadcasted_iota(jnp.int32, (qb, 256), 1)
        real = (lane_b >= lo) & (lane_b < lo + HD)
        for j in range(rows // qb):
            at = slice(j * qb, (j + 1) * qb)
            q_blk = q_ref[at, win]
            g_blk = g_ref[at, win]
            s = dot(km, q_blk, 1, 1)
            p = jnp.exp2(s * SCALE2 - lse_ref[h, :, at])
            dp = dot(vm, g_blk, 1, 1)
            delta = jnp.sum(p * dp, axis=0, keepdims=True)
            ds = (p * (dp - delta)).astype(BF)
            dv_acc[:, win] += dot(p.astype(BF), jnp.where(real, g_blk, zero), 1, 0)
            dk_acc[:, win] += dot(ds, jnp.where(real, q_blk, zero), 1, 0)
            dqt[pl.ds(pl.multiple_of(h * HP, 8), HP), at] = dot(kth, ds, 1, 0)
        return carry

    lax.fori_loop(0, heads, head, 0)
    dq_ref[...] = (dqt[...].T * SCALE).astype(BF)
    dk_ref[...] = (dk_acc[...] * SCALE).astype(BF)
    dv_ref[...] = dv_acc[...].astype(BF)


def attn_bwd(q, k, v, g, lse):
    rows, width = q.shape
    heads = width // HP
    shape = jax.ShapeDtypeStruct((rows, width), BF)
    return pl.pallas_call(
        attn_bwd_kernel,
        out_shape=(shape, shape, shape),
        in_specs=[pl.BlockSpec(memory_space=pltpu.VMEM)] * 5,
        out_specs=[pl.BlockSpec(memory_space=pltpu.VMEM)] * 3,
        scratch_shapes=[
            pltpu.VMEM((width, rows), BF),
            pltpu.VMEM((width, rows), F32),
            pltpu.VMEM((rows, width), F32),
            pltpu.VMEM((rows, width), F32),
        ],
        compiler_params=pltpu.CompilerParams(vmem_limit_bytes=56 << 20),
        cost_estimate=pl.CostEstimate(
            flops=10 * rows * rows * 256 * heads,
            bytes_accessed=14 * rows * width,
            transcendentals=rows * rows * heads,
        ),
    )(q, k, v, g, lse)


def pad_heads(rows_in):
    *lead, n, width = rows_in.shape
    split = rows_in.reshape(*lead, n // HD, HD, width)
    pads = [(0, 0)] * (len(lead) + 1) + [(0, HP - HD), (0, 0)]
    return jnp.pad(split, pads).reshape(*lead, n // HD * HP, width)


def drop_pads(rows_in):
    *lead, n, width = rows_in.shape
    split = rows_in.reshape(*lead, n // HP, HP, width)[..., :HD, :]
    return split.reshape(*lead, n // HP * HD, width)


def on_device(
    patches,
    cotangent,
    conditioning,
    segment,
    image_ids,
    w_ada,
    b_ada,
    w_qkv,
    b_qv,
    w_out,
    b_out,
    w_fc1,
    b_fc1,
    w_fc2,
    b_fc2,
):
    n_dp, n_mp = lax.axis_size("dp"), lax.axis_size("mp")
    n_all = n_dp * n_mp
    z = lax.axis_index("mp")
    d = lax.axis_index("dp")
    core = d & 1
    everyone = ("dp", "mp")
    tokens, width = patches.shape
    n_blocks = tokens // BLOCK
    shard = w_fc2.shape[0]
    hidden_n = shard * n_mp

    part = shard // n_dp
    w1t_own = w_fc1.T
    w1_all = lax.all_gather(
        lax.dynamic_slice_in_dim(w1t_own, d * part, part, 0), ("mp", "dp"), axis=0, tiled=True
    )
    w2_all = lax.all_gather(
        lax.dynamic_slice_in_dim(w_fc2, d * part, part, 0), ("mp", "dp"), axis=0, tiled=True
    )

    heads_shard = w_out.shape[0]
    watt_own = jnp.concatenate(
        [w_qkv.transpose(0, 2, 1), w_out[None]], axis=0
    )
    half = heads_shard // 2
    sent_half = lax.dynamic_slice_in_dim(watt_own, core * half, half, 1)
    got_half = swap(sent_half, "mp", 2)
    got_other = swap(got_half, "dp", 1)
    first = jnp.where(core == 0, got_half, got_other)
    second = jnp.where(core == 0, got_other, got_half)
    watt_other = jnp.concatenate([first, second], axis=1)
    bqv_other = swap(b_qv, "mp", 2)
    watt = jnp.concatenate([pad_heads(watt_own), pad_heads(watt_other)], axis=1)
    wide = watt.shape[1]
    wqkv_t = watt[:3].reshape(3 * wide, width)
    wout_p = watt[3]
    bqv2 = jnp.concatenate(
        [pad_heads(b_qv[..., None])[..., 0], pad_heads(bqv_other[..., None])[..., 0]],
        axis=1,
    ).astype(F32)

    cond_all = lax.all_gather(conditioning, "dp", axis=0, tiled=True)
    n_img = cond_all.shape[0]
    silu_cond = silu_fn(cond_all.astype(F32)).astype(BF)
    table_cols = (dot(silu_cond, w_ada, 1, 0) + b_ada.astype(F32)).astype(BF)
    cols = table_cols.shape[1]
    table = lax.all_to_all(
        jnp.broadcast_to(table_cols[None], (n_all, n_img, cols)), everyone, 0, 0
    )
    ids = image_ids.reshape(n_blocks, BLOCK)[:, 0]
    mods = jnp.stack(
        [
            lax.dynamic_slice(table, (0, ids[b], 0), (n_all, 1, cols)).reshape(6, width)
            for b in range(n_blocks)
        ]
    ).astype(F32)
    shift_attn, scale_attn, gate_attn, shift_mlp, scale_mlp, gate_mlp = [
        mods[:, i, None, :] for i in range(6)
    ]

    def blocks(v):
        return v.reshape(n_blocks, BLOCK, width)

    def flat(v):
        return v.reshape(tokens, width)

    patch_wide = blocks(patches.astype(F32))
    grad_output = blocks(cotangent.astype(F32))
    norm_a, rsig_a = layer_norm(patch_wide)
    attn_in = flat((norm_a * (1.0 + scale_attn) + shift_attn).astype(BF))
    x_row = jnp.concatenate([attn_in, swap(attn_in, "mp", 1)], axis=0)

    seg_own = lax.dynamic_slice_in_dim(segment, z * tokens, tokens, 0)
    seg_peer = lax.dynamic_slice_in_dim(segment, (z ^ 1) * tokens, tokens, 0)
    seg = jnp.concatenate([seg_own, seg_peer])[:, None]
    slot = lax.broadcasted_iota(jnp.int32, (1, wide), 1) % HP - HD
    mark_q = jnp.where(slot == seg, 1.0, 0.0)
    mark_k = jnp.where((slot >= 0) & (slot < 4) & (slot != seg), MASKED, 0.0)
    proj = dot(x_row, wqkv_t, 1, 1)
    q = (proj[:, :wide] + bqv2[0] + mark_q).astype(BF)
    k = (proj[:, wide : 2 * wide] + mark_k).astype(BF)
    v = (proj[:, 2 * wide :] + bqv2[1]).astype(BF)
    ctx, lse = attn_fwd(q, k, v)

    out_peer = swap(dot(ctx[tokens:], wout_p, 1, 0).astype(BF), "mp", 1)
    attn_out = blocks(
        dot(ctx[:tokens], wout_p, 1, 0) + out_peer.astype(F32) + b_out.astype(F32)
    )
    resid = patch_wide + gate_attn * attn_out
    norm_m, rsig_m = layer_norm(resid)
    mlp_in = flat((norm_m * (1.0 + scale_mlp) + shift_mlp).astype(BF))

    b1_all = lax.all_gather(b_fc1, "mp", axis=0, tiled=True).astype(F32)
    pre = dot(mlp_in, w1_all, 1, 1) + b1_all
    act, act_grad = gelu_parts(pre)
    hidden = act.astype(BF)
    mlp_out = blocks(dot(hidden, w2_all, 1, 0) + b_fc2.astype(F32))
    output = flat((resid + gate_mlp * mlp_out).astype(BF))
    g_gate_mlp = jnp.sum(grad_output * mlp_out, axis=1)
    gmo = flat((gate_mlp * grad_output).astype(BF))
    grad_w2 = dot(hidden, gmo, 0, 0).astype(BF)
    grad_b2 = jnp.sum(gmo, axis=0, dtype=F32)
    grad_pre = (dot(gmo, w2_all, 1, 1) * act_grad).astype(BF)
    grad_w1t = dot(grad_pre, mlp_in, 0, 0).astype(BF)
    grad_b1 = jnp.sum(grad_pre, axis=0, dtype=F32)
    red_w2 = lax.psum_scatter(grad_w2, ("mp", "dp"), scatter_dimension=0, tiled=True)
    red_w1 = lax.psum_scatter(grad_w1t, ("mp", "dp"), scatter_dimension=0, tiled=True)
    out_w2 = lax.all_gather(red_w2, "dp", axis=0, tiled=True)
    out_w1 = lax.all_gather(red_w1, "dp", axis=0, tiled=True)

    g_mlp_in = blocks(dot(grad_pre, w1_all, 1, 0))
    g_shift_mlp = jnp.sum(g_mlp_in, axis=1)
    g_scale_mlp = jnp.sum(g_mlp_in * norm_m, axis=1)
    grad_resid = grad_output + norm_back(g_mlp_in, norm_m, rsig_m, scale_mlp)
    g_gate_attn = jnp.sum(grad_resid * attn_out, axis=1)
    gao = flat((gate_attn * grad_resid).astype(BF))
    grad_bout = jnp.sum(gao, axis=0, dtype=F32)
    gao_row = jnp.concatenate([gao, swap(gao, "mp", 1)], axis=0)

    grad_ctx = dot(gao_row, wout_p, 1, 1).astype(BF)
    grad_wout = dot(ctx, gao_row, 0, 0)
    dq, dk, dv = attn_bwd(q, k, v, grad_ctx, lse)
    dqkv = jnp.concatenate([dq, dk, dv], axis=1)
    g_peer = swap(dot(dqkv[tokens:], wqkv_t, 1, 0).astype(BF), "mp", 1)
    g_attn_in = blocks(dot(dqkv[:tokens], wqkv_t, 1, 0) + g_peer.astype(F32))
    grad_wqkv = dot(dqkv, x_row, 0, 0)
    grad_att = drop_pads(
        jnp.concatenate([grad_wqkv, grad_wout], axis=0).astype(BF).reshape(4, 2, wide // 2, width)
    )
    grad_att = grad_att.transpose(1, 0, 2, 3).reshape(2, 4 * heads_shard, width)
    red_att = lax.psum_scatter(grad_att, "dp", scatter_dimension=1, tiled=True)
    red_own = red_att[0].astype(F32) + swap(red_att[1], "mp", 2).astype(F32)
    out_att = lax.all_gather(red_own.astype(BF), "dp", axis=0, tiled=True)
    out_att = out_att.reshape(4, heads_shard, width)

    g_shift_attn = jnp.sum(g_attn_in, axis=1)
    g_scale_attn = jnp.sum(g_attn_in * norm_a, axis=1)
    grad_patches = flat(grad_resid + norm_back(g_attn_in, norm_a, rsig_a, scale_attn))
    sums = jnp.concatenate(
        [g_shift_attn, g_scale_attn, g_gate_attn, g_shift_mlp, g_scale_mlp, g_gate_mlp],
        axis=1,
    )
    to_owner = sums.reshape(n_blocks, n_all, cols).transpose(1, 0, 2)
    with_ids = jnp.concatenate(
        [to_owner, jnp.broadcast_to(ids.astype(F32)[None, :, None], (n_all, n_blocks, 1))],
        axis=2,
    )
    got = lax.all_to_all(with_ids, everyone, 0, 0).reshape(n_all * n_blocks, cols + 1)
    belongs = (
        got[:, cols].astype(jnp.int32)[None, :]
        == lax.broadcasted_iota(jnp.int32, (n_img, 1), 0)
    ).astype(F32)
    grad_cols = lax.dot_general(
        belongs,
        got[:, :cols],
        (((1,), (0,)), ((), ())),
        precision=lax.Precision.HIGHEST,
        preferred_element_type=F32,
    ).astype(BF)
    grad_w_ada = dot(silu_cond, grad_cols, 0, 0)
    grad_b_ada = jnp.sum(grad_cols, axis=0, dtype=F32)
    silu_part = dot(grad_cols, w_ada, 1, 1)

    bq = jnp.sum(dq, axis=0, dtype=F32)
    bv = jnp.sum(dv, axis=0, dtype=F32)
    bqv_g = drop_pads(jnp.stack([bq, bv]).reshape(2, 2, wide // 2)[..., None])[..., 0]
    bqv_g = bqv_g.transpose(1, 0, 2)
    shards = jnp.arange(n_mp)[:, None, None]
    bqv_all = jnp.where(shards == z, bqv_g[0][None], 0.0) + jnp.where(
        shards == (z ^ 2), bqv_g[1][None], 0.0
    )
    images_here = n_img // n_dp
    payload = jnp.concatenate(
        [
            jnp.broadcast_to(
                silu_part.reshape(n_dp, 1, images_here * width),
                (n_dp, n_mp, images_here * width),
            ),
            jnp.broadcast_to(
                jnp.concatenate([grad_bout, grad_b2])[None, None], (n_dp, n_mp, 2 * width)
            ),
            jnp.broadcast_to(grad_b1.reshape(1, n_mp, shard), (n_dp, n_mp, shard)),
            jnp.broadcast_to(
                bqv_all.reshape(1, n_mp, 2 * heads_shard), (n_dp, n_mp, 2 * heads_shard)
            ),
        ],
        axis=2,
    ).reshape(n_all, -1)
    summed = jnp.sum(lax.all_to_all(payload, everyone, 0, 0), axis=0)
    at = images_here * width
    grad_silu = summed[:at].reshape(images_here, width)
    _, silu_back = jax.vjp(silu_fn, conditioning.astype(F32))
    grad_cond = silu_back(grad_silu)[0]
    out_bout = summed[at : at + width]
    out_b2 = summed[at + width : at + 2 * width]
    at += 2 * width
    out_b1 = summed[at : at + shard]
    out_bqv = summed[at + shard :].reshape(2, heads_shard)

    return (
        output,
        grad_patches,
        grad_cond,
        grad_w_ada,
        grad_b_ada,
        out_att[:3].transpose(0, 2, 1).astype(F32),
        out_bqv,
        out_att[3].astype(F32),
        out_bout,
        out_w1.T.astype(F32),
        out_b1,
        out_w2.astype(F32),
        out_b2,
    )


def solution(mesh):
    rows = P(("dp", "mp"), None)
    in_specs = (
        rows,
        rows,
        P("dp", None),
        P("dp"),
        P(("dp", "mp")),
        P(None, ("dp", "mp")),
        P(("dp", "mp")),
        P(None, None, "mp"),
        P(None, "mp"),
        P("mp", None),
        P(),
        P(None, "mp"),
        P("mp"),
        P("mp", None),
        P(),
    )
    out_specs = (
        rows,
        rows,
        P("dp", None),
        P(None, ("dp", "mp")),
        P(("dp", "mp")),
        P(None, None, "mp"),
        P(None, "mp"),
        P("mp", None),
        P(),
        P(None, "mp"),
        P("mp"),
        P("mp", None),
        P(),
    )
    return jax.shard_map(
        on_device, mesh=mesh, in_specs=in_specs, out_specs=out_specs, check_vma=False
    )
```

```python
import functools
import math

import jax
import jax.numpy as jnp
from jax import lax
from jax.experimental import pallas as pl
from jax.experimental.pallas import tpu as pltpu
from jax.sharding import PartitionSpec as P

HD = 72
HP = 80
L = 1024
BLOCK = 256
BF = jnp.bfloat16
F32 = jnp.float32
SCALE = HD**-0.5
SCALE2 = SCALE * math.log2(math.e)
MASKED = -1e30
ORDER = (0, 1, 3, 2)


def swap(value, axis, bit):
    n = lax.axis_size(axis)
    return lax.ppermute(value, axis, [(i, i ^ bit) for i in range(n)])


def dot(a, b, ca, cb):
    return lax.dot_general(
        a, b, (((ca,), (cb,)), ((), ())), preferred_element_type=F32
    )


def after(value, *earlier):
    return lax.optimization_barrier((value, *earlier))[0]


def pick(stacked, index):
    return lax.dynamic_index_in_dim(stacked, index, 0, keepdims=False)


def layer_norm(vector):
    centred = vector - jnp.mean(vector, axis=-1, keepdims=True)
    spread = jnp.mean(centred * centred, axis=-1, keepdims=True)
    rsig = lax.rsqrt(spread + 1e-06)
    return centred * rsig, rsig


def norm_back(grad_in, normed, rsig, scale):
    u = grad_in * (1.0 + scale)
    mean_u = jnp.mean(u, axis=-1, keepdims=True)
    mean_un = jnp.mean(u * normed, axis=-1, keepdims=True)
    return (u - mean_u - normed * mean_un) * rsig


def gelu_parts(u):
    a = math.sqrt(2.0 / math.pi)
    t = jnp.tanh(a * (u + 0.044715 * u * u * u))
    return 0.5 * u * (1.0 + t), 0.5 * (1.0 + t) + 0.5 * u * (1.0 - t * t) * (
        a * (1.0 + 3 * 0.044715 * u * u)
    )


def silu_fn(values_in):
    return values_in * jax.nn.sigmoid(values_in)


def head_windows(width):
    found = []
    for h in range(width // HP):
        base = h * HP // 128 * 128
        end = min(-(-(h + 1) * HP // 128) * 128, width)
        found.append((base, end - base, h * HP - base))
    return found


def attn_fwd_kernel(q_ref, k_ref, v_ref, ctx_ref, lse_ref, vt, ct):
    rows, width = q_ref.shape
    qb = 512
    vt[...] = v_ref[...].T
    for h, (base, size, lo) in enumerate(head_windows(width)):
        win = slice(base, base + size)
        lane = lax.broadcasted_iota(jnp.int32, (rows, size), 1)
        here = (lane >= lo) & (lane < lo + HP)
        km = jnp.where(here, k_ref[:, win], jnp.zeros((), BF))
        head = slice(h * HP, (h + 1) * HP)
        vth = vt[head, :]

        def block(j, carry):
            at = pl.ds(pl.multiple_of(j * qb, qb), qb)
            s = dot(km, q_ref[at, win], 1, 1)
            m = jnp.max(s, axis=0, keepdims=True) * SCALE2
            e = jnp.exp2(s * SCALE2 - m)
            total = jnp.sum(e, axis=0, keepdims=True)
            c = dot(vth, e.astype(BF), 1, 0)
            ct[head, at] = c / total
            lse_ref[h, :, at] = m + jnp.log2(total)
            return carry

        lax.fori_loop(0, rows // qb, block, 0)
    ctx_ref[...] = ct[...].T.astype(BF)


def attn_fwd(q, k, v):
    rows, width = q.shape
    heads = width // HP
    return pl.pallas_call(
        attn_fwd_kernel,
        out_shape=(
            jax.ShapeDtypeStruct((rows, width), BF),
            jax.ShapeDtypeStruct((heads, 1, rows), F32),
        ),
        in_specs=[pl.BlockSpec(memory_space=pltpu.VMEM)] * 3,
        out_specs=[pl.BlockSpec(memory_space=pltpu.VMEM)] * 2,
        scratch_shapes=[
            pltpu.VMEM((width, rows), BF),
            pltpu.VMEM((width, rows), F32),
        ],
        compiler_params=pltpu.CompilerParams(vmem_limit_bytes=40 << 20),
        cost_estimate=pl.CostEstimate(
            flops=4 * rows * rows * 256 * heads,
            bytes_accessed=8 * rows * width,
            transcendentals=rows * rows * heads,
        ),
    )(q, k, v)


def attn_bwd_kernel(
    q_ref, k_ref, v_ref, g_ref, lse_ref, dq_ref, dk_ref, dv_ref, kt, dqt, dk_acc, dv_acc
):
    rows, width = q_ref.shape
    qb = 512
    kt[...] = k_ref[...].T
    dk_acc[...] = jnp.zeros_like(dk_acc)
    dv_acc[...] = jnp.zeros_like(dv_acc)
    zero = jnp.zeros((), BF)
    for h, (base, size, lo) in enumerate(head_windows(width)):
        win = slice(base, base + size)
        lane = lax.broadcasted_iota(jnp.int32, (rows, size), 1)
        here = (lane >= lo) & (lane < lo + HP)
        km = jnp.where(here, k_ref[:, win], zero)
        vm = jnp.where(here, v_ref[:, win], zero)
        head = slice(h * HP, (h + 1) * HP)
        row = lax.broadcasted_iota(jnp.int32, (HP, rows), 0)
        kth = jnp.where(row < HD, kt[head, :], zero)
        lane_b = lax.broadcasted_iota(jnp.int32, (qb, size), 1)
        real = (lane_b >= lo) & (lane_b < lo + HD)

        def block(j, carry):
            at = pl.ds(pl.multiple_of(j * qb, qb), qb)
            q_blk = q_ref[at, win]
            g_blk = g_ref[at, win]
            s = dot(km, q_blk, 1, 1)
            p = jnp.exp2(s * SCALE2 - lse_ref[h, :, at])
            dp = dot(vm, g_blk, 1, 1)
            delta = jnp.sum(p * dp, axis=0, keepdims=True)
            ds = (p * (dp - delta)).astype(BF)
            dv_acc[:, win] += dot(p.astype(BF), jnp.where(real, g_blk, zero), 1, 0)
            dk_acc[:, win] += dot(ds, jnp.where(real, q_blk, zero), 1, 0)
            dqt[head, at] = dot(kth, ds, 1, 0)
            return carry

        lax.fori_loop(0, rows // qb, block, 0)
    dq_ref[...] = (dqt[...].T * SCALE).astype(BF)
    dk_ref[...] = (dk_acc[...] * SCALE).astype(BF)
    dv_ref[...] = dv_acc[...].astype(BF)


def attn_bwd(q, k, v, g, lse):
    rows, width = q.shape
    heads = width // HP
    shape = jax.ShapeDtypeStruct((rows, width), BF)
    return pl.pallas_call(
        attn_bwd_kernel,
        out_shape=(shape, shape, shape),
        in_specs=[pl.BlockSpec(memory_space=pltpu.VMEM)] * 5,
        out_specs=[pl.BlockSpec(memory_space=pltpu.VMEM)] * 3,
        scratch_shapes=[
            pltpu.VMEM((width, rows), BF),
            pltpu.VMEM((width, rows), F32),
            pltpu.VMEM((rows, width), F32),
            pltpu.VMEM((rows, width), F32),
        ],
        compiler_params=pltpu.CompilerParams(vmem_limit_bytes=40 << 20),
        cost_estimate=pl.CostEstimate(
            flops=10 * rows * rows * 256 * heads,
            bytes_accessed=14 * rows * width,
            transcendentals=rows * rows * heads,
        ),
    )(q, k, v, g, lse)


def coords(index, n_mp):
    return index // n_mp, lax.rem(index, n_mp)


def wait_all(ref, count, sem):
    whole = ref.at[pl.ds(0, count)]
    pltpu.make_async_copy(whole, whole, sem).wait()


def modulation_kernel(
    per_dp, cond, ids, bias, w_ada, b_ada, mods, silu_out, ids_out, b1_out, bqv_out,
    cond_all, ids_all, bias_all, send, land, sems,
):
    n_dp, n_all, n_mp = cond_all.shape[0], ids_all.shape[0], bias_all.shape[0]
    d, z = lax.axis_index("dp"), lax.axis_index("mp")
    me = d * n_mp + z
    barrier = pltpu.get_barrier_semaphore()

    def greet(t, carry):
        to = coords(lax.rem(me + t, n_all), n_mp)
        pl.semaphore_signal(barrier, inc=1, device_id=to, device_id_type=pl.DeviceIdType.MESH)
        return carry

    lax.fori_loop(1, n_all, greet, 0)
    pl.semaphore_wait(barrier, n_all - 1)

    def copy(src, dst, k, to):
        return pltpu.make_async_remote_copy(
            src_ref=src, dst_ref=dst, send_sem=sems.at[2 * k], recv_sem=sems.at[2 * k + 1],
            device_id=to, device_id_type=pl.DeviceIdType.MESH,
        )

    def send_cond(t, carry):
        copy(cond, cond_all.at[d], 0, (lax.rem(d + t, n_dp), z)).start()
        return carry

    def send_ids(t, carry):
        copy(ids, ids_all.at[me], 1, coords(lax.rem(me + t, n_all), n_mp)).start()
        return carry

    def send_bias(t, carry):
        copy(bias, bias_all.at[z], 2, (d, lax.rem(z + t, n_mp))).start()
        return carry

    lax.fori_loop(1, n_dp, send_cond, 0)
    lax.fori_loop(1, n_all, send_ids, 0)
    lax.fori_loop(1, n_mp, send_bias, 0)
    cond_all[d] = cond[...]
    ids_all[me] = ids[...]
    bias_all[z] = bias[...]
    for k, (ref, n) in enumerate(((cond_all, n_dp), (ids_all, n_all), (bias_all, n_mp))):
        wait_all(ref, n - 1, sems.at[2 * k + 1])

    rows = n_dp * 8
    c = cond_all[...].reshape(rows, cond_all.shape[2])
    silu = (c * (1.0 / (1.0 + jnp.exp(-c)))).astype(BF)
    silu_out[...] = silu
    table = (dot(silu, w_ada[...], 1, 0) + b_ada[...]).astype(BF)
    k = lax.broadcasted_iota(jnp.int32, (n_all * 8, rows), 1)
    image = jnp.where(lax.rem(k, 8) < per_dp, k // 8 * per_dp + lax.rem(k, 8), -2)
    found = ids_all[...].reshape(n_all * 8, 128)[:, :1] == image.astype(F32)
    picked = dot(jnp.where(found, 1.0, 0.0).astype(BF), table, 1, 0)
    send[...] = picked.reshape(send.shape)

    def send_rows(t, carry):
        other = lax.rem(me + t, n_all)
        copy(send.at[other], land.at[me], 3, coords(other, n_mp)).start()
        return carry

    lax.fori_loop(1, n_all, send_rows, 0)
    land[me] = send[me]
    ids_out[...] = ids_all[...]
    sixth = b1_out.shape[1]
    core, q = lax.rem(d, 2), lax.rem(d // 2, 4)
    at = 0
    for i in ORDER:
        for j in range(n_mp):
            quarter = jnp.bitwise_xor(q, i)
            shard = jnp.bitwise_xor(z, j)
            b1_out[at : at + 1, :] = bias_all[shard, pl.ds(core * 4 + quarter, 1), :sixth]
            at += 1
    bqv_out[...] = bias_all[jnp.bitwise_xor(z, 2), 8:, :]
    wait_all(land, n_all - 1, sems.at[7])
    mods[...] = land[...]
    for k, (ref, n) in enumerate(
        ((cond_all, n_dp), (ids_all, n_all), (bias_all, n_mp), (land, n_all))
    ):
        wait_all(ref, n - 1, sems.at[2 * k])


def modulation_rows(cond, ids, bias, w_ada, b_ada, n_dp, n_mp, sixth):
    n_all, per_dp, width, cols = n_dp * n_mp, cond.shape[0], cond.shape[1], w_ada.shape[1]
    cond8 = jnp.pad(cond.astype(F32), ((0, 8 - per_dp), (0, 0)))
    ids8 = jnp.pad(ids.astype(F32), (0, 8 - ids.shape[0]), constant_values=-1.0)
    shapes = (
        jax.ShapeDtypeStruct((n_all, 8, cols), F32),
        jax.ShapeDtypeStruct((n_dp * 8, width), BF),
        jax.ShapeDtypeStruct((n_all, 8, 128), F32),
        jax.ShapeDtypeStruct((16, sixth), F32),
        jax.ShapeDtypeStruct((8, bias.shape[1]), F32),
    )
    return pl.pallas_call(
        functools.partial(modulation_kernel, per_dp),
        out_shape=shapes,
        in_specs=[pl.BlockSpec(memory_space=pltpu.VMEM)] * 5,
        out_specs=[pl.BlockSpec(memory_space=pltpu.VMEM)] * 5,
        scratch_shapes=[
            pltpu.VMEM((n_dp, 8, width), F32),
            pltpu.VMEM((n_all, 8, 128), F32),
            pltpu.VMEM((n_mp, *bias.shape), F32),
            pltpu.VMEM((n_all, 8, cols), F32),
            pltpu.VMEM((n_all, 8, cols), F32),
            pltpu.SemaphoreType.DMA((8,)),
        ],
        compiler_params=pltpu.CompilerParams(
            collective_id=0, has_side_effects=True, vmem_limit_bytes=32 << 20
        ),
    )(
        cond8,
        jnp.broadcast_to(ids8[:, None], (8, 128)),
        bias,
        w_ada,
        b_ada.astype(F32)[None],
    )


def pad_heads(rows_in):
    *lead, n, width = rows_in.shape
    split = rows_in.reshape(*lead, n // HD, HD, width)
    pads = [(0, 0)] * (len(lead) + 1) + [(0, HP - HD), (0, 0)]
    return jnp.pad(split, pads).reshape(*lead, n // HD * HP, width)


def drop_pads(rows_in):
    *lead, n, width = rows_in.shape
    split = rows_in.reshape(*lead, n // HP, HP, width)[..., :HD, :]
    return split.reshape(*lead, n // HP * HD, width)


def on_device(
    patches,
    cotangent,
    conditioning,
    segment,
    image_ids,
    w_ada,
    b_ada,
    w_qkv,
    b_qv,
    w_out,
    b_out,
    w_fc1,
    b_fc1,
    w_fc2,
    b_fc2,
):
    n_dp, n_mp = lax.axis_size("dp"), lax.axis_size("mp")
    n_all = n_dp * n_mp
    z = lax.axis_index("mp")
    d = lax.axis_index("dp")
    core = d & 1
    everyone = ("dp", "mp")
    tokens, width = patches.shape
    n_blocks = tokens // BLOCK
    shard = w_fc2.shape[0]
    hidden_n = shard * n_mp

    q = (d >> 1) & 3
    sixth = shard // 8

    def quarter(w1, w2, i):
        at = (core * 4 + (q ^ i)) * sixth
        return jnp.stack(
            [
                lax.dynamic_slice_in_dim(w1, at, sixth, 1).T,
                lax.dynamic_slice_in_dim(w2, at, sixth, 0),
            ]
        )

    first = quarter(w_fc1, w_fc2, 0)

    heads_shard = w_out.shape[0]
    watt_own = jnp.concatenate([w_qkv.transpose(0, 2, 1), w_out[None]], axis=0)
    p2 = d & 3
    got0 = swap(pick(watt_own, p2), "mp", 2)
    got1 = swap(got0, "dp", 1)
    got23 = swap(jnp.stack([got0, got1]), "dp", 2)
    got = jnp.stack([got0, got1, got23[0], got23[1]])
    watt_other = jnp.stack([pick(got, p2 ^ m) for m in range(4)])
    watts = [pad_heads(watt_own), pad_heads(watt_other)]
    wide = watts[0].shape[1]

    z1 = swap(first, "mp", 1)
    later = after(first, got0)
    groups = [z1[:, None], jnp.stack([swap(later, "mp", 2), swap(later, "mp", 3)], axis=1)]

    def over_plane(group):
        from_x = swap(group, "dp", 2)
        from_y = swap(group, "dp", 4)
        return from_x, from_y

    def far_side(from_x, from_y):
        return swap(from_x[0], "dp", 4), swap(from_y[1], "dp", 2)

    near_1 = over_plane(groups[0])
    far_1 = far_side(*near_1)

    ids = image_ids.reshape(n_blocks, BLOCK)[:, 0]
    cols = w_ada.shape[1]
    bias = jnp.concatenate(
        [
            jnp.pad(b_fc1.astype(F32).reshape(8, sixth), ((0, 0), (0, heads_shard - sixth))),
            jnp.pad(b_qv.astype(F32), ((0, 6), (0, 0))),
        ]
    )
    mod_rows, silu_cond, ids_all, b1_rel, bqv_other = modulation_rows(
        conditioning, ids, bias, w_ada, b_ada, n_dp, n_mp, sixth
    )
    b1_all = b1_rel.reshape(16 * sixth)
    bqvs = [pad_heads(v[..., None])[..., 0].astype(F32) for v in (b_qv, bqv_other[:2])]
    mods = mod_rows[:, :n_blocks].transpose(1, 0, 2).reshape(n_blocks, 6, width)
    shift_attn, scale_attn, gate_attn, shift_mlp, scale_mlp, gate_mlp = [
        mods[:, i, None, :] for i in range(6)
    ]

    def blocks(v):
        return v.reshape(n_blocks, BLOCK, width)

    def flat(v):
        return v.reshape(tokens, width)

    patch_wide = blocks(patches.astype(F32))
    grad_output = blocks(cotangent.astype(F32))
    norm_a, rsig_a = layer_norm(patch_wide)
    attn_in = flat((norm_a * (1.0 + scale_attn) + shift_attn).astype(BF))
    x_row = jnp.concatenate([attn_in, swap(attn_in, "mp", 1)], axis=0)

    seg_own = lax.dynamic_slice_in_dim(segment, z * tokens, tokens, 0)
    seg_peer = lax.dynamic_slice_in_dim(segment, (z ^ 1) * tokens, tokens, 0)
    seg = jnp.concatenate([seg_own, seg_peer])[:, None]
    slot = lax.broadcasted_iota(jnp.int32, (1, wide), 1) % HP - HD
    mark_q = jnp.where(slot == seg, 1.0, 0.0)
    mark_k = jnp.where((slot >= 0) & (slot < 4) & (slot != seg), MASKED, 0.0)

    def project(watt, bqv, rows_in):
        proj = dot(rows_in, watt[:3].reshape(3 * wide, width), 1, 1)
        qh = (proj[:, :wide] + bqv[0] + mark_q).astype(BF)
        kh = (proj[:, wide : 2 * wide] + mark_k).astype(BF)
        return qh, kh, (proj[:, 2 * wide :] + bqv[1]).astype(BF)

    heads_0 = project(watts[0], bqvs[0], x_row)
    ctx_0, lse_0 = attn_fwd(*heads_0)
    near_2 = over_plane(after(groups[1], heads_0[0]))
    heads_1 = project(watts[1], bqvs[1], after(x_row, ctx_0))
    ctx_1, lse_1 = attn_fwd(*heads_1)
    outs = [watts[0][3], watts[1][3]]

    def out_part(at):
        return dot(ctx_0[at], outs[0], 1, 0) + dot(ctx_1[at], outs[1], 1, 0)

    out_send = out_part(slice(tokens, None)).astype(BF)
    far_2 = far_side(*[after(v, out_send) for v in near_2])
    out_peer = swap(out_send, "mp", 1)
    attn_out = blocks(
        out_part(slice(0, tokens)) + out_peer.astype(F32) + b_out.astype(F32)
    )
    w1_late, w2_late = lax.optimization_barrier((w_fc1, w_fc2, attn_in))[:2]
    own = [first] + [quarter(w1_late, w2_late, i) for i in (1, 2, 3)]
    nears = [jnp.concatenate([a, b], axis=1) for a, b in zip(near_1, near_2)]
    fars = [jnp.concatenate([a, b], axis=0) for a, b in zip(far_1, far_2)]
    from_z = jnp.concatenate(groups, axis=1)

    def laid_out(m):
        pieces = [own[0][m][None], from_z[m], own[1][m][None], nears[0][m]]
        pieces += [own[3][m][None], fars[m], own[2][m][None], nears[1][m]]
        return jnp.concatenate(pieces, axis=0).reshape(16 * sixth, width)

    w1_all = laid_out(0)
    w2_all = laid_out(1)
    resid = patch_wide + gate_attn * attn_out
    norm_m, rsig_m = layer_norm(resid)
    mlp_in = flat((norm_m * (1.0 + scale_mlp) + shift_mlp).astype(BF))

    gmo = flat((gate_mlp * grad_output).astype(BF))
    gmo2 = jnp.concatenate([gmo, swap(gmo, "dp", 1)], axis=0)
    mlp2 = jnp.concatenate([mlp_in, swap(mlp_in, "dp", 1)], axis=0)
    pre = dot(mlp2, w1_all, 1, 1) + b1_all
    act, act_grad = gelu_parts(pre)
    hidden = act.astype(BF)

    quad = 4 * sixth

    def grads(left, right, at, to):
        out = dot(left[:, at * quad : to * quad], right, 0, 0)
        return out.reshape(to - at, 4, sixth, width)

    def low_sum(a, b):
        return (a.astype(F32) + b.astype(F32)).astype(BF)

    send2 = grads(hidden, gmo2, 1, 3).astype(BF)
    come2 = swap(send2, "dp", 2)
    grad_pre = (dot(after(gmo2, send2), w2_all, 1, 1) * act_grad).astype(BF)
    grad_b1 = jnp.sum(grad_pre, axis=0, dtype=F32)
    send1 = grads(grad_pre, mlp2, 2, 4).astype(BF)
    come1 = swap(send1, "dp", 4)
    gin_peer = swap(dot(grad_pre[tokens:], w1_all, 1, 0).astype(BF), "dp", 1)
    g_mlp_in = blocks(dot(grad_pre[:tokens], w1_all, 1, 0) + gin_peer.astype(F32))
    g_shift_mlp = jnp.sum(g_mlp_in, axis=1)
    g_scale_mlp = jnp.sum(g_mlp_in * norm_m, axis=1)
    grad_resid = grad_output + norm_back(g_mlp_in, norm_m, rsig_m, scale_mlp)
    g_gate_attn = jnp.sum(grad_resid * attn_out, axis=1)
    gao = flat((gate_attn * grad_resid).astype(BF))
    grad_bout = jnp.sum(gao, axis=0, dtype=F32)
    gao_row = jnp.concatenate([gao, swap(gao, "mp", 1)], axis=0)

    hidden_w, gmo2_w, gpre_w, mlp2_w = lax.optimization_barrier(
        (hidden, gmo2, grad_pre, mlp2, gao)
    )[:4]
    mlp_peer = swap(dot(hidden_w[tokens:], w2_all, 1, 0).astype(BF), "dp", 1)
    keep2_2 = grads(hidden_w, gmo2_w, 3, 4)[0]
    keep2_0 = grads(hidden_w, gmo2_w, 0, 1)[0]
    mlp_out = blocks(
        dot(hidden_w[:tokens], w2_all, 1, 0) + mlp_peer.astype(F32) + b_fc2.astype(F32)
    )
    output = flat((resid + gate_mlp * mlp_out).astype(BF))
    g_gate_mlp = jnp.sum(grad_output * mlp_out, axis=1)
    grad_b2 = jnp.sum(gmo, axis=0, dtype=F32)

    def back(heads, out_w, lse, rows_in):
        grad_ctx = dot(rows_in, out_w, 1, 1).astype(BF)
        return attn_bwd(*heads, grad_ctx, lse)

    def att_grads(ctx, grad3):
        whole = jnp.concatenate(
            [dot(grad3, x_row, 0, 0).astype(BF), dot(ctx, gao_row, 0, 0).astype(BF)], axis=0
        )
        return drop_pads(whole.reshape(4, wide, width)).reshape(4, 2, sixth, width)

    def over_cores(grad_att):
        send = lax.dynamic_index_in_dim(grad_att, 1 - core, 1, keepdims=False)
        keep = lax.dynamic_index_in_dim(grad_att, core, 1, keepdims=False)
        got = low_sum(keep, swap(send, "dp", 1))
        return [pick(got, q ^ i) for i in range(4)]

    dq_1, dk_1, dv_1 = back(heads_1, outs[1], lse_1, gao_row)
    grad3_1 = jnp.concatenate([dq_1, dk_1, dv_1], axis=1)
    come2, come1 = lax.optimization_barrier((come2, come1, dq_1))[:2]
    two_2 = low_sum(keep2_2, come2[1])
    two_0 = low_sum(keep2_0, come2[0])
    come2 = swap(two_2, "dp", 4)
    keep1 = grads(gpre_w, mlp2_w, 0, 2)
    one_1 = low_sum(keep1[1], come1[0])
    one_0 = low_sum(keep1[0], come1[1])
    come1 = swap(one_1, "dp", 2)
    rel_b = over_cores(att_grads(ctx_1, grad3_1))
    dq_0, dk_0, dv_0 = back(heads_0, outs[0], lse_0, after(gao_row, one_1, rel_b[0]))
    come2, come1 = lax.optimization_barrier((come2, come1, dq_0))[:2]
    grad3_0 = jnp.concatenate([dq_0, dk_0, dv_0], axis=1)
    in_w = [w[:3].reshape(3 * wide, width) for w in watts]

    def g_in_part(at):
        return dot(grad3_0[at], in_w[0], 1, 0) + dot(grad3_1[at], in_w[1], 1, 0)

    g_peer = swap(g_in_part(slice(tokens, None)).astype(BF), "mp", 1)
    g_attn_in = blocks(g_in_part(slice(0, tokens)) + g_peer.astype(F32))
    plane2 = low_sum(two_0, come2)
    plane1 = low_sum(one_0, come1)
    rel_a = over_cores(att_grads(ctx_0, grad3_0))

    both = jnp.stack([plane1, plane2])
    whole = both[:, 0].astype(F32)
    for j in (1, 2, 3):
        whole = whole + swap(both[:, j], "mp", j).astype(F32)
    bit = 8
    while bit < n_dp:
        whole = whole + swap(whole.astype(BF), "dp", bit).astype(F32)
        bit *= 2
    done = whole.astype(BF)
    done_x = swap(done, "dp", 2)
    done_y = swap(done, "dp", 4)
    done_xy = jnp.stack([swap(done_x[0], "dp", 4), swap(done_y[1], "dp", 2)])
    mine = jnp.stack([done, done_x, done_y, done_xy])
    theirs = swap(mine, "dp", 1)

    spot = jnp.arange(8 * sixth)
    came = (spot // (4 * sixth)) ^ core, ((spot // sixth) % 4) ^ q
    target = (came[0] * 4 + came[1]) * sixth + spot % sixth
    places = (target[:, None] == spot[None, :]).astype(BF)
    rel = jnp.stack([mine, theirs])
    out_w1 = dot(rel[:, :, 0].reshape(shard, width), places, 0, 0)
    out_w2 = dot(places, rel[:, :, 1].reshape(shard, width), 0, 0)

    come_b = swap(jnp.stack([rel_b[2], rel_b[3]]), "dp", 4)
    b_1 = low_sum(rel_b[1], come_b[1])
    b_0 = low_sum(low_sum(rel_b[0], come_b[0]), swap(b_1, "dp", 2))
    come_a = swap(jnp.stack([rel_a[1], rel_a[3]]), "dp", 2)
    a_2 = low_sum(rel_a[2], come_a[1])
    a_0 = low_sum(low_sum(rel_a[0], come_a[0]), swap(a_2, "dp", 4))
    att = a_0.astype(F32) + swap(b_0, "mp", 2).astype(F32)
    bit = 8
    while bit < n_dp:
        att = att + swap(att.astype(BF), "dp", bit).astype(F32)
        bit *= 2
    att = att.astype(BF)
    att_x = swap(att, "dp", 2)
    att_y = swap(att, "dp", 4)
    att_mine = jnp.stack([att, att_x, att_y, swap(att_x, "dp", 4)])
    rel = jnp.stack([att_mine, swap(att_mine, "dp", 1)]).reshape(shard, width)
    target_att = (came[1] * 2 + came[0]) * sixth + spot % sixth
    places = (target_att[:, None] == spot[None, :]).astype(BF)
    cut = [places[:, m * heads_shard : (m + 1) * heads_shard] for m in range(4)]
    out_qkv = jnp.stack([dot(rel, cut[m], 0, 0) for m in range(3)])
    out_wout = dot(cut[3], rel, 0, 0)

    g_shift_attn = jnp.sum(g_attn_in, axis=1)
    g_scale_attn = jnp.sum(g_attn_in * norm_a, axis=1)
    grad_patches = flat(grad_resid + norm_back(g_attn_in, norm_a, rsig_a, scale_attn))
    sums = jnp.concatenate(
        [g_shift_attn, g_scale_attn, g_gate_attn, g_shift_mlp, g_scale_mlp, g_gate_mlp],
        axis=1,
    )
    to_owner = sums.reshape(n_blocks, n_all, cols).transpose(1, 0, 2)
    got = lax.all_to_all(to_owner, everyone, 0, 0).reshape(n_all * n_blocks, cols)
    ids_from = ids_all[:, :n_blocks, 0].reshape(1, n_all * n_blocks)
    images_here = conditioning.shape[0]
    row = jnp.arange(n_dp * 8)[:, None]
    image = jnp.where(row % 8 < images_here, row // 8 * images_here + row % 8, -2)
    belongs = (ids_from == image.astype(F32)).astype(F32)
    grad_cols = lax.dot_general(
        belongs,
        got,
        (((1,), (0,)), ((), ())),
        precision=lax.Precision.HIGHEST,
        preferred_element_type=F32,
    ).astype(BF)
    grad_w_ada = dot(silu_cond, grad_cols, 0, 0)
    grad_b_ada = jnp.sum(grad_cols, axis=0, dtype=F32)
    silu_part = dot(grad_cols, w_ada, 1, 1)
    silu_part = silu_part.reshape(n_dp, 8, width)[:, :images_here]

    bqv_g = jnp.stack(
        [
            jnp.stack([jnp.sum(v, axis=0, dtype=F32) for v in pair])
            for pair in ((dq_0, dv_0), (dq_1, dv_1))
        ]
    )
    bqv_g = drop_pads(bqv_g[..., None])[..., 0]
    shards = jnp.arange(n_mp)[:, None, None]
    bqv_all = jnp.where(shards == z, bqv_g[0][None], 0.0) + jnp.where(
        shards == (z ^ 2), bqv_g[1][None], 0.0
    )
    nat, rel_at = jnp.arange(8 * n_mp)[:, None], jnp.arange(16)[None, :]
    step = rel_at // 4
    step = jnp.where(step == 2, 3, jnp.where(step == 3, 2, step))
    comes = ((nat // 8) == (z ^ (rel_at % 4))) & ((nat % 4) == (q ^ step))
    comes = comes & (nat // 4 % 2 == core)
    grad_b1 = lax.dot_general(
        comes.astype(F32),
        grad_b1.reshape(16, sixth),
        (((1,), (0,)), ((), ())),
        precision=lax.Precision.HIGHEST,
        preferred_element_type=F32,
    )
    payload = jnp.concatenate(
        [
            jnp.broadcast_to(
                silu_part.reshape(n_dp, 1, images_here * width),
                (n_dp, n_mp, images_here * width),
            ),
            jnp.broadcast_to(
                jnp.concatenate([grad_bout, grad_b2])[None, None], (n_dp, n_mp, 2 * width)
            ),
            jnp.broadcast_to(grad_b1.reshape(1, n_mp, shard), (n_dp, n_mp, shard)),
            jnp.broadcast_to(
                bqv_all.reshape(1, n_mp, 2 * heads_shard), (n_dp, n_mp, 2 * heads_shard)
            ),
        ],
        axis=2,
    ).reshape(n_all, -1)
    summed = jnp.sum(lax.all_to_all(payload, everyone, 0, 0), axis=0)
    at = images_here * width
    grad_silu = summed[:at].reshape(images_here, width)
    _, silu_back = jax.vjp(silu_fn, conditioning.astype(F32))
    grad_cond = silu_back(grad_silu)[0]
    out_bout = summed[at : at + width]
    out_b2 = summed[at + width : at + 2 * width]
    at += 2 * width
    out_b1 = summed[at : at + shard]
    out_bqv = summed[at + shard :].reshape(2, heads_shard)

    return (
        output,
        grad_patches,
        grad_cond,
        grad_w_ada,
        grad_b_ada,
        out_qkv,
        out_bqv,
        out_wout,
        out_bout,
        out_w1,
        out_b1,
        out_w2,
        out_b2,
    )


def solution(mesh):
    rows = P(("dp", "mp"), None)
    in_specs = (
        rows,
        rows,
        P("dp", None),
        P("dp"),
        P(("dp", "mp")),
        P(None, ("dp", "mp")),
        P(("dp", "mp")),
        P(None, None, "mp"),
        P(None, "mp"),
        P("mp", None),
        P(),
        P(None, "mp"),
        P("mp"),
        P("mp", None),
        P(),
    )
    out_specs = (
        rows,
        rows,
        P("dp", None),
        P(None, ("dp", "mp")),
        P(("dp", "mp")),
        P(None, None, "mp"),
        P(None, "mp"),
        P("mp", None),
        P(),
        P(None, "mp"),
        P("mp"),
        P("mp", None),
        P(),
    )
    return jax.shard_map(
        on_device, mesh=mesh, in_specs=in_specs, out_specs=out_specs, check_vma=False
    )
```

```python
import functools
import math

import jax
import jax.numpy as jnp
from jax import lax
from jax.experimental import pallas as pl
from jax.experimental.pallas import tpu as pltpu
from jax.sharding import PartitionSpec as P

HD = 72
HP = 80
L = 1024
BLOCK = 256
BF = jnp.bfloat16
F32 = jnp.float32
SCALE = HD**-0.5
SCALE2 = SCALE * math.log2(math.e)
MASKED = -1e30
ORDER = (0, 1, 3, 2)


def swap(value, axis, bit):
    n = lax.axis_size(axis)
    return lax.ppermute(value, axis, [(i, i ^ bit) for i in range(n)])


def dot(a, b, ca, cb):
    return lax.dot_general(
        a, b, (((ca,), (cb,)), ((), ())), preferred_element_type=F32
    )


def after(value, *earlier):
    return lax.optimization_barrier((value, *earlier))[0]


def pick(stacked, index):
    return lax.dynamic_index_in_dim(stacked, index, 0, keepdims=False)


def layer_norm(vector):
    centred = vector - jnp.mean(vector, axis=-1, keepdims=True)
    spread = jnp.mean(centred * centred, axis=-1, keepdims=True)
    rsig = lax.rsqrt(spread + 1e-06)
    return centred * rsig, rsig


def norm_back(grad_in, normed, rsig, scale):
    u = grad_in * (1.0 + scale)
    mean_u = jnp.mean(u, axis=-1, keepdims=True)
    mean_un = jnp.mean(u * normed, axis=-1, keepdims=True)
    return (u - mean_u - normed * mean_un) * rsig


def gelu_parts(u):
    a = math.sqrt(2.0 / math.pi)
    t = jnp.tanh(a * (u + 0.044715 * u * u * u))
    return 0.5 * u * (1.0 + t), 0.5 * (1.0 + t) + 0.5 * u * (1.0 - t * t) * (
        a * (1.0 + 3 * 0.044715 * u * u)
    )


def silu_fn(values_in):
    return values_in * jax.nn.sigmoid(values_in)


def head_windows(width):
    found = []
    for h in range(width // HP):
        base = h * HP // 128 * 128
        end = min(-(-(h + 1) * HP // 128) * 128, width)
        found.append((base, end - base, h * HP - base))
    return found


def attn_bwd_kernel(
    q_ref, k_ref, v_ref, g_ref, lse_ref, dq_ref, dk_ref, dv_ref, kt, dqt, dk_acc, dv_acc
):
    rows, width = q_ref.shape
    qb = 512
    kt[...] = k_ref[...].T
    dk_acc[...] = jnp.zeros_like(dk_acc)
    dv_acc[...] = jnp.zeros_like(dv_acc)
    zero = jnp.zeros((), BF)
    for h, (base, size, lo) in enumerate(head_windows(width)):
        win = slice(base, base + size)
        lane = lax.broadcasted_iota(jnp.int32, (rows, size), 1)
        here = (lane >= lo) & (lane < lo + HP)
        km = jnp.where(here, k_ref[:, win], zero)
        vm = jnp.where(here, v_ref[:, win], zero)
        head = slice(h * HP, (h + 1) * HP)
        row = lax.broadcasted_iota(jnp.int32, (HP, rows), 0)
        kth = jnp.where(row < HD, kt[head, :], zero)
        lane_b = lax.broadcasted_iota(jnp.int32, (qb, size), 1)
        real = (lane_b >= lo) & (lane_b < lo + HD)

        def block(j, carry):
            at = pl.ds(pl.multiple_of(j * qb, qb), qb)
            q_blk = q_ref[at, win]
            g_blk = g_ref[at, win]
            s = dot(km, q_blk, 1, 1)
            p = jnp.exp2(s * SCALE2 - lse_ref[h, :, at])
            dp = dot(vm, g_blk, 1, 1)
            delta = jnp.sum(p * dp, axis=0, keepdims=True)
            ds = (p * (dp - delta)).astype(BF)
            dv_acc[:, win] += dot(p.astype(BF), jnp.where(real, g_blk, zero), 1, 0)
            dk_acc[:, win] += dot(ds, jnp.where(real, q_blk, zero), 1, 0)
            dqt[head, at] = dot(kth, ds, 1, 0)
            return carry

        lax.fori_loop(0, rows // qb, block, 0)
    dq_ref[...] = (dqt[...].T * SCALE).astype(BF)
    dk_ref[...] = (dk_acc[...] * SCALE).astype(BF)
    dv_ref[...] = dv_acc[...].astype(BF)


def attn_bwd(q, k, v, g, lse):
    rows, width = q.shape
    heads = width // HP
    shape = jax.ShapeDtypeStruct((rows, width), BF)
    return pl.pallas_call(
        attn_bwd_kernel,
        out_shape=(shape, shape, shape),
        in_specs=[pl.BlockSpec(memory_space=pltpu.VMEM)] * 5,
        out_specs=[pl.BlockSpec(memory_space=pltpu.VMEM)] * 3,
        scratch_shapes=[
            pltpu.VMEM((width, rows), BF),
            pltpu.VMEM((width, rows), F32),
            pltpu.VMEM((rows, width), F32),
            pltpu.VMEM((rows, width), F32),
        ],
        compiler_params=pltpu.CompilerParams(vmem_limit_bytes=40 << 20),
        cost_estimate=pl.CostEstimate(
            flops=10 * rows * rows * 256 * heads,
            bytes_accessed=14 * rows * width,
            transcendentals=rows * rows * heads,
        ),
    )(q, k, v, g, lse)


PLACE = {0: 0, 1: 1, 3: 2, 2: 3}


def flip(index, bit):
    return index + bit - 2 * bit * lax.rem(index // bit, 2)


def flips(index, bits):
    for bit in (1, 2):
        index = flip(index, bit) if bits & bit else index
    return index


def coords(index, n_mp):
    return index // n_mp, lax.rem(index, n_mp)


def wait_all(ref, count, sem):
    whole = ref.at[pl.ds(0, count)]
    pltpu.make_async_copy(whole, whole, sem).wait()


class Copies:
    def __init__(self, sems):
        self.sems, self.made = sems, {}

    def make(self, name, src, dst, to):
        k = 2 * len(self.made)
        self.made[name] = pltpu.make_async_remote_copy(
            src_ref=src,
            dst_ref=dst,
            send_sem=self.sems.at[k],
            recv_sem=self.sems.at[k + 1],
            device_id=to,
            device_id_type=pl.DeviceIdType.MESH,
        )
        return self.made[name]

    def beside(self, name, src, dst, to):
        k = 2 * list(self.made).index(name)
        return pltpu.make_async_remote_copy(
            src_ref=src,
            dst_ref=dst,
            send_sem=self.sems.at[k],
            recv_sem=self.sems.at[k + 1],
            device_id=to,
            device_id_type=pl.DeviceIdType.MESH,
        )

    def start(self, name, src, dst, to):
        self.make(name, src, dst, to).start()

    def arrived(self, name):
        self.made[name].wait_recv()

    def finish(self, but=()):
        for name, made in self.made.items():
            if name not in but:
                made.wait_send()


def front_kernel(
    per_dp, cond, ids, bias, w_ada, b_ada, patches, cotangent, seg, watt_own, w_fc1, w_fc2, bqv_own, b_out,
    silu_out, ids_out, b1_out, mods, x_row, q0, k0, v0, q1, k1, v1, c0, c1, l0, l1,
    watt_other, w1_all, w2_all, attn_out, mlp2, gmo2,
    cond_all, ids_all, bias_all, send, land, w1t, normed, out_send, out_land, vts, ct, bqv_other,
    small, local, sems,
):
    n_dp, n_all, n_mp = cond_all.shape[0], ids_all.shape[0], bias_all.shape[0]
    tokens, width = patches.shape
    wide = watt_own.shape[1]
    sixth = b1_out.shape[1]
    half_w = wide // 2
    d, z = lax.axis_index("dp"), lax.axis_index("mp")
    me = d * n_mp + z
    core, q = lax.rem(d, 2), lax.rem(d // 2, 4)
    mid = (z == 1) | (z == 2)
    at_z = [(d, z), (d, flip(z, 1)), (d, flip(z, 2)), (d, 3 - z)]
    at_core, at_x, at_y = (flip(d, 1), z), (flip(d, 2), z), (flip(d, 4), z)
    copies = Copies(sems)
    barrier = pltpu.get_barrier_semaphore()

    def greet(t, carry):
        to = coords(lax.rem(me + t, n_all), n_mp)
        pl.semaphore_signal(barrier, inc=1, device_id=to, device_id_type=pl.DeviceIdType.MESH)
        return carry

    lax.fori_loop(1, n_all, greet, 0)
    pl.semaphore_wait(barrier, n_all - 1)

    def copy(src, dst, k, to):
        return pltpu.make_async_remote_copy(
            src_ref=src, dst_ref=dst, send_sem=small.at[2 * k], recv_sem=small.at[2 * k + 1],
            device_id=to, device_id_type=pl.DeviceIdType.MESH,
        )

    def send_cond(t, carry):
        copy(cond, cond_all.at[d], 0, (lax.rem(d + t, n_dp), z)).start()
        return carry

    def send_ids(t, carry):
        copy(ids, ids_all.at[me], 1, coords(lax.rem(me + t, n_all), n_mp)).start()
        return carry

    def send_bias(t, carry):
        copy(bias, bias_all.at[z], 2, (d, lax.rem(z + t, n_mp))).start()
        return carry

    lax.fori_loop(1, n_dp, send_cond, 0)
    lax.fori_loop(1, n_all, send_ids, 0)
    lax.fori_loop(1, n_mp, send_bias, 0)

    cond_all[d] = cond[...]
    ids_all[me] = ids[...]
    bias_all[z] = bias[...]
    w1t[...] = w_fc1[...].T
    for k, (ref, n) in enumerate(((cond_all, n_dp), (ids_all, n_all), (bias_all, n_mp))):
        wait_all(ref, n - 1, small.at[2 * k + 1])

    rows = n_dp * 8
    c = cond_all[...].reshape(rows, width)
    silu = (c * (1.0 / (1.0 + jnp.exp(-c)))).astype(BF)
    silu_out[...] = silu
    table = (dot(silu, w_ada[...], 1, 0) + b_ada[...]).astype(BF)
    k = lax.broadcasted_iota(jnp.int32, (n_all * 8, rows), 1)
    image = jnp.where(lax.rem(k, 8) < per_dp, k // 8 * per_dp + lax.rem(k, 8), -2)
    found = ids_all[...].reshape(n_all * 8, 128)[:, :1] == image.astype(F32)
    picked = dot(jnp.where(found, 1.0, 0.0).astype(BF), table, 1, 0)
    send[...] = picked.reshape(send.shape)

    def send_rows(t, carry):
        other = lax.rem(me + t, n_all)
        copy(send.at[other], land.at[me], 3, coords(other, n_mp)).start()
        return carry

    lax.fori_loop(1, n_all, send_rows, 0)
    my_half = pl.ds(pl.multiple_of(core * half_w, 16), half_w)
    copies.start("a_z", watt_own.at[q, my_half], watt_other.at[q, my_half], at_z[2])
    w_in, w_all, ends = [w1t, w_fc2], [w1_all, w2_all], {}

    def rows_of(i):
        return pl.ds(pl.multiple_of((core * 4 + flips(q, i)) * sixth, 16), sixth)

    for m in (1, 0):
        copies.start(("w_z", m, 1), w_in[m].at[rows_of(0)], w_all[m].at[0, 1], at_z[1])
        copies.make(("w_z", m, 3), w_in[m].at[rows_of(0)], w_all[m].at[0, 3], at_z[3])
        copies.make(("w_z", m, 2), w_all[m].at[0, 1], w_all[m].at[0, 2], at_z[3])
        ends[m] = [
            copies.beside(("w_z", m, there), w_all[m].at[0, here], w_all[m].at[0, there], at_z[1])
            for here, there in ((3, 2), (2, 3))
        ]

        @pl.when(mid)
        def _():
            copies.made["w_z", m, 3].start()

    own = [
        pltpu.make_async_copy(w_in[m].at[rows_of(i)], w_all[m].at[PLACE[i], 0], local.at[2 * i + m])
        for i in range(4)
        for m in range(2)
    ]
    for made in own:
        made.start()

    land[me] = send[me]
    ids_out[...] = ids_all[...]
    at = 0
    for i in ORDER:
        for j in range(n_mp):
            shard = 3 - z if j == 3 else flip(z, j) if j else z
            b1_out[at : at + 1, :] = bias_all[shard, pl.ds(core * 4 + flips(q, i), 1), :sixth]
            at += 1
    bqv = bias_all[flip(z, 2), 8:, :]
    heads = wide // HP
    bqv_other[...] = jnp.zeros_like(bqv_other)
    for h in range(heads):
        bqv_other[:, h * HP : h * HP + HD] = bqv[:, h * HD : (h + 1) * HD]

    step = 128

    def norm(v):
        centred = v - jnp.mean(v, axis=-1, keepdims=True)
        spread = jnp.mean(centred * centred, axis=-1, keepdims=True)
        return centred * lax.rsqrt(spread + 1e-06)

    def norm_patches(t, carry):
        part = pl.ds(pl.multiple_of(t * step, step), step)
        normed[part, :] = norm(patches[part, :].astype(F32))
        return carry

    lax.fori_loop(0, tokens // step, norm_patches, 0)
    copies.arrived("a_z")
    copies.start("a_c", watt_other.at[q, my_half], watt_other.at[q, my_half], at_core)
    wait_all(land, n_all - 1, small.at[7])
    cols = land.shape[2]
    for s in range(n_all):
        mods[:, s * cols : (s + 1) * cols] = land[s]

    def vector(b, which):
        return mods[b : b + 1, which * width : (which + 1) * width]

    for b in range(tokens // BLOCK):
        shift, scale = vector(b, 0), 1.0 + vector(b, 1)

        def modulate(t, carry):
            part = pl.ds(pl.multiple_of(b * BLOCK + t * step, step), step)
            x_row[part, :] = (normed[part, :] * scale + shift).astype(BF)
            return carry

        lax.fori_loop(0, BLOCK // step, modulate, 0)
    mine, theirs = slice(0, tokens), slice(tokens, 2 * tokens)
    copies.start("x", x_row.at[mine], x_row.at[theirs], at_z[1])
    for b in range(tokens // BLOCK):
        gate_mlp = vector(b, 5)

        def scaled(t, carry):
            part = pl.ds(pl.multiple_of(b * BLOCK + t * step, step), step)
            gmo2[part, :] = (gate_mlp * cotangent[part, :].astype(F32)).astype(BF)
            return carry

        lax.fori_loop(0, BLOCK // step, scaled, 0)
    copies.start("gmo", gmo2.at[mine], gmo2.at[theirs], at_core)

    def w_near(j):
        for m in (1, 0):
            copies.arrived(("w_z", m, j))
            if j == 1:

                @pl.when(mid)
                def _():
                    copies.made["w_z", m, 2].start()

            src = w_all[m].at[0, j]
            copies.start(("w_x", m, j), src, w_all[m].at[PLACE[1], j], at_x)
            copies.start(("w_y", m, j), src, w_all[m].at[PLACE[2], j], at_y)

    def w_near_late(j):
        @pl.when(jnp.logical_not(mid))
        def _():
            for m in (1, 0):
                copies.arrived(("w_z", m, j))

        for m in (1, 0):
            src = w_all[m].at[0, j]
            copies.start(("w_x", m, j), src, w_all[m].at[PLACE[1], j], at_x)
            copies.start(("w_y", m, j), src, w_all[m].at[PLACE[2], j], at_y)

    def w_far(j):
        for m, way, i, to in ((0, "w_x", 1, at_y), (1, "w_y", 2, at_x)):
            copies.arrived((way, m, j))
            copies.start(
                ("w_far", m, j), w_all[m].at[PLACE[i], j], w_all[m].at[PLACE[3], j], to
            )

    qx, qy = flips(q, 1), flips(q, 2)
    low, high = slice(0, half_w), slice(half_w, wide)

    lane = lax.rem(lax.broadcasted_iota(jnp.int32, (tokens, wide), 1), HP) - HD
    slots = ((watt_own, bqv_own, q0, k0, v0, c0, l0), (watt_other, bqv_other, q1, k1, v1, c1, l1))

    def project(slot, part):
        watt, bqv, qr, kr, vr = slots[slot][:5]
        x = x_row[part, :]
        same = lane == seg[part, :]
        marks = jnp.where(same, 1.0, 0.0)
        qr[part, :] = (dot(x, watt[0], 1, 1) + bqv[0:1, :] + marks).astype(BF)
        off = jnp.where((lane >= 0) & (lane < 4) & jnp.logical_not(same), MASKED, 0.0)
        kr[part, :] = (dot(x, watt[1], 1, 1) + off).astype(BF)
        vr[part, :] = (dot(x, watt[2], 1, 1) + bqv[1:2, :]).astype(BF)

    qb = 256

    def attend(slot, first, count):
        qr, kr, _, _, lr = slots[slot][2:]
        for h, (base, size, lo) in enumerate(head_windows(wide)):
            win = slice(base, base + size)
            ln = lax.broadcasted_iota(jnp.int32, (2 * tokens, size), 1)
            km = jnp.where((ln >= lo) & (ln < lo + HP), kr[:, win], jnp.zeros((), BF))
            head = slice(h * HP, (h + 1) * HP)
            vth = vts[slot, head, :]

            def block(j, carry):
                at = pl.ds(pl.multiple_of(j * qb, qb), qb)
                s = dot(km, qr[at, win], 1, 1)
                m = jnp.max(s, axis=0, keepdims=True) * SCALE2
                e = jnp.exp2(s * SCALE2 - m)
                total = jnp.sum(e, axis=0, keepdims=True)
                c = dot(vth, e.astype(BF), 1, 0)
                ct[head, at] = c / total
                lr[h, :, at] = m + jnp.log2(total)
                return carry

            lax.fori_loop(first, first + count, block, 0)
        part = slice(first * qb, (first + count) * qb)
        slots[slot][5][part, :] = ct[:, part].T.astype(BF)

    def out_part(part):
        return dot(c0[part, :], watt_own[3], 1, 0) + dot(c1[part, :], watt_other[3], 1, 0)

    def att_plane():
        copies.arrived("a_c")
        copies.start("a_x", watt_other.at[q], watt_other.at[q], at_x)
        copies.start("a_y", watt_other.at[q], watt_other.at[q], at_y)

    def att_far():
        copies.arrived("a_x")
        copies.start("a_xy", watt_other.at[qx, low], watt_other.at[qx, low], at_y)
        copies.arrived("a_y")
        copies.start("a_yx", watt_other.at[qy, high], watt_other.at[qy, high], at_x)

    def att_here():
        copies.arrived("a_xy")
        copies.arrived("a_yx")

    att_plane()
    project(0, mine)
    w_near(1)
    copies.arrived("x")

    @pl.when(mid)
    def _():
        for m in (1, 0):
            for j in (3, 2):
                copies.arrived(("w_z", m, j))
            for made in ends[m]:
                made.start()

    att_far()
    project(0, theirs)
    vts[0] = v0[...].T
    n_peer = tokens // qb
    attend(0, n_peer, n_peer)
    att_here()
    project(1, mine)
    project(1, theirs)
    vts[1] = v1[...].T
    for t in range(n_peer):
        attend(1, n_peer + t, 1)
        part = slice(t * qb, (t + 1) * qb)
        out_send[part, :] = out_part(slice(tokens + t * qb, tokens + (t + 1) * qb)).astype(BF)
        copies.start(("out", t), out_send.at[part], out_land.at[part], at_z[1])
        if t == 0:
            w_far(1)
    w_near_late(2)
    attend(0, 0, n_peer)
    w_near_late(3)
    attend(1, 0, n_peer)
    w_far(2)
    attn_out[...] = out_part(mine) + b_out[...]
    w_far(3)
    for t in range(n_peer):
        copies.arrived(("out", t))
    for b in range(tokens // BLOCK):
        gate, shift, scale = vector(b, 2), vector(b, 3), 1.0 + vector(b, 4)

        def second(t, carry):
            part = pl.ds(pl.multiple_of(b * BLOCK + t * step, step), step)
            out = attn_out[part, :] + out_land[part, :].astype(F32)
            attn_out[part, :] = out
            resid = patches[part, :].astype(F32) + gate * out
            mlp2[part, :] = (norm(resid) * scale + shift).astype(BF)
            return carry

        lax.fori_loop(0, BLOCK // step, second, 0)
    copies.start("mlp", mlp2.at[mine], mlp2.at[theirs], at_core)
    copies.arrived("mlp")
    copies.arrived("gmo")
    for j in (1, 2, 3):
        for m in (1, 0):
            copies.arrived((("w_y", "w_x")[m], m, j))
            copies.arrived(("w_far", m, j))
    for made in own:
        made.wait()
    copies.finish(but=[("w_z", m, j) for m in range(2) for j in (2, 3)])

    @pl.when(mid)
    def _():
        for m in range(2):
            for j in (2, 3):
                copies.made["w_z", m, j].wait_send()
            for made in ends[m]:
                made.wait_send()

    for k, (ref, n) in enumerate(
        ((cond_all, n_dp), (ids_all, n_all), (bias_all, n_mp), (land, n_all))
    ):
        wait_all(ref, n - 1, small.at[2 * k])


def front(cond, ids, bias, w_ada, b_ada, patches, cotangent, seg, watt_own, w_fc1, w_fc2, bqv_own, b_out):
    n_dp, n_mp = lax.axis_size("dp"), lax.axis_size("mp")
    n_all, per_dp, width, cols = n_dp * n_mp, cond.shape[0], cond.shape[1], w_ada.shape[1]
    tokens, wide = patches.shape[0], watt_own.shape[1]
    sixth = w_fc2.shape[0] // 8
    cond8 = jnp.pad(cond.astype(F32), ((0, 8 - per_dp), (0, 0)))
    ids8 = jnp.pad(ids.astype(F32), (0, 8 - ids.shape[0]), constant_values=-1.0)
    row = jax.ShapeDtypeStruct((2 * tokens, wide), BF)
    lse = jax.ShapeDtypeStruct((wide // HP, 1, 2 * tokens), F32)
    shapes = (
        jax.ShapeDtypeStruct((n_dp * 8, width), BF),
        jax.ShapeDtypeStruct((n_all, 8, 128), F32),
        jax.ShapeDtypeStruct((16, sixth), F32),
        jax.ShapeDtypeStruct((8, 6 * width), F32),
        jax.ShapeDtypeStruct((2 * tokens, width), BF),
        *([row] * 8),
        lse,
        lse,
        jax.ShapeDtypeStruct(watt_own.shape, BF),
        jax.ShapeDtypeStruct((4, n_mp, sixth, width), BF),
        jax.ShapeDtypeStruct((4, n_mp, sixth, width), BF),
        jax.ShapeDtypeStruct((tokens, width), F32),
        jax.ShapeDtypeStruct((2 * tokens, width), BF),
        jax.ShapeDtypeStruct((2 * tokens, width), BF),
    )
    vmem, anywhere = pl.BlockSpec(memory_space=pltpu.VMEM), pl.BlockSpec(memory_space=pl.ANY)
    in_specs = [vmem] * 13
    in_specs[10] = anywhere
    out_specs = [vmem] * len(shapes)
    out_specs[16] = out_specs[17] = anywhere
    return pl.pallas_call(
        functools.partial(front_kernel, per_dp),
        out_shape=shapes,
        in_specs=in_specs,
        out_specs=out_specs,
        scratch_shapes=[
            pltpu.VMEM((n_dp, 8, width), F32),
            pltpu.VMEM((n_all, 8, 128), F32),
            pltpu.VMEM((n_mp, *bias.shape), F32),
            pltpu.VMEM((n_all, 8, cols), F32),
            pltpu.VMEM((n_all, 8, cols), F32),
            pltpu.VMEM((w_fc1.shape[1], width), BF),
            pltpu.VMEM((tokens, width), F32),
            pltpu.VMEM((tokens, width), BF),
            pltpu.VMEM((tokens, width), BF),
            pltpu.VMEM((2, wide, 2 * tokens), BF),
            pltpu.VMEM((wide, 2 * tokens), F32),
            pltpu.VMEM((8, wide), F32),
            pltpu.SemaphoreType.DMA((8,)),
            pltpu.SemaphoreType.DMA((8,)),
            pltpu.SemaphoreType.DMA((96,)),
        ],
        compiler_params=pltpu.CompilerParams(
            collective_id=0, has_side_effects=True, vmem_limit_bytes=62 << 20
        ),
    )(
        cond8,
        jnp.broadcast_to(ids8[:, None], (8, 128)),
        bias,
        w_ada,
        b_ada.astype(F32)[None],
        patches,
        cotangent,
        seg,
        watt_own,
        w_fc1,
        w_fc2,
        bqv_own,
        b_out.astype(F32)[None],
    )


def pad_heads(rows_in):
    *lead, n, width = rows_in.shape
    split = rows_in.reshape(*lead, n // HD, HD, width)
    pads = [(0, 0)] * (len(lead) + 1) + [(0, HP - HD), (0, 0)]
    return jnp.pad(split, pads).reshape(*lead, n // HD * HP, width)


def drop_pads(rows_in):
    *lead, n, width = rows_in.shape
    split = rows_in.reshape(*lead, n // HP, HP, width)[..., :HD, :]
    return split.reshape(*lead, n // HP * HD, width)


def on_device(
    patches,
    cotangent,
    conditioning,
    segment,
    image_ids,
    w_ada,
    b_ada,
    w_qkv,
    b_qv,
    w_out,
    b_out,
    w_fc1,
    b_fc1,
    w_fc2,
    b_fc2,
):
    n_dp, n_mp = lax.axis_size("dp"), lax.axis_size("mp")
    n_all = n_dp * n_mp
    z = lax.axis_index("mp")
    d = lax.axis_index("dp")
    core = d & 1
    everyone = ("dp", "mp")
    tokens, width = patches.shape
    n_blocks = tokens // BLOCK
    shard = w_fc2.shape[0]
    hidden_n = shard * n_mp

    q = (d >> 1) & 3
    sixth = shard // 8

    heads_shard = w_out.shape[0]
    watt_own = pad_heads(jnp.concatenate([w_qkv.transpose(0, 2, 1), w_out[None]], axis=0))
    wide = watt_own.shape[1]
    ids = image_ids.reshape(n_blocks, BLOCK)[:, 0]
    cols = w_ada.shape[1]
    bias = jnp.concatenate(
        [
            jnp.pad(b_fc1.astype(F32).reshape(8, sixth), ((0, 0), (0, heads_shard - sixth))),
            jnp.pad(b_qv.astype(F32), ((0, 6), (0, 0))),
        ]
    )
    bqv_own = jnp.pad(pad_heads(b_qv[..., None])[..., 0].astype(F32), ((0, 6), (0, 0)))
    seg_own = lax.dynamic_slice_in_dim(segment, z * tokens, tokens, 0)
    seg_peer = lax.dynamic_slice_in_dim(segment, (z ^ 1) * tokens, tokens, 0)
    seg = jnp.concatenate([seg_own, seg_peer])[:, None]
    (
        silu_cond, ids_all, b1_rel, mods, x_row, q0, k0, v0, q1, k1, v1, ctx_0, ctx_1,
        lse_0, lse_1, watt_other, w1_all, w2_all, attn_out, mlp2, gmo2,
    ) = front(
        conditioning, ids, bias, w_ada, b_ada, patches, cotangent, seg, watt_own, w_fc1, w_fc2,
        bqv_own, b_out,
    )
    heads_0, heads_1 = (q0, k0, v0), (q1, k1, v1)
    watts = [watt_own, watt_other]
    outs = [watt_own[3], watt_other[3]]
    w1_all, w2_all = [w.reshape(16 * sixth, width) for w in (w1_all, w2_all)]
    b1_all = b1_rel.reshape(16 * sixth)
    mods = mods[:n_blocks].reshape(n_blocks, 6, width)
    shift_attn, scale_attn, gate_attn, shift_mlp, scale_mlp, gate_mlp = [
        mods[:, i, None, :] for i in range(6)
    ]

    def blocks(v):
        return v.reshape(n_blocks, BLOCK, width)

    def flat(v):
        return v.reshape(tokens, width)

    patch_wide = blocks(patches.astype(F32))
    grad_output = blocks(cotangent.astype(F32))
    norm_a, rsig_a = layer_norm(patch_wide)
    attn_out = blocks(attn_out)
    resid = patch_wide + gate_attn * attn_out
    norm_m, rsig_m = layer_norm(resid)

    gmo = gmo2[:tokens]
    pre = dot(mlp2, w1_all, 1, 1) + b1_all
    act, act_grad = gelu_parts(pre)
    hidden = act.astype(BF)

    quad = 4 * sixth

    def grads(left, right, at, to):
        out = dot(left[:, at * quad : to * quad], right, 0, 0)
        return out.reshape(to - at, 4, sixth, width)

    def low_sum(a, b):
        return (a.astype(F32) + b.astype(F32)).astype(BF)

    send2 = grads(hidden, gmo2, 1, 3).astype(BF)
    come2 = swap(send2, "dp", 2)
    grad_pre = (dot(after(gmo2, send2), w2_all, 1, 1) * act_grad).astype(BF)
    grad_b1 = jnp.sum(grad_pre, axis=0, dtype=F32)
    send1 = grads(grad_pre, mlp2, 2, 4).astype(BF)
    come1 = swap(send1, "dp", 4)
    gin_peer = swap(dot(grad_pre[tokens:], w1_all, 1, 0).astype(BF), "dp", 1)
    g_mlp_in = blocks(dot(grad_pre[:tokens], w1_all, 1, 0) + gin_peer.astype(F32))
    g_shift_mlp = jnp.sum(g_mlp_in, axis=1)
    g_scale_mlp = jnp.sum(g_mlp_in * norm_m, axis=1)
    grad_resid = grad_output + norm_back(g_mlp_in, norm_m, rsig_m, scale_mlp)
    g_gate_attn = jnp.sum(grad_resid * attn_out, axis=1)
    gao = flat((gate_attn * grad_resid).astype(BF))
    grad_bout = jnp.sum(gao, axis=0, dtype=F32)
    gao_row = jnp.concatenate([gao, swap(gao, "mp", 1)], axis=0)

    hidden_w, gmo2_w, gpre_w, mlp2_w = lax.optimization_barrier(
        (hidden, gmo2, grad_pre, mlp2, gao)
    )[:4]
    mlp_peer = swap(dot(hidden_w[tokens:], w2_all, 1, 0).astype(BF), "dp", 1)
    keep2_2 = grads(hidden_w, gmo2_w, 3, 4)[0]
    keep2_0 = grads(hidden_w, gmo2_w, 0, 1)[0]
    mlp_out = blocks(
        dot(hidden_w[:tokens], w2_all, 1, 0) + mlp_peer.astype(F32) + b_fc2.astype(F32)
    )
    output = flat((resid + gate_mlp * mlp_out).astype(BF))
    g_gate_mlp = jnp.sum(grad_output * mlp_out, axis=1)
    grad_b2 = jnp.sum(gmo, axis=0, dtype=F32)

    def back(heads, out_w, lse, rows_in):
        grad_ctx = dot(rows_in, out_w, 1, 1).astype(BF)
        return attn_bwd(*heads, grad_ctx, lse)

    def att_grads(ctx, grad3):
        whole = jnp.concatenate(
            [dot(grad3, x_row, 0, 0).astype(BF), dot(ctx, gao_row, 0, 0).astype(BF)], axis=0
        )
        return drop_pads(whole.reshape(4, wide, width)).reshape(4, 2, sixth, width)

    def over_cores(grad_att):
        send = lax.dynamic_index_in_dim(grad_att, 1 - core, 1, keepdims=False)
        keep = lax.dynamic_index_in_dim(grad_att, core, 1, keepdims=False)
        got = low_sum(keep, swap(send, "dp", 1))
        return [pick(got, q ^ i) for i in range(4)]

    dq_1, dk_1, dv_1 = back(heads_1, outs[1], lse_1, gao_row)
    grad3_1 = jnp.concatenate([dq_1, dk_1, dv_1], axis=1)
    come2, come1 = lax.optimization_barrier((come2, come1, dq_1))[:2]
    two_2 = low_sum(keep2_2, come2[1])
    two_0 = low_sum(keep2_0, come2[0])
    come2 = swap(two_2, "dp", 4)
    keep1 = grads(gpre_w, mlp2_w, 0, 2)
    one_1 = low_sum(keep1[1], come1[0])
    one_0 = low_sum(keep1[0], come1[1])
    come1 = swap(one_1, "dp", 2)
    rel_b = over_cores(att_grads(ctx_1, grad3_1))
    dq_0, dk_0, dv_0 = back(heads_0, outs[0], lse_0, after(gao_row, one_1, rel_b[0]))
    come2, come1 = lax.optimization_barrier((come2, come1, dq_0))[:2]
    grad3_0 = jnp.concatenate([dq_0, dk_0, dv_0], axis=1)
    in_w = [w[:3].reshape(3 * wide, width) for w in watts]

    def g_in_part(at):
        return dot(grad3_0[at], in_w[0], 1, 0) + dot(grad3_1[at], in_w[1], 1, 0)

    g_peer = swap(g_in_part(slice(tokens, None)).astype(BF), "mp", 1)
    g_attn_in = blocks(g_in_part(slice(0, tokens)) + g_peer.astype(F32))
    plane2 = low_sum(two_0, come2)
    plane1 = low_sum(one_0, come1)
    rel_a = over_cores(att_grads(ctx_0, grad3_0))

    both = jnp.stack([plane1, plane2])
    whole = both[:, 0].astype(F32)
    for j in (1, 2, 3):
        whole = whole + swap(both[:, j], "mp", j).astype(F32)
    bit = 8
    while bit < n_dp:
        whole = whole + swap(whole.astype(BF), "dp", bit).astype(F32)
        bit *= 2
    done = whole.astype(BF)
    done_x = swap(done, "dp", 2)
    done_y = swap(done, "dp", 4)
    done_xy = jnp.stack([swap(done_x[0], "dp", 4), swap(done_y[1], "dp", 2)])
    mine = jnp.stack([done, done_x, done_y, done_xy])
    theirs = swap(mine, "dp", 1)

    spot = jnp.arange(8 * sixth)
    came = (spot // (4 * sixth)) ^ core, ((spot // sixth) % 4) ^ q
    target = (came[0] * 4 + came[1]) * sixth + spot % sixth
    places = (target[:, None] == spot[None, :]).astype(BF)
    rel = jnp.stack([mine, theirs])
    out_w1 = dot(rel[:, :, 0].reshape(shard, width), places, 0, 0)
    out_w2 = dot(places, rel[:, :, 1].reshape(shard, width), 0, 0)

    come_b = swap(jnp.stack([rel_b[2], rel_b[3]]), "dp", 4)
    b_1 = low_sum(rel_b[1], come_b[1])
    b_0 = low_sum(low_sum(rel_b[0], come_b[0]), swap(b_1, "dp", 2))
    come_a = swap(jnp.stack([rel_a[1], rel_a[3]]), "dp", 2)
    a_2 = low_sum(rel_a[2], come_a[1])
    a_0 = low_sum(low_sum(rel_a[0], come_a[0]), swap(a_2, "dp", 4))
    att = a_0.astype(F32) + swap(b_0, "mp", 2).astype(F32)
    bit = 8
    while bit < n_dp:
        att = att + swap(att.astype(BF), "dp", bit).astype(F32)
        bit *= 2
    att = att.astype(BF)
    att_x = swap(att, "dp", 2)
    att_y = swap(att, "dp", 4)
    att_mine = jnp.stack([att, att_x, att_y, swap(att_x, "dp", 4)])
    rel = jnp.stack([att_mine, swap(att_mine, "dp", 1)]).reshape(shard, width)
    target_att = (came[1] * 2 + came[0]) * sixth + spot % sixth
    places = (target_att[:, None] == spot[None, :]).astype(BF)
    cut = [places[:, m * heads_shard : (m + 1) * heads_shard] for m in range(4)]
    out_qkv = jnp.stack([dot(rel, cut[m], 0, 0) for m in range(3)])
    out_wout = dot(cut[3], rel, 0, 0)

    g_shift_attn = jnp.sum(g_attn_in, axis=1)
    g_scale_attn = jnp.sum(g_attn_in * norm_a, axis=1)
    grad_patches = flat(grad_resid + norm_back(g_attn_in, norm_a, rsig_a, scale_attn))
    sums = jnp.concatenate(
        [g_shift_attn, g_scale_attn, g_gate_attn, g_shift_mlp, g_scale_mlp, g_gate_mlp],
        axis=1,
    )
    to_owner = sums.reshape(n_blocks, n_all, cols).transpose(1, 0, 2)
    got = lax.all_to_all(to_owner, everyone, 0, 0).reshape(n_all * n_blocks, cols)
    ids_from = ids_all[:, :n_blocks, 0].reshape(1, n_all * n_blocks)
    images_here = conditioning.shape[0]
    row = jnp.arange(n_dp * 8)[:, None]
    image = jnp.where(row % 8 < images_here, row // 8 * images_here + row % 8, -2)
    belongs = (ids_from == image.astype(F32)).astype(F32)
    grad_cols = lax.dot_general(
        belongs,
        got,
        (((1,), (0,)), ((), ())),
        precision=lax.Precision.HIGHEST,
        preferred_element_type=F32,
    ).astype(BF)
    grad_w_ada = dot(silu_cond, grad_cols, 0, 0)
    grad_b_ada = jnp.sum(grad_cols, axis=0, dtype=F32)
    silu_part = dot(grad_cols, w_ada, 1, 1)
    silu_part = silu_part.reshape(n_dp, 8, width)[:, :images_here]

    bqv_g = jnp.stack(
        [
            jnp.stack([jnp.sum(v, axis=0, dtype=F32) for v in pair])
            for pair in ((dq_0, dv_0), (dq_1, dv_1))
        ]
    )
    bqv_g = drop_pads(bqv_g[..., None])[..., 0]
    shards = jnp.arange(n_mp)[:, None, None]
    bqv_all = jnp.where(shards == z, bqv_g[0][None], 0.0) + jnp.where(
        shards == (z ^ 2), bqv_g[1][None], 0.0
    )
    nat, rel_at = jnp.arange(8 * n_mp)[:, None], jnp.arange(16)[None, :]
    step = rel_at // 4
    step = jnp.where(step == 2, 3, jnp.where(step == 3, 2, step))
    comes = ((nat // 8) == (z ^ (rel_at % 4))) & ((nat % 4) == (q ^ step))
    comes = comes & (nat // 4 % 2 == core)
    grad_b1 = lax.dot_general(
        comes.astype(F32),
        grad_b1.reshape(16, sixth),
        (((1,), (0,)), ((), ())),
        precision=lax.Precision.HIGHEST,
        preferred_element_type=F32,
    )
    payload = jnp.concatenate(
        [
            jnp.broadcast_to(
                silu_part.reshape(n_dp, 1, images_here * width),
                (n_dp, n_mp, images_here * width),
            ),
            jnp.broadcast_to(
                jnp.concatenate([grad_bout, grad_b2])[None, None], (n_dp, n_mp, 2 * width)
            ),
            jnp.broadcast_to(grad_b1.reshape(1, n_mp, shard), (n_dp, n_mp, shard)),
            jnp.broadcast_to(
                bqv_all.reshape(1, n_mp, 2 * heads_shard), (n_dp, n_mp, 2 * heads_shard)
            ),
        ],
        axis=2,
    ).reshape(n_all, -1)
    summed = jnp.sum(lax.all_to_all(payload, everyone, 0, 0), axis=0)
    at = images_here * width
    grad_silu = summed[:at].reshape(images_here, width)
    _, silu_back = jax.vjp(silu_fn, conditioning.astype(F32))
    grad_cond = silu_back(grad_silu)[0]
    out_bout = summed[at : at + width]
    out_b2 = summed[at + width : at + 2 * width]
    at += 2 * width
    out_b1 = summed[at : at + shard]
    out_bqv = summed[at + shard :].reshape(2, heads_shard)

    return (
        output,
        grad_patches,
        grad_cond,
        grad_w_ada,
        grad_b_ada,
        out_qkv,
        out_bqv,
        out_wout,
        out_bout,
        out_w1,
        out_b1,
        out_w2,
        out_b2,
    )


def solution(mesh):
    rows = P(("dp", "mp"), None)
    in_specs = (
        rows,
        rows,
        P("dp", None),
        P("dp"),
        P(("dp", "mp")),
        P(None, ("dp", "mp")),
        P(("dp", "mp")),
        P(None, None, "mp"),
        P(None, "mp"),
        P("mp", None),
        P(),
        P(None, "mp"),
        P("mp"),
        P("mp", None),
        P(),
    )
    out_specs = (
        rows,
        rows,
        P("dp", None),
        P(None, ("dp", "mp")),
        P(("dp", "mp")),
        P(None, None, "mp"),
        P(None, "mp"),
        P("mp", None),
        P(),
        P(None, "mp"),
        P("mp"),
        P("mp", None),
        P(),
    )
    return jax.shard_map(
        on_device, mesh=mesh, in_specs=in_specs, out_specs=out_specs, check_vma=False
    )
```

```python
import functools
import math

import jax
import jax.numpy as jnp
from jax import lax
from jax.experimental import pallas as pl
from jax.experimental.pallas import tpu as pltpu
from jax.sharding import PartitionSpec as P

HD = 72
HP = 80
L = 1024
BLOCK = 256
BF = jnp.bfloat16
F32 = jnp.float32
SCALE = HD**-0.5
SCALE2 = SCALE * math.log2(math.e)
MASKED = -1e30
ORDER = (0, 1, 3, 2)


def swap(value, axis, bit):
    n = lax.axis_size(axis)
    return lax.ppermute(value, axis, [(i, i ^ bit) for i in range(n)])


def dot(a, b, ca, cb):
    return lax.dot_general(
        a, b, (((ca,), (cb,)), ((), ())), preferred_element_type=F32
    )


def after(value, *earlier):
    return lax.optimization_barrier((value, *earlier))[0]


def pick(stacked, index):
    return lax.dynamic_index_in_dim(stacked, index, 0, keepdims=False)


def layer_norm(vector):
    centred = vector - jnp.mean(vector, axis=-1, keepdims=True)
    spread = jnp.mean(centred * centred, axis=-1, keepdims=True)
    rsig = lax.rsqrt(spread + 1e-06)
    return centred * rsig, rsig


def norm_back(grad_in, normed, rsig, scale):
    u = grad_in * (1.0 + scale)
    mean_u = jnp.mean(u, axis=-1, keepdims=True)
    mean_un = jnp.mean(u * normed, axis=-1, keepdims=True)
    return (u - mean_u - normed * mean_un) * rsig


def gelu_parts(u):
    a = math.sqrt(2.0 / math.pi)
    t = jnp.tanh(a * (u + 0.044715 * u * u * u))
    return 0.5 * u * (1.0 + t), 0.5 * (1.0 + t) + 0.5 * u * (1.0 - t * t) * (
        a * (1.0 + 3 * 0.044715 * u * u)
    )


def silu_fn(values_in):
    return values_in * jax.nn.sigmoid(values_in)


def head_windows(width):
    found = []
    for h in range(width // HP):
        base = h * HP // 128 * 128
        end = min(-(-(h + 1) * HP // 128) * 128, width)
        found.append((base, end - base, h * HP - base))
    return found


PLACE = {0: 0, 1: 1, 3: 2, 2: 3}


def flip(index, bit):
    return index + bit - 2 * bit * lax.rem(index // bit, 2)


def flips(index, bits):
    for bit in (1, 2):
        index = flip(index, bit) if bits & bit else index
    return index


def coords(index, n_mp):
    return index // n_mp, lax.rem(index, n_mp)


def wait_all(ref, count, sem):
    whole = ref.at[pl.ds(0, count)]
    pltpu.make_async_copy(whole, whole, sem).wait()


class Copies:
    def __init__(self, sems):
        self.sems, self.made = sems, {}

    def make(self, name, src, dst, to):
        k = 2 * len(self.made)
        self.made[name] = pltpu.make_async_remote_copy(
            src_ref=src,
            dst_ref=dst,
            send_sem=self.sems.at[k],
            recv_sem=self.sems.at[k + 1],
            device_id=to,
            device_id_type=pl.DeviceIdType.MESH,
        )
        return self.made[name]

    def beside(self, name, src, dst, to):
        k = 2 * list(self.made).index(name)
        return pltpu.make_async_remote_copy(
            src_ref=src,
            dst_ref=dst,
            send_sem=self.sems.at[k],
            recv_sem=self.sems.at[k + 1],
            device_id=to,
            device_id_type=pl.DeviceIdType.MESH,
        )

    def start(self, name, src, dst, to):
        self.make(name, src, dst, to).start()

    def arrived(self, name):
        self.made[name].wait_recv()

    def finish(self, but=()):
        for name, made in self.made.items():
            if name not in but:
                made.wait_send()


def front_kernel(
    per_dp, cond, ids, bias, w_ada, b_ada, patches, cotangent, seg, watt_own, w_fc1, w_fc2, bqv_own, b_out,
    silu_out, ids_out, b1_out, mods, x_row, q0, k0, v0, q1, k1, v1, c0, c1, l0, l1,
    watt_other, w1_all, w2_all, attn_out, mlp2, gmo2,
    cond_all, ids_all, bias_all, send, land, w1t, normed, out_send, out_land, vts, ct, bqv_other,
    small, local, sems,
):
    n_dp, n_all, n_mp = cond_all.shape[0], ids_all.shape[0], bias_all.shape[0]
    tokens, width = patches.shape
    wide = watt_own.shape[1]
    sixth = b1_out.shape[1]
    half_w = wide // 2
    d, z = lax.axis_index("dp"), lax.axis_index("mp")
    me = d * n_mp + z
    core, q = lax.rem(d, 2), lax.rem(d // 2, 4)
    mid = (z == 1) | (z == 2)
    at_z = [(d, z), (d, flip(z, 1)), (d, flip(z, 2)), (d, 3 - z)]
    at_core, at_x, at_y = (flip(d, 1), z), (flip(d, 2), z), (flip(d, 4), z)
    copies = Copies(sems)
    barrier = pltpu.get_barrier_semaphore()

    def greet(t, carry):
        to = coords(lax.rem(me + t, n_all), n_mp)
        pl.semaphore_signal(barrier, inc=1, device_id=to, device_id_type=pl.DeviceIdType.MESH)
        return carry

    lax.fori_loop(1, n_all, greet, 0)
    pl.semaphore_wait(barrier, n_all - 1)

    def copy(src, dst, k, to):
        return pltpu.make_async_remote_copy(
            src_ref=src, dst_ref=dst, send_sem=small.at[2 * k], recv_sem=small.at[2 * k + 1],
            device_id=to, device_id_type=pl.DeviceIdType.MESH,
        )

    def send_cond(t, carry):
        copy(cond, cond_all.at[d], 0, (lax.rem(d + t, n_dp), z)).start()
        return carry

    def send_ids(t, carry):
        copy(ids, ids_all.at[me], 1, coords(lax.rem(me + t, n_all), n_mp)).start()
        return carry

    def send_bias(t, carry):
        copy(bias, bias_all.at[z], 2, (d, lax.rem(z + t, n_mp))).start()
        return carry

    lax.fori_loop(1, n_dp, send_cond, 0)
    lax.fori_loop(1, n_all, send_ids, 0)
    lax.fori_loop(1, n_mp, send_bias, 0)

    cond_all[d] = cond[...]
    ids_all[me] = ids[...]
    bias_all[z] = bias[...]
    w1t[...] = w_fc1[...].T
    for k, (ref, n) in enumerate(((cond_all, n_dp), (ids_all, n_all), (bias_all, n_mp))):
        wait_all(ref, n - 1, small.at[2 * k + 1])

    rows = n_dp * 8
    c = cond_all[...].reshape(rows, width)
    silu = (c * (1.0 / (1.0 + jnp.exp(-c)))).astype(BF)
    silu_out[...] = silu
    table = (dot(silu, w_ada[...], 1, 0) + b_ada[...]).astype(BF)
    k = lax.broadcasted_iota(jnp.int32, (n_all * 8, rows), 1)
    image = jnp.where(lax.rem(k, 8) < per_dp, k // 8 * per_dp + lax.rem(k, 8), -2)
    found = ids_all[...].reshape(n_all * 8, 128)[:, :1] == image.astype(F32)
    picked = dot(jnp.where(found, 1.0, 0.0).astype(BF), table, 1, 0)
    send[...] = picked.reshape(send.shape)

    def send_rows(t, carry):
        other = lax.rem(me + t, n_all)
        copy(send.at[other], land.at[me], 3, coords(other, n_mp)).start()
        return carry

    lax.fori_loop(1, n_all, send_rows, 0)
    my_half = pl.ds(pl.multiple_of(core * half_w, 16), half_w)
    copies.start("a_z", watt_own.at[q, my_half], watt_other.at[q, my_half], at_z[2])
    w_in, w_all, ends = [w1t, w_fc2], [w1_all, w2_all], {}

    def rows_of(i):
        return pl.ds(pl.multiple_of((core * 4 + flips(q, i)) * sixth, 16), sixth)

    for m in (1, 0):
        copies.start(("w_z", m, 1), w_in[m].at[rows_of(0)], w_all[m].at[0, 1], at_z[1])
        copies.make(("w_z", m, 3), w_in[m].at[rows_of(0)], w_all[m].at[0, 3], at_z[3])
        copies.make(("w_z", m, 2), w_all[m].at[0, 1], w_all[m].at[0, 2], at_z[3])
        ends[m] = [
            copies.beside(("w_z", m, there), w_all[m].at[0, here], w_all[m].at[0, there], at_z[1])
            for here, there in ((3, 2), (2, 3))
        ]

        @pl.when(mid)
        def _():
            copies.made["w_z", m, 3].start()

    own = [
        pltpu.make_async_copy(w_in[m].at[rows_of(i)], w_all[m].at[PLACE[i], 0], local.at[2 * i + m])
        for i in range(4)
        for m in range(2)
    ]
    for made in own:
        made.start()

    land[me] = send[me]
    ids_out[...] = ids_all[...]
    at = 0
    for i in ORDER:
        for j in range(n_mp):
            shard = 3 - z if j == 3 else flip(z, j) if j else z
            b1_out[at : at + 1, :] = bias_all[shard, pl.ds(core * 4 + flips(q, i), 1), :sixth]
            at += 1
    bqv = bias_all[flip(z, 2), 8:, :]
    heads = wide // HP
    bqv_other[...] = jnp.zeros_like(bqv_other)
    for h in range(heads):
        bqv_other[:, h * HP : h * HP + HD] = bqv[:, h * HD : (h + 1) * HD]

    step = 128

    def norm(v):
        centred = v - jnp.mean(v, axis=-1, keepdims=True)
        spread = jnp.mean(centred * centred, axis=-1, keepdims=True)
        return centred * lax.rsqrt(spread + 1e-06)

    def norm_patches(t, carry):
        part = pl.ds(pl.multiple_of(t * step, step), step)
        normed[part, :] = norm(patches[part, :].astype(F32))
        return carry

    lax.fori_loop(0, tokens // step, norm_patches, 0)
    copies.arrived("a_z")
    copies.start("a_c", watt_other.at[q, my_half], watt_other.at[q, my_half], at_core)
    wait_all(land, n_all - 1, small.at[7])
    cols = land.shape[2]
    for s in range(n_all):
        mods[:, s * cols : (s + 1) * cols] = land[s]

    def vector(b, which):
        return mods[b : b + 1, which * width : (which + 1) * width]

    for b in range(tokens // BLOCK):
        shift, scale = vector(b, 0), 1.0 + vector(b, 1)

        def modulate(t, carry):
            part = pl.ds(pl.multiple_of(b * BLOCK + t * step, step), step)
            x_row[part, :] = (normed[part, :] * scale + shift).astype(BF)
            return carry

        lax.fori_loop(0, BLOCK // step, modulate, 0)
    mine, theirs = slice(0, tokens), slice(tokens, 2 * tokens)
    copies.start("x", x_row.at[mine], x_row.at[theirs], at_z[1])
    for b in range(tokens // BLOCK):
        gate_mlp = vector(b, 5)

        def scaled(t, carry):
            part = pl.ds(pl.multiple_of(b * BLOCK + t * step, step), step)
            gmo2[part, :] = (gate_mlp * cotangent[part, :].astype(F32)).astype(BF)
            return carry

        lax.fori_loop(0, BLOCK // step, scaled, 0)
    copies.start("gmo", gmo2.at[mine], gmo2.at[theirs], at_core)

    def w_near(j):
        for m in (1, 0):
            copies.arrived(("w_z", m, j))
            if j == 1:

                @pl.when(mid)
                def _():
                    copies.made["w_z", m, 2].start()

            src = w_all[m].at[0, j]
            copies.start(("w_x", m, j), src, w_all[m].at[PLACE[1], j], at_x)
            copies.start(("w_y", m, j), src, w_all[m].at[PLACE[2], j], at_y)

    def w_near_late(j):
        @pl.when(jnp.logical_not(mid))
        def _():
            for m in (1, 0):
                copies.arrived(("w_z", m, j))

        for m in (1, 0):
            src = w_all[m].at[0, j]
            copies.start(("w_x", m, j), src, w_all[m].at[PLACE[1], j], at_x)
            copies.start(("w_y", m, j), src, w_all[m].at[PLACE[2], j], at_y)

    def w_far(j):
        for m, way, i, to in ((0, "w_x", 1, at_y), (1, "w_y", 2, at_x)):
            copies.arrived((way, m, j))
            copies.start(
                ("w_far", m, j), w_all[m].at[PLACE[i], j], w_all[m].at[PLACE[3], j], to
            )

    qx, qy = flips(q, 1), flips(q, 2)
    low, high = slice(0, half_w), slice(half_w, wide)

    lane = lax.rem(lax.broadcasted_iota(jnp.int32, (tokens, wide), 1), HP) - HD
    slots = ((watt_own, bqv_own, q0, k0, v0, c0, l0), (watt_other, bqv_other, q1, k1, v1, c1, l1))

    def project(slot, part):
        watt, bqv, qr, kr, vr = slots[slot][:5]
        x = x_row[part, :]
        same = lane == seg[part, :]
        marks = jnp.where(same, 1.0, 0.0)
        qr[part, :] = (dot(x, watt[0], 1, 1) + bqv[0:1, :] + marks).astype(BF)
        off = jnp.where((lane >= 0) & (lane < 4) & jnp.logical_not(same), MASKED, 0.0)
        kr[part, :] = (dot(x, watt[1], 1, 1) + off).astype(BF)
        vr[part, :] = (dot(x, watt[2], 1, 1) + bqv[1:2, :]).astype(BF)

    qb = 256

    def attend(slot, first, count):
        qr, kr, _, _, lr = slots[slot][2:]
        for h, (base, size, lo) in enumerate(head_windows(wide)):
            win = slice(base, base + size)
            ln = lax.broadcasted_iota(jnp.int32, (2 * tokens, size), 1)
            km = jnp.where((ln >= lo) & (ln < lo + HP), kr[:, win], jnp.zeros((), BF))
            head = slice(h * HP, (h + 1) * HP)
            vth = vts[slot, head, :]

            def block(j, carry):
                at = pl.ds(pl.multiple_of(j * qb, qb), qb)
                s = dot(km, qr[at, win], 1, 1)
                m = jnp.max(s, axis=0, keepdims=True) * SCALE2
                e = jnp.exp2(s * SCALE2 - m)
                total = jnp.sum(e, axis=0, keepdims=True)
                c = dot(vth, e.astype(BF), 1, 0)
                ct[head, at] = c / total
                lr[h, :, at] = m + jnp.log2(total)
                return carry

            lax.fori_loop(first, first + count, block, 0)
        part = slice(first * qb, (first + count) * qb)
        slots[slot][5][part, :] = ct[:, part].T.astype(BF)

    def out_part(part):
        return dot(c0[part, :], watt_own[3], 1, 0) + dot(c1[part, :], watt_other[3], 1, 0)

    def att_plane():
        copies.arrived("a_c")
        copies.start("a_x", watt_other.at[q], watt_other.at[q], at_x)
        copies.start("a_y", watt_other.at[q], watt_other.at[q], at_y)

    def att_far():
        copies.arrived("a_x")
        copies.start("a_xy", watt_other.at[qx, low], watt_other.at[qx, low], at_y)
        copies.arrived("a_y")
        copies.start("a_yx", watt_other.at[qy, high], watt_other.at[qy, high], at_x)

    def att_here():
        copies.arrived("a_xy")
        copies.arrived("a_yx")

    att_plane()
    project(0, mine)
    w_near(1)
    copies.arrived("x")

    @pl.when(mid)
    def _():
        for m in (1, 0):
            for j in (3, 2):
                copies.arrived(("w_z", m, j))
            for made in ends[m]:
                made.start()

    att_far()
    project(0, theirs)
    vts[0] = v0[...].T
    n_peer = tokens // qb
    attend(0, n_peer, n_peer)
    att_here()
    project(1, mine)
    project(1, theirs)
    vts[1] = v1[...].T
    for t in range(n_peer):
        attend(1, n_peer + t, 1)
        part = slice(t * qb, (t + 1) * qb)
        out_send[part, :] = out_part(slice(tokens + t * qb, tokens + (t + 1) * qb)).astype(BF)
        copies.start(("out", t), out_send.at[part], out_land.at[part], at_z[1])
        if t == 0:
            w_far(1)
    w_near_late(2)
    attend(0, 0, n_peer)
    w_near_late(3)
    attend(1, 0, n_peer)
    w_far(2)
    attn_out[...] = out_part(mine) + b_out[...]
    w_far(3)
    for t in range(n_peer):
        copies.arrived(("out", t))
    for b in range(tokens // BLOCK):
        gate, shift, scale = vector(b, 2), vector(b, 3), 1.0 + vector(b, 4)

        def second(t, carry):
            part = pl.ds(pl.multiple_of(b * BLOCK + t * step, step), step)
            out = attn_out[part, :] + out_land[part, :].astype(F32)
            attn_out[part, :] = out
            resid = patches[part, :].astype(F32) + gate * out
            mlp2[part, :] = (norm(resid) * scale + shift).astype(BF)
            return carry

        lax.fori_loop(0, BLOCK // step, second, 0)
    copies.start("mlp", mlp2.at[mine], mlp2.at[theirs], at_core)
    copies.arrived("mlp")
    copies.arrived("gmo")
    for j in (1, 2, 3):
        for m in (1, 0):
            copies.arrived((("w_y", "w_x")[m], m, j))
            copies.arrived(("w_far", m, j))
    for made in own:
        made.wait()
    copies.finish(but=[("w_z", m, j) for m in range(2) for j in (2, 3)])

    @pl.when(mid)
    def _():
        for m in range(2):
            for j in (2, 3):
                copies.made["w_z", m, j].wait_send()
            for made in ends[m]:
                made.wait_send()

    for k, (ref, n) in enumerate(
        ((cond_all, n_dp), (ids_all, n_all), (bias_all, n_mp), (land, n_all))
    ):
        wait_all(ref, n - 1, small.at[2 * k])


def front(cond, ids, bias, w_ada, b_ada, patches, cotangent, seg, watt_own, w_fc1, w_fc2, bqv_own, b_out):
    n_dp, n_mp = lax.axis_size("dp"), lax.axis_size("mp")
    n_all, per_dp, width, cols = n_dp * n_mp, cond.shape[0], cond.shape[1], w_ada.shape[1]
    tokens, wide = patches.shape[0], watt_own.shape[1]
    sixth = w_fc2.shape[0] // 8
    cond8 = jnp.pad(cond.astype(F32), ((0, 8 - per_dp), (0, 0)))
    ids8 = jnp.pad(ids.astype(F32), (0, 8 - ids.shape[0]), constant_values=-1.0)
    row = jax.ShapeDtypeStruct((2 * tokens, wide), BF)
    lse = jax.ShapeDtypeStruct((wide // HP, 1, 2 * tokens), F32)
    shapes = (
        jax.ShapeDtypeStruct((n_dp * 8, width), BF),
        jax.ShapeDtypeStruct((n_all, 8, 128), F32),
        jax.ShapeDtypeStruct((16, sixth), F32),
        jax.ShapeDtypeStruct((8, 6 * width), F32),
        jax.ShapeDtypeStruct((2 * tokens, width), BF),
        *([row] * 8),
        lse,
        lse,
        jax.ShapeDtypeStruct(watt_own.shape, BF),
        jax.ShapeDtypeStruct((4, n_mp, sixth, width), BF),
        jax.ShapeDtypeStruct((4, n_mp, sixth, width), BF),
        jax.ShapeDtypeStruct((tokens, width), F32),
        jax.ShapeDtypeStruct((2 * tokens, width), BF),
        jax.ShapeDtypeStruct((2 * tokens, width), BF),
    )
    vmem, anywhere = pl.BlockSpec(memory_space=pltpu.VMEM), pl.BlockSpec(memory_space=pl.ANY)
    in_specs = [vmem] * 13
    in_specs[10] = anywhere
    out_specs = [vmem] * len(shapes)
    out_specs[16] = out_specs[17] = anywhere
    return pl.pallas_call(
        functools.partial(front_kernel, per_dp),
        out_shape=shapes,
        in_specs=in_specs,
        out_specs=out_specs,
        scratch_shapes=[
            pltpu.VMEM((n_dp, 8, width), F32),
            pltpu.VMEM((n_all, 8, 128), F32),
            pltpu.VMEM((n_mp, *bias.shape), F32),
            pltpu.VMEM((n_all, 8, cols), F32),
            pltpu.VMEM((n_all, 8, cols), F32),
            pltpu.VMEM((w_fc1.shape[1], width), BF),
            pltpu.VMEM((tokens, width), F32),
            pltpu.VMEM((tokens, width), BF),
            pltpu.VMEM((tokens, width), BF),
            pltpu.VMEM((2, wide, 2 * tokens), BF),
            pltpu.VMEM((wide, 2 * tokens), F32),
            pltpu.VMEM((8, wide), F32),
            pltpu.SemaphoreType.DMA((8,)),
            pltpu.SemaphoreType.DMA((8,)),
            pltpu.SemaphoreType.DMA((96,)),
        ],
        compiler_params=pltpu.CompilerParams(
            collective_id=0, has_side_effects=True, vmem_limit_bytes=62 << 20
        ),
    )(
        cond8,
        jnp.broadcast_to(ids8[:, None], (8, 128)),
        bias,
        w_ada,
        b_ada.astype(F32)[None],
        patches,
        cotangent,
        seg,
        watt_own,
        w_fc1,
        w_fc2,
        bqv_own,
        b_out.astype(F32)[None],
    )


def back_kernel(
    per_dp, gao_row, x_row, watt_own, watt_other, q0, k0, v0, q1, k1, v1, c0, c1, l0, l1,
    two_2, two_0, one_1, one_0, patches, sums_4, b_sums, ids_all, w_ada,
    g_out, grad_cols, final, mlp_all, att_all,
    kt, dqt, wide_acc, gc, d3, att, core_land, come, plane, z_land, first_land, second_land,
    part_send, last_land, mlp_done, g_send, g_land, more_mlp, more_att,
    sums_6, col_send, col_land, row_send, shared, z_rows, small, sems,
):
    rows, width = gao_row.shape
    tokens = rows // 2
    wide = watt_own.shape[1]
    half = wide // 2
    d, z = lax.axis_index("dp"), lax.axis_index("mp")
    core, q = lax.rem(d, 2), lax.rem(d // 2, 4)
    at_z = [(d, z), (d, flip(z, 1)), (d, flip(z, 2)), (d, 3 - z)]
    at_core, at_x, at_y = (flip(d, 1), z), (flip(d, 2), z), (flip(d, 4), z)
    extra, bit = [], 8
    while bit < lax.axis_size("dp"):
        extra.append((flip(d, bit), z))
        bit *= 2
    barrier = pltpu.get_barrier_semaphore()
    n_dp, n_mp = lax.axis_size("dp"), lax.axis_size("mp")
    n_all, me = n_dp * n_mp, d * n_mp + z

    def greet(t, carry):
        to = coords(lax.rem(me + t, n_all), n_mp)
        pl.semaphore_signal(barrier, inc=1, device_id=to, device_id_type=pl.DeviceIdType.MESH)
        return carry

    lax.fori_loop(1, n_all, greet, 0)
    pl.semaphore_wait(barrier, n_all - 1)
    copies = Copies(sems)
    copies.start("two", two_2, come.at[1], at_y)
    copies.start("one", one_1, come.at[0], at_x)
    kept = [
        pltpu.make_async_copy(one_0, plane.at[0], sems.at[sems.shape[0] - 3]),
        pltpu.make_async_copy(two_0, plane.at[1], sems.at[sems.shape[0] - 4]),
    ]
    for made in kept:
        made.start()
    zero = jnp.zeros((), BF)
    qb = 256
    slots = ((watt_own, q0, k0, v0, c0, l0), (watt_other, q1, k1, v1, c1, l1))

    att_done = first_land.at[0, 0]
    dv_at = [slice(384 + base, 384 + base + size) for base, size, _ in head_windows(wide)]

    def back(slot):
        watt, qr, kr, vr, _, lr = slots[slot]
        for t in range(2):
            at = slice(t * tokens, (t + 1) * tokens)
            gc[at, :] = dot(gao_row[at, :], watt[3], 1, 1).astype(BF)
        kt[...] = kr[...].T
        wide_acc[...] = jnp.zeros_like(wide_acc)
        for h, (base, size, lo) in enumerate(head_windows(wide)):
            win = slice(base, base + size)
            lane = lax.broadcasted_iota(jnp.int32, (rows, size), 1)
            here = (lane >= lo) & (lane < lo + HP)
            km = jnp.where(here, kr[:, win], zero)
            vm = jnp.where(here, vr[:, win], zero)
            head = slice(h * HP, (h + 1) * HP)
            row = lax.broadcasted_iota(jnp.int32, (HP, rows), 0)
            kth = jnp.where(row < HD, kt[head, :], zero)
            lane_b = lax.broadcasted_iota(jnp.int32, (qb, size), 1)
            real = (lane_b >= lo) & (lane_b < lo + HD)

            def block(j, carry):
                at = pl.ds(pl.multiple_of(j * qb, qb), qb)
                q_blk = qr[at, win]
                g_blk = gc[at, win]
                s = dot(km, q_blk, 1, 1)
                p = jnp.exp2(s * SCALE2 - lr[h, :, at])
                dp = dot(vm, g_blk, 1, 1)
                delta = jnp.sum(p * dp, axis=0, keepdims=True)
                ds = (p * (dp - delta)).astype(BF)
                wide_acc[:rows, dv_at[h]] += dot(p.astype(BF), jnp.where(real, g_blk, zero), 1, 0)
                wide_acc[:rows, win] += dot(ds, jnp.where(real, q_blk, zero), 1, 0)
                dqt[head, at] = dot(kth, ds, 1, 0)
                return carry

            lax.fori_loop(0, rows // qb, block, 0)
        d3[slot, 0] = (dqt[...].T * SCALE).astype(BF)
        d3[slot, 1] = (wide_acc[:rows, :wide] * SCALE).astype(BF)
        d3[slot, 2] = wide_acc[:rows, 384 : 384 + wide].astype(BF)
        for n, m in enumerate((0, 2)):
            shared[6 + slot : 7 + slot, n * 384 : n * 384 + wide] = jnp.sum(
                d3[slot, m].astype(F32), axis=0, keepdims=True
            )

    def weight_grads(slot):
        ctx = slots[slot][4]

        def one(m, carry):
            att[m] = dot(d3[slot, m], x_row[...], 0, 0).astype(BF)
            return carry

        lax.fori_loop(0, 3, one, 0)
        att[3] = dot(ctx[...], gao_row[...], 0, 0).astype(BF)
        away = pl.ds(pl.multiple_of((1 - core) * half, 16), half)
        copies.start(("c", slot), att.at[:, away], core_land.at[slot], at_core)

    keep = pl.ds(pl.multiple_of(core * half, 16), half)

    def add(a, b):
        return (a.astype(F32) + b.astype(F32)).astype(BF)

    def core_sum(slot):
        copies.arrived(("c", slot))

        def one(m, carry):
            core_land[slot, m] = add(core_land[slot, m], att[m, keep])
            return carry

        lax.fori_loop(0, 4, one, 0)
        bits, to = ((1, at_x), (2, at_y))[slot]
        for n, i in enumerate((bits, 3)):
            copies.start(
                ("p", slot, n), core_land.at[slot, flips(q, i)], first_land.at[slot, n], to
            )

    def second_way(slot):
        other, to = ((2, at_y), (1, at_x))[slot]
        for n in range(2):
            copies.arrived(("p", slot, n))
        part_send[slot] = add(core_land[slot, flips(q, other)], first_land[slot, 1])
        copies.start(("s", slot), part_send.at[slot], second_land.at[slot], to)
        first_land[slot, 0] = add(core_land[slot, q], first_land[slot, 0])

    def plane_sum(slot):
        copies.arrived(("s", slot))
        first_land[slot, 0] = add(first_land[slot, 0], second_land[slot])

    shared[...] = b_sums[...]
    back(1)
    weight_grads(1)
    copies.arrived("two")
    copies.arrived("one")
    for m in (1, 0):
        kept[m].wait()

        def one(j, carry):
            plane[m, j] = add(plane[m, j], come[m, j])
            return carry

        lax.fori_loop(0, 4, one, 0)
        for j in (1, 2, 3):
            copies.start(("z", m, j), plane.at[m, j], z_land.at[m, j - 1], at_z[j])
    core_sum(1)
    back(0)
    second_way(1)

    def g_part(at):
        total = None
        for slot in (0, 1):
            for m in range(3):
                term = dot(d3[slot, m, at], slots[slot][0][m], 1, 0)
                total = term if total is None else total + term
        return total

    g_send[...] = g_part(slice(tokens, rows)).astype(BF)
    copies.start("g", g_send, g_land, at_z[1])
    plane_sum(1)
    copies.start("b", first_land.at[1, 0], last_land, at_z[2])
    copies.made["c", 1].wait_send()
    weight_grads(0)
    core_sum(0)
    g_out[...] = g_part(slice(0, tokens))
    second_way(0)
    for m in (1, 0):
        for j in (1, 2, 3):
            copies.arrived(("z", m, j))
        total = plane[m, 0].astype(F32)
        for j in (1, 2, 3):
            total = total + z_land[m, j - 1].astype(F32)
        mlp_done[m] = total.astype(BF)
    for n, to in enumerate(extra):
        copies.start(("mlp_more", n), mlp_done, more_mlp.at[n], to)
        copies.arrived(("mlp_more", n))
        copies.made["mlp_more", n].wait_send()
        mlp_done[...] = add(mlp_done[...], more_mlp[n])
    last = sems.shape[0]
    here = [pltpu.make_async_copy(mlp_done, mlp_all.at[core, q], sems.at[last - 1])]
    here[0].start()
    copies.start("m_x", mlp_done, mlp_all.at[core, q], at_x)
    copies.start("m_y", mlp_done, mlp_all.at[core, q], at_y)
    plane_sum(0)
    copies.arrived("b")
    att_done[...] = add(first_land[0, 0], last_land[...])
    for n, to in enumerate(extra):
        copies.start(("att_more", n), att_done, more_att.at[n], to)
        copies.arrived(("att_more", n))
        copies.made["att_more", n].wait_send()
        att_done[...] = add(att_done[...], more_att[n])
    here.append(pltpu.make_async_copy(att_done, att_all.at[q, core], sems.at[last - 2]))
    here[1].start()
    copies.start("a_x", att_done, att_all.at[q, core], at_x)
    copies.start("a_y", att_done, att_all.at[q, core], at_y)

    copies.made["g"].wait_send()
    fetch = pltpu.make_async_copy(patches, g_send, sems.at[last - 5])
    fetch.start()
    copies.arrived("g")
    step = 128
    sums_6[:, 2 * width :] = sums_4[...]
    sums_6[:, : 2 * width] = jnp.zeros((8, 2 * width), F32)
    fetch.wait()
    for b in range(tokens // BLOCK):

        def total(t, carry):
            part = pl.ds(pl.multiple_of(b * BLOCK + t * step, step), step)
            g = g_out[part, :] + g_land[part, :].astype(F32)
            g_out[part, :] = g
            v = g_send[part, :].astype(F32)
            centred = v - jnp.mean(v, axis=-1, keepdims=True)
            spread = jnp.mean(centred * centred, axis=-1, keepdims=True)
            scaled = g * (centred * lax.rsqrt(spread + 1e-06))
            return (
                carry[0] + jnp.sum(g, axis=0, keepdims=True),
                carry[1] + jnp.sum(scaled, axis=0, keepdims=True),
            )

        nothing = jnp.zeros((1, width), F32)
        shift, scale = lax.fori_loop(0, BLOCK // step, total, (nothing, nothing))
        sums_6[b : b + 1, :width] = shift
        sums_6[b : b + 1, width : 2 * width] = scale
    cols = col_send.shape[2]
    for t in range(n_all):
        col_send[t] = sums_6[:, t * cols : (t + 1) * cols]

    def remote(src, dst, k, to):
        return pltpu.make_async_remote_copy(
            src_ref=src, dst_ref=dst, send_sem=small.at[2 * k], recv_sem=small.at[2 * k + 1],
            device_id=to, device_id_type=pl.DeviceIdType.MESH,
        )

    def send_cols(t, carry):
        other = lax.rem(me + t, n_all)
        remote(col_send.at[other], col_land.at[me], 0, coords(other, n_mp)).start()
        return carry

    lax.fori_loop(1, n_all, send_cols, 0)
    col_land[me] = col_send[me]
    qx, qy = flips(q, 1), flips(q, 2)
    copies.arrived("m_x")
    copies.start("m_xy", mlp_all.at[core, qx, 0], mlp_all.at[core, qx, 0], at_y)
    copies.arrived("m_y")
    copies.start("m_yx", mlp_all.at[core, qy, 1], mlp_all.at[core, qy, 1], at_x)
    here[0].wait()
    for i in range(3):
        at = flips(q, i)
        copies.start(("m_c", i), mlp_all.at[core, at], mlp_all.at[core, at], at_core)
    copies.arrived("a_x")
    copies.start("a_xy", att_all.at[qx, core], att_all.at[qx, core], at_y)

    wait_all(col_land, n_all - 1, small.at[1])
    rows_8 = n_dp * 8
    some = min(32, n_all)
    k = lax.broadcasted_iota(jnp.int32, (some * 8, rows_8), 1)
    image = jnp.where(lax.rem(k, 8) < per_dp, k // 8 * per_dp + lax.rem(k, 8), -2).astype(F32)

    def collect(t, carry):
        part = pl.ds(t * some, some)
        found = ids_all[part].reshape(some * 8, 128)[:, :1] == image
        return carry + lax.dot_general(
            jnp.where(found, 1.0, 0.0),
            col_land[part].reshape(some * 8, cols),
            (((0,), (0,)), ((), ())),
            precision=lax.Precision.HIGHEST,
            preferred_element_type=F32,
        )

    summed = lax.fori_loop(0, n_all // some, collect, jnp.zeros((rows_8, cols), F32)).astype(BF)
    grad_cols[...] = summed
    silu_part = dot(summed, w_ada[...], 1, 1)
    row_send[...] = silu_part

    def block_of(t, size, start):
        return pl.ds(pl.multiple_of(t * size + start, 8), 8)

    def send_rows(t, carry):
        other = lax.rem(d + t, n_dp)
        to = (other, z)
        remote(row_send.at[block_of(other, 8, 0)], wide_acc.at[block_of(d, 16, 0)], 1, to).start()
        remote(shared, wide_acc.at[block_of(d, 16, 8)], 1, to).start()
        return carry

    lax.fori_loop(1, n_dp, send_rows, 0)
    wide_acc[block_of(d, 16, 0), :] = row_send[block_of(d, 8, 0), :]
    wide_acc[block_of(d, 16, 8), :] = shared[...]
    copies.arrived("m_xy")
    copies.arrived("m_yx")
    q3 = flips(q, 3)
    copies.start(("m_c", 3), mlp_all.at[core, q3], mlp_all.at[core, q3], at_core)
    copies.arrived("a_y")
    here[1].wait()
    copies.arrived("a_xy")
    copies.start("a_c", att_all.at[:, core], att_all.at[:, core], at_core)
    wait_all(wide_acc, (n_dp - 1) * 16, small.at[3])

    def sum_rows(t, carry):
        return carry + wide_acc[pl.ds(pl.multiple_of(t * 16, 16), 16), :]

    z_rows[0] = lax.fori_loop(0, n_dp, sum_rows, jnp.zeros((16, width), F32))
    for j in (1, 2, 3):
        copies.start(("rows", j), z_rows.at[0], z_rows.at[j], at_z[j])
    for j in (1, 2, 3):
        copies.arrived(("rows", j))
    final[...] = z_rows[0] + z_rows[1] + z_rows[2] + z_rows[3]
    final[14:15, :] = z_rows[0, 14:15, :] + z_rows[2, 15:16, :]
    for i in range(4):
        copies.arrived(("m_c", i))
    copies.arrived("a_c")
    copies.finish(but=[n for n in copies.made if n[0] in ("mlp_more", "att_more") or n in ("g", ("c", 1))])
    wait_all(col_land, n_all - 1, small.at[0])
    wait_all(wide_acc, (n_dp - 1) * 16, small.at[2])


def back(
    per_dp, gao_row, x_row, watt_own, watt_other, heads_0, heads_1, ctx, lse,
    two_2, two_0, one_1, one_0, patches, sums_4, b_sums, ids_all, w_ada,
):
    rows, width = gao_row.shape
    tokens, wide = rows // 2, watt_own.shape[1]
    half, sixth = wide // 2, two_2.shape[1]
    more = max(1, (lax.axis_size("dp") // 8).bit_length() - 1)
    n_dp, n_mp, cols = lax.axis_size("dp"), lax.axis_size("mp"), w_ada.shape[1]
    n_all = n_dp * n_mp
    shapes = (
        jax.ShapeDtypeStruct((tokens, width), F32),
        jax.ShapeDtypeStruct((n_dp * 8, cols), BF),
        jax.ShapeDtypeStruct((16, width), F32),
        jax.ShapeDtypeStruct((2, 4, 2, sixth, width), BF),
        jax.ShapeDtypeStruct((4, 2, half, width), BF),
    )
    vmem, anywhere = pl.BlockSpec(memory_space=pltpu.VMEM), pl.BlockSpec(memory_space=pl.ANY)
    return pl.pallas_call(
        functools.partial(back_kernel, per_dp),
        out_shape=shapes,
        in_specs=[vmem] * 14 + [anywhere] * 5 + [vmem] * 4,
        out_specs=[vmem, vmem, vmem, anywhere, anywhere],
        scratch_shapes=[
            pltpu.VMEM((wide, rows), BF),
            pltpu.VMEM((wide, rows), F32),
            pltpu.VMEM((max(rows, n_dp * 16), width), F32),
            pltpu.VMEM((rows, wide), BF),
            pltpu.VMEM((2, 3, rows, wide), BF),
            pltpu.VMEM((4, wide, width), BF),
            pltpu.VMEM((2, 4, half, width), BF),
            pltpu.VMEM((2, 4, sixth, width), BF),
            pltpu.VMEM((2, 4, sixth, width), BF),
            pltpu.VMEM((2, 3, sixth, width), BF),
            pltpu.VMEM((2, 2, half, width), BF),
            pltpu.VMEM((2, half, width), BF),
            pltpu.VMEM((2, half, width), BF),
            pltpu.VMEM((half, width), BF),
            pltpu.VMEM((2, sixth, width), BF),
            pltpu.VMEM((tokens, width), BF),
            pltpu.VMEM((tokens, width), BF),
            pltpu.VMEM((more, 2, sixth, width), BF),
            pltpu.VMEM((more, half, width), BF),
            pltpu.VMEM((8, 6 * width), F32),
            pltpu.VMEM((n_all, 8, cols), F32),
            pltpu.VMEM((n_all, 8, cols), F32),
            pltpu.VMEM((n_dp * 8, width), F32),
            pltpu.VMEM((8, width), F32),
            pltpu.VMEM((4, 16, width), F32),
            pltpu.SemaphoreType.DMA((4,)),
            pltpu.SemaphoreType.DMA((96,)),
        ],
        compiler_params=pltpu.CompilerParams(
            collective_id=1, has_side_effects=True, vmem_limit_bytes=63 << 20
        ),
    )(
        gao_row, x_row, watt_own, watt_other, *heads_0, *heads_1, *ctx, *lse,
        two_2, two_0, one_1, one_0, patches, sums_4, b_sums, ids_all, w_ada,
    )


def pad_heads(rows_in):
    *lead, n, width = rows_in.shape
    split = rows_in.reshape(*lead, n // HD, HD, width)
    pads = [(0, 0)] * (len(lead) + 1) + [(0, HP - HD), (0, 0)]
    return jnp.pad(split, pads).reshape(*lead, n // HD * HP, width)


def drop_pads(rows_in):
    *lead, n, width = rows_in.shape
    split = rows_in.reshape(*lead, n // HP, HP, width)[..., :HD, :]
    return split.reshape(*lead, n // HP * HD, width)


def on_device(
    patches,
    cotangent,
    conditioning,
    segment,
    image_ids,
    w_ada,
    b_ada,
    w_qkv,
    b_qv,
    w_out,
    b_out,
    w_fc1,
    b_fc1,
    w_fc2,
    b_fc2,
):
    n_dp, n_mp = lax.axis_size("dp"), lax.axis_size("mp")
    n_all = n_dp * n_mp
    z = lax.axis_index("mp")
    d = lax.axis_index("dp")
    core = d & 1
    everyone = ("dp", "mp")
    tokens, width = patches.shape
    n_blocks = tokens // BLOCK
    shard = w_fc2.shape[0]
    hidden_n = shard * n_mp

    q = (d >> 1) & 3
    sixth = shard // 8

    heads_shard = w_out.shape[0]
    watt_own = pad_heads(jnp.concatenate([w_qkv.transpose(0, 2, 1), w_out[None]], axis=0))
    wide = watt_own.shape[1]
    ids = image_ids.reshape(n_blocks, BLOCK)[:, 0]
    cols = w_ada.shape[1]
    bias = jnp.concatenate(
        [
            jnp.pad(b_fc1.astype(F32).reshape(8, sixth), ((0, 0), (0, heads_shard - sixth))),
            jnp.pad(b_qv.astype(F32), ((0, 6), (0, 0))),
        ]
    )
    bqv_own = jnp.pad(pad_heads(b_qv[..., None])[..., 0].astype(F32), ((0, 6), (0, 0)))
    seg_own = lax.dynamic_slice_in_dim(segment, z * tokens, tokens, 0)
    seg_peer = lax.dynamic_slice_in_dim(segment, (z ^ 1) * tokens, tokens, 0)
    seg = jnp.concatenate([seg_own, seg_peer])[:, None]
    (
        silu_cond, ids_all, b1_rel, mods, x_row, q0, k0, v0, q1, k1, v1, ctx_0, ctx_1,
        lse_0, lse_1, watt_other, w1_all, w2_all, attn_out, mlp2, gmo2,
    ) = front(
        conditioning, ids, bias, w_ada, b_ada, patches, cotangent, seg, watt_own, w_fc1, w_fc2,
        bqv_own, b_out,
    )
    heads_0, heads_1 = (q0, k0, v0), (q1, k1, v1)
    w1_all, w2_all = [w.reshape(16 * sixth, width) for w in (w1_all, w2_all)]
    b1_all = b1_rel.reshape(16 * sixth)
    mods = mods[:n_blocks].reshape(n_blocks, 6, width)
    shift_attn, scale_attn, gate_attn, shift_mlp, scale_mlp, gate_mlp = [
        mods[:, i, None, :] for i in range(6)
    ]

    def blocks(v):
        return v.reshape(n_blocks, BLOCK, width)

    def flat(v):
        return v.reshape(tokens, width)

    patch_wide = blocks(patches.astype(F32))
    grad_output = blocks(cotangent.astype(F32))
    norm_a, rsig_a = layer_norm(patch_wide)
    attn_out = blocks(attn_out)
    resid = patch_wide + gate_attn * attn_out
    norm_m, rsig_m = layer_norm(resid)

    gmo = gmo2[:tokens]
    pre = dot(mlp2, w1_all, 1, 1) + b1_all
    act, act_grad = gelu_parts(pre)
    hidden = act.astype(BF)

    quad = 4 * sixth

    def grads(left, right, at, to):
        out = dot(left[:, at * quad : to * quad], right, 0, 0)
        return out.reshape(to - at, 4, sixth, width)

    def low_sum(a, b):
        return (a.astype(F32) + b.astype(F32)).astype(BF)

    send2 = grads(hidden, gmo2, 1, 3).astype(BF)
    come2 = swap(send2, "dp", 2)
    grad_pre = (dot(after(gmo2, send2), w2_all, 1, 1) * act_grad).astype(BF)
    grad_b1 = jnp.sum(grad_pre, axis=0, dtype=F32)
    send1 = grads(grad_pre, mlp2, 2, 4).astype(BF)
    come1 = swap(send1, "dp", 4)
    gin_peer = swap(dot(grad_pre[tokens:], w1_all, 1, 0).astype(BF), "dp", 1)
    g_mlp_in = blocks(dot(grad_pre[:tokens], w1_all, 1, 0) + gin_peer.astype(F32))
    g_shift_mlp = jnp.sum(g_mlp_in, axis=1)
    g_scale_mlp = jnp.sum(g_mlp_in * norm_m, axis=1)
    grad_resid = grad_output + norm_back(g_mlp_in, norm_m, rsig_m, scale_mlp)
    g_gate_attn = jnp.sum(grad_resid * attn_out, axis=1)
    gao = flat((gate_attn * grad_resid).astype(BF))
    grad_bout = jnp.sum(gao, axis=0, dtype=F32)
    gao_row = jnp.concatenate([gao, swap(gao, "mp", 1)], axis=0)

    hidden_w, gmo2_w, gpre_w, mlp2_w = lax.optimization_barrier(
        (hidden, gmo2, grad_pre, mlp2, gao)
    )[:4]
    mlp_peer = swap(dot(hidden_w[tokens:], w2_all, 1, 0).astype(BF), "dp", 1)
    keep2_2 = grads(hidden_w, gmo2_w, 3, 4)[0]
    keep2_0 = grads(hidden_w, gmo2_w, 0, 1)[0]
    mlp_out = blocks(
        dot(hidden_w[:tokens], w2_all, 1, 0) + mlp_peer.astype(F32) + b_fc2.astype(F32)
    )
    output = flat((resid + gate_mlp * mlp_out).astype(BF))
    g_gate_mlp = jnp.sum(grad_output * mlp_out, axis=1)
    grad_b2 = jnp.sum(gmo, axis=0, dtype=F32)

    come2, come1 = lax.optimization_barrier((come2, come1, keep2_0))[:2]
    two_2 = low_sum(keep2_2, come2[1])
    two_0 = low_sum(keep2_0, come2[0])
    keep1 = grads(gpre_w, mlp2_w, 0, 2)
    one_1 = low_sum(keep1[1], come1[0])
    one_0 = low_sum(keep1[0], come1[1])
    nat, rel_at = jnp.arange(8 * n_mp)[:, None], jnp.arange(16)[None, :]
    step = rel_at // 4
    step = jnp.where(step == 2, 3, jnp.where(step == 3, 2, step))
    comes = ((nat // 8) == (z ^ (rel_at % 4))) & ((nat % 4) == (q ^ step))
    comes = comes & (nat // 4 % 2 == core)
    grad_b1 = lax.dot_general(
        comes.astype(F32),
        grad_b1.reshape(16, sixth),
        (((1,), (0,)), ((), ())),
        precision=lax.Precision.HIGHEST,
        preferred_element_type=F32,
    )
    b_sums = jnp.concatenate(
        [grad_bout[None], grad_b2[None], grad_b1.reshape(n_mp, shard), jnp.zeros((2, width), F32)]
    )
    sums_4 = jnp.concatenate([g_gate_attn, g_shift_mlp, g_scale_mlp, g_gate_mlp], axis=1)
    sums_4 = jnp.pad(sums_4, ((0, 8 - n_blocks), (0, 0)))
    g_attn_in, grad_cols, final, mlp_all, att_all = back(
        conditioning.shape[0], gao_row, x_row, watt_own, watt_other, heads_0, heads_1,
        (ctx_0, ctx_1), (lse_0, lse_1), two_2, two_0, one_1, one_0, patches, sums_4, b_sums,
        ids_all, w_ada,
    )
    g_attn_in = blocks(g_attn_in)
    out_w1 = mlp_all[:, :, 0].reshape(shard, width)
    unit = (jnp.arange(shard)[:, None] == jnp.arange(shard)[None, :]).astype(BF)
    out_w1 = dot(out_w1, unit, 0, 0)
    out_w2 = mlp_all[:, :, 1].reshape(shard, width).astype(F32)
    att_all = drop_pads(att_all.reshape(4, wide, width))
    out_qkv = att_all[:3].transpose(0, 2, 1).astype(F32)
    out_wout = att_all[3].astype(F32)
    grad_patches = flat(grad_resid + norm_back(g_attn_in, norm_a, rsig_a, scale_attn))
    grad_w_ada = dot(silu_cond, grad_cols, 0, 0)
    grad_b_ada = jnp.sum(grad_cols, axis=0, dtype=F32)
    grad_silu = final[: conditioning.shape[0]]
    _, silu_back = jax.vjp(silu_fn, conditioning.astype(F32))
    grad_cond = silu_back(grad_silu)[0]
    out_bout, out_b2 = final[8], final[9]
    out_b1 = lax.dynamic_index_in_dim(final, 10 + z, 0, keepdims=False)
    out_bqv = jnp.stack([final[14, :wide], final[14, 384 : 384 + wide]])
    out_bqv = drop_pads(out_bqv[..., None])[..., 0]

    return (
        output,
        grad_patches,
        grad_cond,
        grad_w_ada,
        grad_b_ada,
        out_qkv,
        out_bqv,
        out_wout,
        out_bout,
        out_w1,
        out_b1,
        out_w2,
        out_b2,
    )


def solution(mesh):
    rows = P(("dp", "mp"), None)
    in_specs = (
        rows,
        rows,
        P("dp", None),
        P("dp"),
        P(("dp", "mp")),
        P(None, ("dp", "mp")),
        P(("dp", "mp")),
        P(None, None, "mp"),
        P(None, "mp"),
        P("mp", None),
        P(),
        P(None, "mp"),
        P("mp"),
        P("mp", None),
        P(),
    )
    out_specs = (
        rows,
        rows,
        P("dp", None),
        P(None, ("dp", "mp")),
        P(("dp", "mp")),
        P(None, None, "mp"),
        P(None, "mp"),
        P("mp", None),
        P(),
        P(None, "mp"),
        P("mp"),
        P("mp", None),
        P(),
    )
    return jax.shard_map(
        on_device, mesh=mesh, in_specs=in_specs, out_specs=out_specs, check_vma=False
    )
```

```python
import functools
import math

import jax
import jax.numpy as jnp
from jax import lax
from jax.experimental import pallas as pl
from jax.experimental.pallas import tpu as pltpu
from jax.sharding import PartitionSpec as P

HD = 72
HP = 80
L = 1024
BLOCK = 256
BF = jnp.bfloat16
F32 = jnp.float32
SCALE = HD**-0.5
SCALE2 = SCALE * math.log2(math.e)
MASKED = -1e30
ORDER = (0, 1, 3, 2)


def swap(value, axis, bit):
    n = lax.axis_size(axis)
    return lax.ppermute(value, axis, [(i, i ^ bit) for i in range(n)])


def dot(a, b, ca, cb):
    return lax.dot_general(
        a, b, (((ca,), (cb,)), ((), ())), preferred_element_type=F32
    )


def after(value, *earlier):
    return lax.optimization_barrier((value, *earlier))[0]


def pick(stacked, index):
    return lax.dynamic_index_in_dim(stacked, index, 0, keepdims=False)


def layer_norm(vector):
    centred = vector - jnp.mean(vector, axis=-1, keepdims=True)
    spread = jnp.mean(centred * centred, axis=-1, keepdims=True)
    rsig = lax.rsqrt(spread + 1e-06)
    return centred * rsig, rsig


def norm_back(u, normed, rsig):
    mean_u = jnp.mean(u, axis=-1, keepdims=True)
    mean_un = jnp.mean(u * normed, axis=-1, keepdims=True)
    return (u - mean_u - normed * mean_un) * rsig


def gelu_parts(u):
    a = math.sqrt(2.0 / math.pi)
    t = jnp.tanh(a * (u + 0.044715 * u * u * u))
    return 0.5 * u * (1.0 + t), 0.5 * (1.0 + t) + 0.5 * u * (1.0 - t * t) * (
        a * (1.0 + 3 * 0.044715 * u * u)
    )


def silu_fn(values_in):
    return values_in * jax.nn.sigmoid(values_in)


def head_windows(width):
    found = []
    for h in range(width // HP):
        base = h * HP // 128 * 128
        end = min(-(-(h + 1) * HP // 128) * 128, width)
        found.append((base, end - base, h * HP - base))
    return found


PLACE = {0: 0, 1: 1, 3: 2, 2: 3}


def flip(index, bit):
    return index + bit - 2 * bit * lax.rem(index // bit, 2)


def flips(index, bits):
    for bit in (1, 2):
        index = flip(index, bit) if bits & bit else index
    return index


def coords(index, n_mp):
    return index // n_mp, lax.rem(index, n_mp)


def wait_all(ref, count, sem):
    whole = ref.at[pl.ds(0, count)]
    pltpu.make_async_copy(whole, whole, sem).wait()


class Copies:
    def __init__(self, sems):
        self.sems, self.made = sems, {}

    def make(self, name, src, dst, to):
        k = 2 * len(self.made)
        self.made[name] = pltpu.make_async_remote_copy(
            src_ref=src,
            dst_ref=dst,
            send_sem=self.sems.at[k],
            recv_sem=self.sems.at[k + 1],
            device_id=to,
            device_id_type=pl.DeviceIdType.MESH,
        )
        return self.made[name]

    def beside(self, name, src, dst, to):
        k = 2 * list(self.made).index(name)
        return pltpu.make_async_remote_copy(
            src_ref=src,
            dst_ref=dst,
            send_sem=self.sems.at[k],
            recv_sem=self.sems.at[k + 1],
            device_id=to,
            device_id_type=pl.DeviceIdType.MESH,
        )

    def start(self, name, src, dst, to):
        self.make(name, src, dst, to).start()

    def arrived(self, name):
        self.made[name].wait_recv()

    def finish(self, but=()):
        for name, made in self.made.items():
            if name not in but:
                made.wait_send()


def front_kernel(
    per_dp, cond, ids, bias, w_ada, b_ada, patches, cotangent, seg, watt_own, w_fc1, w_fc2, bqv_own, b_out,
    silu_out, ids_out, b1_out, mods, x_row, q0, k0, v0, q1, k1, v1, c0, c1, l0, l1,
    watt_other, w1_all, w2_all, attn_out, mlp2, gmo2,
    cond_all, ids_all, bias_all, send, land, w1t, normed, out_send, out_land, vts, ct, bqv_other,
    small, local, sems,
):
    n_dp, n_all, n_mp = cond_all.shape[0], ids_all.shape[0], bias_all.shape[0]
    tokens, width = patches.shape
    wide = watt_own.shape[1]
    sixth = b1_out.shape[1]
    half_w = wide // 2
    d, z = lax.axis_index("dp"), lax.axis_index("mp")
    me = d * n_mp + z
    core, q = lax.rem(d, 2), lax.rem(d // 2, 4)
    mid = (z == 1) | (z == 2)
    at_z = [(d, z), (d, flip(z, 1)), (d, flip(z, 2)), (d, 3 - z)]
    at_core, at_x, at_y = (flip(d, 1), z), (flip(d, 2), z), (flip(d, 4), z)
    copies = Copies(sems)
    barrier = pltpu.get_barrier_semaphore()

    def greet(t, carry):
        to = coords(lax.rem(me + t, n_all), n_mp)
        pl.semaphore_signal(barrier, inc=1, device_id=to, device_id_type=pl.DeviceIdType.MESH)
        return carry

    lax.fori_loop(1, n_all, greet, 0)
    pl.semaphore_wait(barrier, n_all - 1)

    def copy(src, dst, k, to):
        return pltpu.make_async_remote_copy(
            src_ref=src, dst_ref=dst, send_sem=small.at[2 * k], recv_sem=small.at[2 * k + 1],
            device_id=to, device_id_type=pl.DeviceIdType.MESH,
        )

    def send_cond(t, carry):
        copy(cond, cond_all.at[d], 0, (lax.rem(d + t, n_dp), z)).start()
        return carry

    def send_ids(t, carry):
        copy(ids, ids_all.at[me], 1, coords(lax.rem(me + t, n_all), n_mp)).start()
        return carry

    def send_bias(t, carry):
        copy(bias, bias_all.at[z], 2, (d, lax.rem(z + t, n_mp))).start()
        return carry

    lax.fori_loop(1, n_dp, send_cond, 0)
    lax.fori_loop(1, n_all, send_ids, 0)
    lax.fori_loop(1, n_mp, send_bias, 0)

    cond_all[d] = cond[...]
    ids_all[me] = ids[...]
    bias_all[z] = bias[...]
    w1t[...] = w_fc1[...].T
    for k, (ref, n) in enumerate(((cond_all, n_dp), (ids_all, n_all), (bias_all, n_mp))):
        wait_all(ref, n - 1, small.at[2 * k + 1])

    rows = n_dp * 8
    c = cond_all[...].reshape(rows, width)
    silu = (c * (1.0 / (1.0 + jnp.exp(-c)))).astype(BF)
    silu_out[...] = silu
    table = (dot(silu, w_ada[...], 1, 0) + b_ada[...]).astype(BF)
    k = lax.broadcasted_iota(jnp.int32, (n_all * 8, rows), 1)
    image = jnp.where(lax.rem(k, 8) < per_dp, k // 8 * per_dp + lax.rem(k, 8), -2)
    found = ids_all[...].reshape(n_all * 8, 128)[:, :1] == image.astype(F32)
    picked = dot(jnp.where(found, 1.0, 0.0).astype(BF), table, 1, 0)
    send[...] = picked.reshape(send.shape)

    def send_rows(t, carry):
        other = lax.rem(me + t, n_all)
        copy(send.at[other], land.at[me], 3, coords(other, n_mp)).start()
        return carry

    lax.fori_loop(1, n_all, send_rows, 0)
    my_half = pl.ds(pl.multiple_of(core * half_w, 16), half_w)
    copies.start("a_z", watt_own.at[q, my_half], watt_other.at[q, my_half], at_z[2])
    w_in, w_all, ends = [w1t, w_fc2], [w1_all, w2_all], {}

    def rows_of(i):
        return pl.ds(pl.multiple_of((core * 4 + flips(q, i)) * sixth, 16), sixth)

    for m in (1, 0):
        copies.start(("w_z", m, 1), w_in[m].at[rows_of(0)], w_all[m].at[0, 1], at_z[1])
        copies.make(("w_z", m, 3), w_in[m].at[rows_of(0)], w_all[m].at[0, 3], at_z[3])
        copies.make(("w_z", m, 2), w_all[m].at[0, 1], w_all[m].at[0, 2], at_z[3])
        ends[m] = [
            copies.beside(("w_z", m, there), w_all[m].at[0, here], w_all[m].at[0, there], at_z[1])
            for here, there in ((3, 2), (2, 3))
        ]

        @pl.when(mid)
        def _():
            copies.made["w_z", m, 3].start()

    own = [
        pltpu.make_async_copy(w_in[m].at[rows_of(i)], w_all[m].at[PLACE[i], 0], local.at[2 * i + m])
        for i in range(4)
        for m in range(2)
    ]
    for made in own:
        made.start()

    land[me] = send[me]
    ids_out[...] = ids_all[...]
    at = 0
    for i in ORDER:
        for j in range(n_mp):
            shard = 3 - z if j == 3 else flip(z, j) if j else z
            b1_out[at : at + 1, :] = bias_all[shard, pl.ds(core * 4 + flips(q, i), 1), :sixth]
            at += 1
    bqv = bias_all[flip(z, 2), 8:, :]
    heads = wide // HP
    bqv_other[...] = jnp.zeros_like(bqv_other)
    for h in range(heads):
        bqv_other[:, h * HP : h * HP + HD] = bqv[:, h * HD : (h + 1) * HD]

    step = 128

    def norm(v):
        centred = v - jnp.mean(v, axis=-1, keepdims=True)
        spread = jnp.mean(centred * centred, axis=-1, keepdims=True)
        return centred * lax.rsqrt(spread + 1e-06)

    def norm_patches(t, carry):
        part = pl.ds(pl.multiple_of(t * step, step), step)
        normed[part, :] = norm(patches[part, :].astype(F32))
        return carry

    lax.fori_loop(0, tokens // step, norm_patches, 0)
    copies.arrived("a_z")
    copies.start("a_c", watt_other.at[q, my_half], watt_other.at[q, my_half], at_core)
    wait_all(land, n_all - 1, small.at[7])
    cols = land.shape[2]
    for s in range(n_all):
        mods[:, s * cols : (s + 1) * cols] = land[s]

    def vector(b, which):
        return mods[b : b + 1, which * width : (which + 1) * width]

    for b in range(tokens // BLOCK):
        shift, scale = vector(b, 0), 1.0 + vector(b, 1)

        def modulate(t, carry):
            part = pl.ds(pl.multiple_of(b * BLOCK + t * step, step), step)
            x_row[part, :] = (normed[part, :] * scale + shift).astype(BF)
            return carry

        lax.fori_loop(0, BLOCK // step, modulate, 0)
    mine, theirs = slice(0, tokens), slice(tokens, 2 * tokens)
    copies.start("x", x_row.at[mine], x_row.at[theirs], at_z[1])
    for b in range(tokens // BLOCK):
        gate_mlp = vector(b, 5)

        def scaled(t, carry):
            part = pl.ds(pl.multiple_of(b * BLOCK + t * step, step), step)
            gmo2[part, :] = (gate_mlp * cotangent[part, :].astype(F32)).astype(BF)
            return carry

        lax.fori_loop(0, BLOCK // step, scaled, 0)
    copies.start("gmo", gmo2.at[mine], gmo2.at[theirs], at_core)

    def w_near(j):
        for m in (1, 0):
            copies.arrived(("w_z", m, j))
            if j == 1:

                @pl.when(mid)
                def _():
                    copies.made["w_z", m, 2].start()

            src = w_all[m].at[0, j]
            copies.start(("w_x", m, j), src, w_all[m].at[PLACE[1], j], at_x)
            copies.start(("w_y", m, j), src, w_all[m].at[PLACE[2], j], at_y)

    def w_near_late(j):
        @pl.when(jnp.logical_not(mid))
        def _():
            for m in (1, 0):
                copies.arrived(("w_z", m, j))

        for m in (1, 0):
            src = w_all[m].at[0, j]
            copies.start(("w_x", m, j), src, w_all[m].at[PLACE[1], j], at_x)
            copies.start(("w_y", m, j), src, w_all[m].at[PLACE[2], j], at_y)

    def w_far(j):
        for m, way, i, to in ((0, "w_x", 1, at_y), (1, "w_y", 2, at_x)):
            copies.arrived((way, m, j))
            copies.start(
                ("w_far", m, j), w_all[m].at[PLACE[i], j], w_all[m].at[PLACE[3], j], to
            )

    qx, qy = flips(q, 1), flips(q, 2)
    low, high = slice(0, half_w), slice(half_w, wide)

    lane = lax.rem(lax.broadcasted_iota(jnp.int32, (tokens, wide), 1), HP) - HD
    slots = ((watt_own, bqv_own, q0, k0, v0, c0, l0), (watt_other, bqv_other, q1, k1, v1, c1, l1))

    def project(slot, part):
        watt, bqv, qr, kr, vr = slots[slot][:5]
        x = x_row[part, :]
        same = lane == seg[part, :]
        marks = jnp.where(same, 1.0, 0.0)
        qr[part, :] = (dot(x, watt[0], 1, 1) + bqv[0:1, :] + marks).astype(BF)
        off = jnp.where((lane >= 0) & (lane < 4) & jnp.logical_not(same), MASKED, 0.0)
        kr[part, :] = (dot(x, watt[1], 1, 1) + off).astype(BF)
        vr[part, :] = (dot(x, watt[2], 1, 1) + bqv[1:2, :]).astype(BF)

    qb = 256

    def attend(slot, first, count):
        qr, kr, _, _, lr = slots[slot][2:]
        for h, (base, size, lo) in enumerate(head_windows(wide)):
            win = slice(base, base + size)
            ln = lax.broadcasted_iota(jnp.int32, (2 * tokens, size), 1)
            km = jnp.where((ln >= lo) & (ln < lo + HP), kr[:, win], jnp.zeros((), BF))
            head = slice(h * HP, (h + 1) * HP)
            vth = vts[slot, head, :]

            def block(j, carry):
                at = pl.ds(pl.multiple_of(j * qb, qb), qb)
                s = dot(km, qr[at, win], 1, 1)
                m = jnp.max(s, axis=0, keepdims=True) * SCALE2
                e = jnp.exp2(s * SCALE2 - m)
                total = jnp.sum(e, axis=0, keepdims=True)
                c = dot(vth, e.astype(BF), 1, 0)
                ct[head, at] = c / total
                lr[h, :, at] = m + jnp.log2(total)
                return carry

            lax.fori_loop(first, first + count, block, 0)
        part = slice(first * qb, (first + count) * qb)
        slots[slot][5][part, :] = ct[:, part].T.astype(BF)

    def out_part(part):
        return dot(c0[part, :], watt_own[3], 1, 0) + dot(c1[part, :], watt_other[3], 1, 0)

    def att_plane():
        copies.arrived("a_c")
        copies.start("a_x", watt_other.at[q], watt_other.at[q], at_x)
        copies.start("a_y", watt_other.at[q], watt_other.at[q], at_y)

    def att_far():
        copies.arrived("a_x")
        copies.start("a_xy", watt_other.at[qx, low], watt_other.at[qx, low], at_y)
        copies.arrived("a_y")
        copies.start("a_yx", watt_other.at[qy, high], watt_other.at[qy, high], at_x)

    def att_here():
        copies.arrived("a_xy")
        copies.arrived("a_yx")

    att_plane()
    project(0, mine)
    w_near(1)
    copies.arrived("x")

    @pl.when(mid)
    def _():
        for m in (1, 0):
            for j in (3, 2):
                copies.arrived(("w_z", m, j))
            for made in ends[m]:
                made.start()

    att_far()
    project(0, theirs)
    vts[0] = v0[...].T
    n_peer = tokens // qb
    attend(0, n_peer, n_peer)
    att_here()
    project(1, mine)
    project(1, theirs)
    vts[1] = v1[...].T
    for t in range(n_peer):
        attend(1, n_peer + t, 1)
        part = slice(t * qb, (t + 1) * qb)
        out_send[part, :] = out_part(slice(tokens + t * qb, tokens + (t + 1) * qb)).astype(BF)
        copies.start(("out", t), out_send.at[part], out_land.at[part], at_z[1])
        if t == 0:
            w_far(1)
    w_near_late(2)
    attend(0, 0, n_peer)
    w_near_late(3)
    attend(1, 0, n_peer)
    w_far(2)
    attn_out[...] = out_part(mine) + b_out[...]
    w_far(3)
    for t in range(n_peer):
        copies.arrived(("out", t))
    for b in range(tokens // BLOCK):
        gate, shift, scale = vector(b, 2), vector(b, 3), 1.0 + vector(b, 4)

        def second(t, carry):
            part = pl.ds(pl.multiple_of(b * BLOCK + t * step, step), step)
            out = attn_out[part, :] + out_land[part, :].astype(F32)
            attn_out[part, :] = out
            resid = patches[part, :].astype(F32) + gate * out
            mlp2[part, :] = (norm(resid) * scale + shift).astype(BF)
            return carry

        lax.fori_loop(0, BLOCK // step, second, 0)
    copies.start("mlp", mlp2.at[mine], mlp2.at[theirs], at_core)
    copies.arrived("mlp")
    copies.arrived("gmo")
    for j in (1, 2, 3):
        for m in (1, 0):
            copies.arrived((("w_y", "w_x")[m], m, j))
            copies.arrived(("w_far", m, j))
    for made in own:
        made.wait()
    copies.finish(but=[("w_z", m, j) for m in range(2) for j in (2, 3)])

    @pl.when(mid)
    def _():
        for m in range(2):
            for j in (2, 3):
                copies.made["w_z", m, j].wait_send()
            for made in ends[m]:
                made.wait_send()

    for k, (ref, n) in enumerate(
        ((cond_all, n_dp), (ids_all, n_all), (bias_all, n_mp), (land, n_all))
    ):
        wait_all(ref, n - 1, small.at[2 * k])


def front(cond, ids, bias, w_ada, b_ada, patches, cotangent, seg, watt_own, w_fc1, w_fc2, bqv_own, b_out):
    n_dp, n_mp = lax.axis_size("dp"), lax.axis_size("mp")
    n_all, per_dp, width, cols = n_dp * n_mp, cond.shape[0], cond.shape[1], w_ada.shape[1]
    tokens, wide = patches.shape[0], watt_own.shape[1]
    sixth = w_fc2.shape[0] // 8
    cond8 = jnp.pad(cond.astype(F32), ((0, 8 - per_dp), (0, 0)))
    ids8 = jnp.pad(ids.astype(F32), (0, 8 - ids.shape[0]), constant_values=-1.0)
    row = jax.ShapeDtypeStruct((2 * tokens, wide), BF)
    lse = jax.ShapeDtypeStruct((wide // HP, 1, 2 * tokens), F32)
    shapes = (
        jax.ShapeDtypeStruct((n_dp * 8, width), BF),
        jax.ShapeDtypeStruct((n_all, 8, 128), F32),
        jax.ShapeDtypeStruct((16, sixth), F32),
        jax.ShapeDtypeStruct((8, 6 * width), F32),
        jax.ShapeDtypeStruct((2 * tokens, width), BF),
        *([row] * 8),
        lse,
        lse,
        jax.ShapeDtypeStruct(watt_own.shape, BF),
        jax.ShapeDtypeStruct((4, n_mp, sixth, width), BF),
        jax.ShapeDtypeStruct((4, n_mp, sixth, width), BF),
        jax.ShapeDtypeStruct((tokens, width), F32),
        jax.ShapeDtypeStruct((2 * tokens, width), BF),
        jax.ShapeDtypeStruct((2 * tokens, width), BF),
    )
    vmem, anywhere = pl.BlockSpec(memory_space=pltpu.VMEM), pl.BlockSpec(memory_space=pl.ANY)
    in_specs = [vmem] * 13
    in_specs[10] = anywhere
    out_specs = [vmem] * len(shapes)
    out_specs[16] = out_specs[17] = anywhere
    return pl.pallas_call(
        functools.partial(front_kernel, per_dp),
        out_shape=shapes,
        in_specs=in_specs,
        out_specs=out_specs,
        scratch_shapes=[
            pltpu.VMEM((n_dp, 8, width), F32),
            pltpu.VMEM((n_all, 8, 128), F32),
            pltpu.VMEM((n_mp, *bias.shape), F32),
            pltpu.VMEM((n_all, 8, cols), F32),
            pltpu.VMEM((n_all, 8, cols), F32),
            pltpu.VMEM((w_fc1.shape[1], width), BF),
            pltpu.VMEM((tokens, width), F32),
            pltpu.VMEM((tokens, width), BF),
            pltpu.VMEM((tokens, width), BF),
            pltpu.VMEM((2, wide, 2 * tokens), BF),
            pltpu.VMEM((wide, 2 * tokens), F32),
            pltpu.VMEM((8, wide), F32),
            pltpu.SemaphoreType.DMA((8,)),
            pltpu.SemaphoreType.DMA((8,)),
            pltpu.SemaphoreType.DMA((96,)),
        ],
        compiler_params=pltpu.CompilerParams(
            collective_id=0, has_side_effects=True, vmem_limit_bytes=62 << 20
        ),
    )(
        cond8,
        jnp.broadcast_to(ids8[:, None], (8, 128)),
        bias,
        w_ada,
        b_ada.astype(F32)[None],
        patches,
        cotangent,
        seg,
        watt_own,
        w_fc1,
        w_fc2,
        bqv_own,
        b_out.astype(F32)[None],
    )


def back_kernel(
    per_dp, gao_row, x_row, watt_own, watt_other, q0, k0, v0, q1, k1, v1, c0, c1, l0, l1,
    two_2, two_0, one_1, one_0, patches, sums_4, b_sums, ids_all, w_ada,
    g_out, grad_cols, final, mlp_all, att_all,
    kt, dqt, wide_acc, gc, d3, att, core_land, come, plane, z_land, first_land, second_land,
    part_send, last_land, mlp_done, g_send, g_land, more_mlp, more_att,
    sums_6, col_send, col_land, row_send, shared, z_rows, small, sems,
):
    rows, width = gao_row.shape
    tokens = rows // 2
    wide = watt_own.shape[1]
    half = wide // 2
    d, z = lax.axis_index("dp"), lax.axis_index("mp")
    core, q = lax.rem(d, 2), lax.rem(d // 2, 4)
    at_z = [(d, z), (d, flip(z, 1)), (d, flip(z, 2)), (d, 3 - z)]
    at_core, at_x, at_y = (flip(d, 1), z), (flip(d, 2), z), (flip(d, 4), z)
    extra, bit = [], 8
    while bit < lax.axis_size("dp"):
        extra.append((flip(d, bit), z))
        bit *= 2
    barrier = pltpu.get_barrier_semaphore()
    n_dp, n_mp = lax.axis_size("dp"), lax.axis_size("mp")
    n_all, me = n_dp * n_mp, d * n_mp + z

    def greet(t, carry):
        to = coords(lax.rem(me + t, n_all), n_mp)
        pl.semaphore_signal(barrier, inc=1, device_id=to, device_id_type=pl.DeviceIdType.MESH)
        return carry

    lax.fori_loop(1, n_all, greet, 0)
    pl.semaphore_wait(barrier, n_all - 1)
    copies = Copies(sems)
    copies.start("two", two_2, come.at[1], at_y)
    copies.start("one", one_1, come.at[0], at_x)
    kept = [
        pltpu.make_async_copy(one_0, plane.at[0], sems.at[sems.shape[0] - 3]),
        pltpu.make_async_copy(two_0, plane.at[1], sems.at[sems.shape[0] - 4]),
    ]
    for made in kept:
        made.start()
    zero = jnp.zeros((), BF)
    qb = 256
    slots = ((watt_own, q0, k0, v0, c0, l0), (watt_other, q1, k1, v1, c1, l1))

    att_done = first_land.at[0, 0]
    dv_at = [slice(384 + base, 384 + base + size) for base, size, _ in head_windows(wide)]

    def back(slot):
        watt, qr, kr, vr, _, lr = slots[slot]
        for t in range(2):
            at = slice(t * tokens, (t + 1) * tokens)
            gc[at, :] = dot(gao_row[at, :], watt[3], 1, 1).astype(BF)
        kt[...] = kr[...].T
        wide_acc[...] = jnp.zeros_like(wide_acc)
        for h, (base, size, lo) in enumerate(head_windows(wide)):
            win = slice(base, base + size)
            lane = lax.broadcasted_iota(jnp.int32, (rows, size), 1)
            here = (lane >= lo) & (lane < lo + HP)
            km = jnp.where(here, kr[:, win], zero)
            vm = jnp.where(here, vr[:, win], zero)
            head = slice(h * HP, (h + 1) * HP)
            row = lax.broadcasted_iota(jnp.int32, (HP, rows), 0)
            kth = jnp.where(row < HD, kt[head, :], zero)
            lane_b = lax.broadcasted_iota(jnp.int32, (qb, size), 1)
            real = (lane_b >= lo) & (lane_b < lo + HD)

            def block(j, carry):
                at = pl.ds(pl.multiple_of(j * qb, qb), qb)
                q_blk = qr[at, win]
                g_blk = gc[at, win]
                s = dot(km, q_blk, 1, 1)
                p = jnp.exp2(s * SCALE2 - lr[h, :, at])
                dp = dot(vm, g_blk, 1, 1)
                delta = jnp.sum(p * dp, axis=0, keepdims=True)
                ds = (p * (dp - delta)).astype(BF)
                wide_acc[:rows, dv_at[h]] += dot(p.astype(BF), jnp.where(real, g_blk, zero), 1, 0)
                wide_acc[:rows, win] += dot(ds, jnp.where(real, q_blk, zero), 1, 0)
                dqt[head, at] = dot(kth, ds, 1, 0)
                return carry

            lax.fori_loop(0, rows // qb, block, 0)
        d3[slot, 0] = (dqt[...].T * SCALE).astype(BF)
        d3[slot, 1] = (wide_acc[:rows, :wide] * SCALE).astype(BF)
        d3[slot, 2] = wide_acc[:rows, 384 : 384 + wide].astype(BF)
        for n, m in enumerate((0, 2)):
            shared[6 + slot : 7 + slot, n * 384 : n * 384 + wide] = jnp.sum(
                d3[slot, m].astype(F32), axis=0, keepdims=True
            )

    def weight_grads(slot):
        ctx = slots[slot][4]

        def one(m, carry):
            att[m] = dot(d3[slot, m], x_row[...], 0, 0).astype(BF)
            return carry

        lax.fori_loop(0, 3, one, 0)
        att[3] = dot(ctx[...], gao_row[...], 0, 0).astype(BF)
        away = pl.ds(pl.multiple_of((1 - core) * half, 16), half)
        copies.start(("c", slot), att.at[:, away], core_land.at[slot], at_core)

    keep = pl.ds(pl.multiple_of(core * half, 16), half)

    def add(a, b):
        return (a.astype(F32) + b.astype(F32)).astype(BF)

    def core_sum(slot):
        copies.arrived(("c", slot))

        def one(m, carry):
            core_land[slot, m] = add(core_land[slot, m], att[m, keep])
            return carry

        lax.fori_loop(0, 4, one, 0)
        bits, to = ((1, at_x), (2, at_y))[slot]
        for n, i in enumerate((bits, 3)):
            copies.start(
                ("p", slot, n), core_land.at[slot, flips(q, i)], first_land.at[slot, n], to
            )

    def second_way(slot):
        other, to = ((2, at_y), (1, at_x))[slot]
        for n in range(2):
            copies.arrived(("p", slot, n))
        part_send[slot] = add(core_land[slot, flips(q, other)], first_land[slot, 1])
        copies.start(("s", slot), part_send.at[slot], second_land.at[slot], to)
        first_land[slot, 0] = add(core_land[slot, q], first_land[slot, 0])

    def plane_sum(slot):
        copies.arrived(("s", slot))
        first_land[slot, 0] = add(first_land[slot, 0], second_land[slot])

    shared[...] = b_sums[...]
    back(1)
    weight_grads(1)
    copies.arrived("two")
    copies.arrived("one")
    for m in (1, 0):
        kept[m].wait()

        def one(j, carry):
            plane[m, j] = add(plane[m, j], come[m, j])
            return carry

        lax.fori_loop(0, 4, one, 0)
        for j in (1, 2, 3):
            copies.start(("z", m, j), plane.at[m, j], z_land.at[m, j - 1], at_z[j])
    core_sum(1)
    back(0)
    second_way(1)

    def g_part(at):
        total = None
        for slot in (0, 1):
            for m in range(3):
                term = dot(d3[slot, m, at], slots[slot][0][m], 1, 0)
                total = term if total is None else total + term
        return total

    g_send[...] = g_part(slice(tokens, rows)).astype(BF)
    copies.start("g", g_send, g_land, at_z[1])
    plane_sum(1)
    copies.start("b", first_land.at[1, 0], last_land, at_z[2])
    copies.made["c", 1].wait_send()
    weight_grads(0)
    core_sum(0)
    g_out[...] = g_part(slice(0, tokens))
    second_way(0)
    for m in (1, 0):
        for j in (1, 2, 3):
            copies.arrived(("z", m, j))
        total = plane[m, 0].astype(F32)
        for j in (1, 2, 3):
            total = total + z_land[m, j - 1].astype(F32)
        mlp_done[m] = total.astype(BF)
    for n, to in enumerate(extra):
        copies.start(("mlp_more", n), mlp_done, more_mlp.at[n], to)
        copies.arrived(("mlp_more", n))
        copies.made["mlp_more", n].wait_send()
        mlp_done[...] = add(mlp_done[...], more_mlp[n])
    last = sems.shape[0]
    here = [pltpu.make_async_copy(mlp_done, mlp_all.at[core, q], sems.at[last - 1])]
    here[0].start()
    copies.start("m_x", mlp_done, mlp_all.at[core, q], at_x)
    copies.start("m_y", mlp_done, mlp_all.at[core, q], at_y)
    plane_sum(0)
    copies.arrived("b")
    att_done[...] = add(first_land[0, 0], last_land[...])
    for n, to in enumerate(extra):
        copies.start(("att_more", n), att_done, more_att.at[n], to)
        copies.arrived(("att_more", n))
        copies.made["att_more", n].wait_send()
        att_done[...] = add(att_done[...], more_att[n])
    here.append(pltpu.make_async_copy(att_done, att_all.at[q, core], sems.at[last - 2]))
    here[1].start()
    copies.start("a_x", att_done, att_all.at[q, core], at_x)
    copies.start("a_y", att_done, att_all.at[q, core], at_y)

    copies.made["g"].wait_send()
    fetch = pltpu.make_async_copy(patches, g_send, sems.at[last - 5])
    fetch.start()
    copies.arrived("g")
    step = 128
    sums_6[:, 2 * width :] = sums_4[...]
    sums_6[:, : 2 * width] = jnp.zeros((8, 2 * width), F32)
    fetch.wait()
    for b in range(tokens // BLOCK):

        def total(t, carry):
            part = pl.ds(pl.multiple_of(b * BLOCK + t * step, step), step)
            g = g_out[part, :] + g_land[part, :].astype(F32)
            g_out[part, :] = g
            v = g_send[part, :].astype(F32)
            centred = v - jnp.mean(v, axis=-1, keepdims=True)
            spread = jnp.mean(centred * centred, axis=-1, keepdims=True)
            scaled = g * (centred * lax.rsqrt(spread + 1e-06))
            return (
                carry[0] + jnp.sum(g, axis=0, keepdims=True),
                carry[1] + jnp.sum(scaled, axis=0, keepdims=True),
            )

        nothing = jnp.zeros((1, width), F32)
        shift, scale = lax.fori_loop(0, BLOCK // step, total, (nothing, nothing))
        sums_6[b : b + 1, :width] = shift
        sums_6[b : b + 1, width : 2 * width] = scale
    cols = col_send.shape[2]
    for t in range(n_all):
        col_send[t] = sums_6[:, t * cols : (t + 1) * cols]

    def remote(src, dst, k, to):
        return pltpu.make_async_remote_copy(
            src_ref=src, dst_ref=dst, send_sem=small.at[2 * k], recv_sem=small.at[2 * k + 1],
            device_id=to, device_id_type=pl.DeviceIdType.MESH,
        )

    def send_cols(t, carry):
        other = lax.rem(me + t, n_all)
        remote(col_send.at[other], col_land.at[me], 0, coords(other, n_mp)).start()
        return carry

    lax.fori_loop(1, n_all, send_cols, 0)
    col_land[me] = col_send[me]
    qx, qy = flips(q, 1), flips(q, 2)
    copies.arrived("m_x")
    copies.start("m_xy", mlp_all.at[core, qx, 0], mlp_all.at[core, qx, 0], at_y)
    copies.arrived("m_y")
    copies.start("m_yx", mlp_all.at[core, qy, 1], mlp_all.at[core, qy, 1], at_x)
    here[0].wait()
    for i in range(3):
        at = flips(q, i)
        copies.start(("m_c", i), mlp_all.at[core, at], mlp_all.at[core, at], at_core)
    copies.arrived("a_x")
    copies.start("a_xy", att_all.at[qx, core], att_all.at[qx, core], at_y)

    wait_all(col_land, n_all - 1, small.at[1])
    rows_8 = n_dp * 8
    some = min(32, n_all)
    k = lax.broadcasted_iota(jnp.int32, (some * 8, rows_8), 1)
    image = jnp.where(lax.rem(k, 8) < per_dp, k // 8 * per_dp + lax.rem(k, 8), -2).astype(F32)

    def collect(t, carry):
        part = pl.ds(t * some, some)
        found = ids_all[part].reshape(some * 8, 128)[:, :1] == image
        return carry + lax.dot_general(
            jnp.where(found, 1.0, 0.0),
            col_land[part].reshape(some * 8, cols),
            (((0,), (0,)), ((), ())),
            precision=lax.Precision.HIGHEST,
            preferred_element_type=F32,
        )

    summed = lax.fori_loop(0, n_all // some, collect, jnp.zeros((rows_8, cols), F32)).astype(BF)
    grad_cols[...] = summed
    silu_part = dot(summed, w_ada[...], 1, 1)
    row_send[...] = silu_part

    def block_of(t, size, start):
        return pl.ds(pl.multiple_of(t * size + start, 8), 8)

    def send_rows(t, carry):
        other = lax.rem(d + t, n_dp)
        to = (other, z)
        remote(row_send.at[block_of(other, 8, 0)], wide_acc.at[block_of(d, 16, 0)], 1, to).start()
        remote(shared, wide_acc.at[block_of(d, 16, 8)], 1, to).start()
        return carry

    lax.fori_loop(1, n_dp, send_rows, 0)
    wide_acc[block_of(d, 16, 0), :] = row_send[block_of(d, 8, 0), :]
    wide_acc[block_of(d, 16, 8), :] = shared[...]
    copies.arrived("m_xy")
    copies.arrived("m_yx")
    q3 = flips(q, 3)
    copies.start(("m_c", 3), mlp_all.at[core, q3], mlp_all.at[core, q3], at_core)
    copies.arrived("a_y")
    here[1].wait()
    copies.arrived("a_xy")
    copies.start("a_c", att_all.at[:, core], att_all.at[:, core], at_core)
    wait_all(wide_acc, (n_dp - 1) * 16, small.at[3])

    def sum_rows(t, carry):
        return carry + wide_acc[pl.ds(pl.multiple_of(t * 16, 16), 16), :]

    z_rows[0] = lax.fori_loop(0, n_dp, sum_rows, jnp.zeros((16, width), F32))
    for j in (1, 2, 3):
        copies.start(("rows", j), z_rows.at[0], z_rows.at[j], at_z[j])
    for j in (1, 2, 3):
        copies.arrived(("rows", j))
    final[...] = z_rows[0] + z_rows[1] + z_rows[2] + z_rows[3]
    final[14:15, :] = z_rows[0, 14:15, :] + z_rows[2, 15:16, :]
    for i in range(4):
        copies.arrived(("m_c", i))
    copies.arrived("a_c")
    copies.finish(but=[n for n in copies.made if n[0] in ("mlp_more", "att_more") or n in ("g", ("c", 1))])
    wait_all(col_land, n_all - 1, small.at[0])
    wait_all(wide_acc, (n_dp - 1) * 16, small.at[2])


def back(
    per_dp, gao_row, x_row, watt_own, watt_other, heads_0, heads_1, ctx, lse,
    two_2, two_0, one_1, one_0, patches, sums_4, b_sums, ids_all, w_ada,
):
    rows, width = gao_row.shape
    tokens, wide = rows // 2, watt_own.shape[1]
    half, sixth = wide // 2, two_2.shape[1]
    more = max(1, (lax.axis_size("dp") // 8).bit_length() - 1)
    n_dp, n_mp, cols = lax.axis_size("dp"), lax.axis_size("mp"), w_ada.shape[1]
    n_all = n_dp * n_mp
    shapes = (
        jax.ShapeDtypeStruct((tokens, width), F32),
        jax.ShapeDtypeStruct((n_dp * 8, cols), BF),
        jax.ShapeDtypeStruct((16, width), F32),
        jax.ShapeDtypeStruct((2, 4, 2, sixth, width), BF),
        jax.ShapeDtypeStruct((4, 2, half, width), BF),
    )
    vmem, anywhere = pl.BlockSpec(memory_space=pltpu.VMEM), pl.BlockSpec(memory_space=pl.ANY)
    return pl.pallas_call(
        functools.partial(back_kernel, per_dp),
        out_shape=shapes,
        in_specs=[vmem] * 14 + [anywhere] * 5 + [vmem] * 4,
        out_specs=[vmem, vmem, vmem, anywhere, anywhere],
        scratch_shapes=[
            pltpu.VMEM((wide, rows), BF),
            pltpu.VMEM((wide, rows), F32),
            pltpu.VMEM((max(rows, n_dp * 16), width), F32),
            pltpu.VMEM((rows, wide), BF),
            pltpu.VMEM((2, 3, rows, wide), BF),
            pltpu.VMEM((4, wide, width), BF),
            pltpu.VMEM((2, 4, half, width), BF),
            pltpu.VMEM((2, 4, sixth, width), BF),
            pltpu.VMEM((2, 4, sixth, width), BF),
            pltpu.VMEM((2, 3, sixth, width), BF),
            pltpu.VMEM((2, 2, half, width), BF),
            pltpu.VMEM((2, half, width), BF),
            pltpu.VMEM((2, half, width), BF),
            pltpu.VMEM((half, width), BF),
            pltpu.VMEM((2, sixth, width), BF),
            pltpu.VMEM((tokens, width), BF),
            pltpu.VMEM((tokens, width), BF),
            pltpu.VMEM((more, 2, sixth, width), BF),
            pltpu.VMEM((more, half, width), BF),
            pltpu.VMEM((8, 6 * width), F32),
            pltpu.VMEM((n_all, 8, cols), F32),
            pltpu.VMEM((n_all, 8, cols), F32),
            pltpu.VMEM((n_dp * 8, width), F32),
            pltpu.VMEM((8, width), F32),
            pltpu.VMEM((4, 16, width), F32),
            pltpu.SemaphoreType.DMA((4,)),
            pltpu.SemaphoreType.DMA((96,)),
        ],
        compiler_params=pltpu.CompilerParams(
            collective_id=1, has_side_effects=True, vmem_limit_bytes=63 << 20
        ),
    )(
        gao_row, x_row, watt_own, watt_other, *heads_0, *heads_1, *ctx, *lse,
        two_2, two_0, one_1, one_0, patches, sums_4, b_sums, ids_all, w_ada,
    )


def pad_heads(rows_in):
    *lead, n, width = rows_in.shape
    split = rows_in.reshape(*lead, n // HD, HD, width)
    pads = [(0, 0)] * (len(lead) + 1) + [(0, HP - HD), (0, 0)]
    return jnp.pad(split, pads).reshape(*lead, n // HD * HP, width)


def drop_pads(rows_in):
    *lead, n, width = rows_in.shape
    split = rows_in.reshape(*lead, n // HP, HP, width)[..., :HD, :]
    return split.reshape(*lead, n // HP * HD, width)


def on_device(
    patches,
    cotangent,
    conditioning,
    segment,
    image_ids,
    w_ada,
    b_ada,
    w_qkv,
    b_qv,
    w_out,
    b_out,
    w_fc1,
    b_fc1,
    w_fc2,
    b_fc2,
):
    n_dp, n_mp = lax.axis_size("dp"), lax.axis_size("mp")
    n_all = n_dp * n_mp
    z = lax.axis_index("mp")
    d = lax.axis_index("dp")
    core = d & 1
    everyone = ("dp", "mp")
    tokens, width = patches.shape
    n_blocks = tokens // BLOCK
    shard = w_fc2.shape[0]
    hidden_n = shard * n_mp

    q = (d >> 1) & 3
    sixth = shard // 8

    heads_shard = w_out.shape[0]
    watt_own = pad_heads(jnp.concatenate([w_qkv.transpose(0, 2, 1), w_out[None]], axis=0))
    wide = watt_own.shape[1]
    ids = image_ids.reshape(n_blocks, BLOCK)[:, 0]
    cols = w_ada.shape[1]
    bias = jnp.concatenate(
        [
            jnp.pad(b_fc1.astype(F32).reshape(8, sixth), ((0, 0), (0, heads_shard - sixth))),
            jnp.pad(b_qv.astype(F32), ((0, 6), (0, 0))),
        ]
    )
    bqv_own = jnp.pad(pad_heads(b_qv[..., None])[..., 0].astype(F32), ((0, 6), (0, 0)))
    seg_own = lax.dynamic_slice_in_dim(segment, z * tokens, tokens, 0)
    seg_peer = lax.dynamic_slice_in_dim(segment, (z ^ 1) * tokens, tokens, 0)
    seg = jnp.concatenate([seg_own, seg_peer])[:, None]
    (
        silu_cond, ids_all, b1_rel, mods, x_row, q0, k0, v0, q1, k1, v1, ctx_0, ctx_1,
        lse_0, lse_1, watt_other, w1_all, w2_all, attn_out, mlp2, gmo2,
    ) = front(
        conditioning, ids, bias, w_ada, b_ada, patches, cotangent, seg, watt_own, w_fc1, w_fc2,
        bqv_own, b_out,
    )
    heads_0, heads_1 = (q0, k0, v0), (q1, k1, v1)
    w1_all, w2_all = [w.reshape(16 * sixth, width) for w in (w1_all, w2_all)]
    b1_all = b1_rel.reshape(16 * sixth)
    mods = mods[:n_blocks].reshape(n_blocks, 6, width)
    shift_attn, scale_attn, gate_attn, shift_mlp, scale_mlp, gate_mlp = [
        mods[:, i, None, :] for i in range(6)
    ]

    def blocks(v):
        return v.reshape(n_blocks, BLOCK, width)

    def flat(v):
        return v.reshape(tokens, width)

    patch_wide = blocks(patches.astype(F32))
    grad_output = blocks(cotangent.astype(F32))
    norm_a, rsig_a = layer_norm(flat(patch_wide))
    attn_out = blocks(attn_out)
    resid = patch_wide + gate_attn * attn_out
    norm_m, rsig_m = layer_norm(flat(resid))

    gmo = gmo2[:tokens]
    pre = dot(mlp2, w1_all, 1, 1) + b1_all
    act, act_grad = gelu_parts(pre)
    hidden = act.astype(BF)

    quad = 4 * sixth

    def grads(left, right, at, to):
        out = dot(left[:, at * quad : to * quad], right, 0, 0)
        return out.reshape(to - at, 4, sixth, width)

    def low_sum(a, b):
        return (a.astype(F32) + b.astype(F32)).astype(BF)

    send2 = grads(hidden, gmo2, 1, 3).astype(BF)
    come2 = swap(send2, "dp", 2)
    grad_pre = (dot(after(gmo2, send2), w2_all, 1, 1) * act_grad).astype(BF)
    grad_b1 = jnp.sum(grad_pre, axis=0, dtype=F32)
    send1 = grads(grad_pre, mlp2, 2, 4).astype(BF)
    come1 = swap(send1, "dp", 4)
    gin_peer = swap(dot(grad_pre[tokens:], w1_all, 1, 0).astype(BF), "dp", 1)
    g_mlp_in = blocks(dot(grad_pre[:tokens], w1_all, 1, 0) + gin_peer.astype(F32))
    g_shift_mlp = jnp.sum(g_mlp_in, axis=1)
    g_scale_mlp = jnp.sum(g_mlp_in * blocks(norm_m), axis=1)
    u_mlp = flat(g_mlp_in * (1.0 + scale_mlp))
    grad_resid = grad_output + blocks(norm_back(u_mlp, norm_m, rsig_m))
    g_gate_attn = jnp.sum(grad_resid * attn_out, axis=1)
    gao = flat((gate_attn * grad_resid).astype(BF))
    gao_row = jnp.concatenate([gao, swap(gao, "mp", 1)], axis=0)

    hidden_w, gmo2_w, gpre_w, mlp2_w = lax.optimization_barrier(
        (hidden, gmo2, grad_pre, mlp2, gao)
    )[:4]
    mlp_peer = swap(dot(hidden_w[tokens:], w2_all, 1, 0).astype(BF), "dp", 1)
    keep2_2 = grads(hidden_w, gmo2_w, 3, 4)[0]
    keep2_0 = grads(hidden_w, gmo2_w, 0, 1)[0]
    mlp_out = blocks(
        dot(hidden_w[:tokens], w2_all, 1, 0) + mlp_peer.astype(F32) + b_fc2.astype(F32)
    )
    output = flat((resid + gate_mlp * mlp_out).astype(BF))
    g_gate_mlp = jnp.sum(grad_output * mlp_out, axis=1)
    grad_b2 = jnp.sum(after(gmo, gao), axis=0, dtype=F32)
    grad_b1 = after(grad_b1, gao)
    grad_bout = jnp.sum(gao, axis=0, dtype=F32)

    come2, come1 = lax.optimization_barrier((come2, come1, keep2_0))[:2]
    two_2 = low_sum(keep2_2, come2[1])
    two_0 = low_sum(keep2_0, come2[0])
    keep1 = grads(gpre_w, mlp2_w, 0, 2)
    one_1 = low_sum(keep1[1], come1[0])
    one_0 = low_sum(keep1[0], come1[1])
    nat, rel_at = jnp.arange(8 * n_mp)[:, None], jnp.arange(16)[None, :]
    step = rel_at // 4
    step = jnp.where(step == 2, 3, jnp.where(step == 3, 2, step))
    comes = ((nat // 8) == (z ^ (rel_at % 4))) & ((nat % 4) == (q ^ step))
    comes = comes & (nat // 4 % 2 == core)
    grad_b1 = lax.dot_general(
        comes.astype(F32),
        grad_b1.reshape(16, sixth),
        (((1,), (0,)), ((), ())),
        precision=lax.Precision.HIGHEST,
        preferred_element_type=F32,
    )
    b_sums = jnp.concatenate(
        [grad_bout[None], grad_b2[None], grad_b1.reshape(n_mp, shard), jnp.zeros((2, width), F32)]
    )
    sums_4 = jnp.concatenate([g_gate_attn, g_shift_mlp, g_scale_mlp, g_gate_mlp], axis=1)
    sums_4 = jnp.pad(sums_4, ((0, 8 - n_blocks), (0, 0)))
    g_attn_in, grad_cols, final, mlp_all, att_all = back(
        conditioning.shape[0], gao_row, x_row, watt_own, watt_other, heads_0, heads_1,
        (ctx_0, ctx_1), (lse_0, lse_1), two_2, two_0, one_1, one_0, patches, sums_4, b_sums,
        ids_all, w_ada,
    )
    g_attn_in = blocks(g_attn_in)
    out_w1 = mlp_all[:, :, 0].reshape(shard, width)
    unit = (jnp.arange(shard)[:, None] == jnp.arange(shard)[None, :]).astype(BF)
    out_w1 = dot(out_w1, unit, 0, 0)
    out_w2 = mlp_all[:, :, 1].reshape(shard, width).astype(F32)
    att_all = drop_pads(att_all.reshape(4, wide, width))
    out_qkv = att_all[:3].transpose(0, 2, 1).astype(F32)
    out_wout = att_all[3].astype(F32)
    u_attn = flat(g_attn_in * (1.0 + scale_attn))
    grad_patches = flat(grad_resid) + norm_back(u_attn, norm_a, rsig_a)
    grad_w_ada = dot(silu_cond, grad_cols, 0, 0)
    grad_b_ada = jnp.sum(grad_cols, axis=0, dtype=F32)
    grad_silu = final[: conditioning.shape[0]]
    _, silu_back = jax.vjp(silu_fn, conditioning.astype(F32))
    grad_cond = silu_back(grad_silu)[0]
    out_bout, out_b2 = final[8], final[9]
    out_b1 = lax.dynamic_index_in_dim(final, 10 + z, 0, keepdims=False)
    out_bqv = jnp.stack([final[14, :wide], final[14, 384 : 384 + wide]])
    out_bqv = drop_pads(out_bqv[..., None])[..., 0]

    return (
        output,
        grad_patches,
        grad_cond,
        grad_w_ada,
        grad_b_ada,
        out_qkv,
        out_bqv,
        out_wout,
        out_bout,
        out_w1,
        out_b1,
        out_w2,
        out_b2,
    )


def solution(mesh):
    rows = P(("dp", "mp"), None)
    in_specs = (
        rows,
        rows,
        P("dp", None),
        P("dp"),
        P(("dp", "mp")),
        P(None, ("dp", "mp")),
        P(("dp", "mp")),
        P(None, None, "mp"),
        P(None, "mp"),
        P("mp", None),
        P(),
        P(None, "mp"),
        P("mp"),
        P("mp", None),
        P(),
    )
    out_specs = (
        rows,
        rows,
        P("dp", None),
        P(None, ("dp", "mp")),
        P(("dp", "mp")),
        P(None, None, "mp"),
        P(None, "mp"),
        P("mp", None),
        P(),
        P(None, "mp"),
        P("mp"),
        P("mp", None),
        P(),
    )
    return jax.shard_map(
        on_device, mesh=mesh, in_specs=in_specs, out_specs=out_specs, check_vma=False
    )
```
